32 devices in a mesh: seq: 8 (over z, x), chan: 4 (over y, core).
Axes of the slice: x: 2, y: 2, z: 4, core: 2. Of those that a mesh axis runs over, the one named last changes fastest.
Arguments:
- q_gate: bfloat16 [4096, 1024], P('seq', 'chan'), may hold values from -6 to 6
- k_gate: bfloat16 [4096, 1024], P('seq', 'chan'), may hold values from -6 to 6
- value: bfloat16 [4096, 1024], P('seq', 'chan'), may hold values from -6 to 6
- decay: float32 [16, 1024], P(None, 'chan'), may hold values from 6.1035156e-05 to 0.0333333333
- residue: float32 [16, 1024], P(None, 'chan'), may hold values from -1 to 1
- skip: float32 [1024], P('chan'), may hold values from -1 to 1
- out_weight: bfloat16 [1024, 1024], P(None, 'chan'), may hold values from -0.1875 to 0.1875
- out_bias: float32 [1024], P('chan'), may hold values from -3 to 3
Outputs:
- layer_out: bfloat16 [4096, 1024], P('seq', 'chan')
The draws below stay inside these ranges and needn't reach their ends.
All inputs are finite; a program needn't handle non-finite values.
Results may differ from the reference program's by a relative error of at most 0.015.
Values may be sent and summed in bfloat16 or wider, within the bound.
No kernel may reach another device: no remote copies, remote signals or barrier semaphores. Data moves between devices by JAX's collectives and lax.ppermute only.
A program may use at most 64 MiB of HBM per device.

```python
import jax
import jax.numpy as jnp
from jax import lax

CH = 1024
MODES = 16
SEQ_LEN = 4096


def mode_lengths(key, shortest, longest):
    spread = jax.random.uniform(key, (MODES, CH), jnp.float32)
    return jnp.exp(jnp.log(shortest) + spread * (jnp.log(longest) - jnp.log(shortest)))


def draw_decay(key, part):
    lengths = mode_lengths(key, 30.0, 4.0 * SEQ_LEN)
    return 1.0 / lengths


def draw_residue(key, part):
    lengths = mode_lengths(key, 30.0, 4.0 * SEQ_LEN)
    key = jax.random.fold_in(key, 7)
    scales = jnp.clip(jax.random.normal(key, (MODES, CH), jnp.float32), -4.0, 4.0)
    return scales * jnp.sqrt(2.0 / (MODES * jnp.minimum(lengths, 1.0 * SEQ_LEN)))


def level_of(rng, dims, cuts, least, largest):
    def one(axis_at, shards_of):
        steps = jax.random.uniform(jax.random.fold_in(jax.random.fold_in(rng, 6), axis_at), (shards_of,), jnp.float32, least / len(cuts), largest / len(cuts))
        return jnp.repeat(jnp.exp(steps), dims[axis_at] // shards_of).reshape((-1,) + (1,) * (len(dims) - axis_at - 1))

    gain = one(*cuts[0])
    for cut in cuts[1:]:
        gain = gain * one(*cut)
    return gain


def scatter_about(rng, extent, width, bound, split=(), kind=jnp.bfloat16):
    gain = level_of(rng, extent, split, -0.22, 0.18) if split else 1.0
    drawn = jax.random.normal(rng, extent, jnp.float32) * width * gain
    return jnp.minimum(jnp.maximum(drawn, -bound), bound).astype(kind)


def setup_inputs(seed: int = 0) -> dict:
    keys = jax.random.split(jax.random.key(seed), 9)
    return {
        "q_gate": scatter_about(keys[0], (SEQ_LEN, CH), 1.0, 6.0, ((0, 8), (1, 4))),
        "k_gate": scatter_about(keys[1], (SEQ_LEN, CH), 1.0, 6.0, ((0, 8), (1, 4))),
        "value": scatter_about(keys[2], (SEQ_LEN, CH), 1.0, 6.0, ((0, 8), (1, 4))),
        "decay": draw_decay(jax.random.fold_in(keys[8], 71), 0),
        "residue": draw_residue(jax.random.fold_in(keys[8], 71), 0),
        "skip": jnp.clip(jax.random.uniform(keys[5], (CH,), jnp.float32, -1.0, 1.0) * level_of(keys[5], (CH,), ((0, 4),), -0.4, 0.0), -1.0, 1.0),
        "out_weight": scatter_about(keys[6], (CH, CH), CH ** -0.5, 0.1875, ((1, 4),)),
        "out_bias": scatter_about(keys[7], (CH,), 0.5, 3.0, ((0, 4),), jnp.float32),
    }


def reference(q_gate, k_gate, value, decay, residue, skip, out_weight, out_bias):
    gated = (k_gate.astype(jnp.float32) * value.astype(jnp.float32)).astype(jnp.bfloat16)
    block_width = min(CH, 128)
    group_count = CH // block_width
    padded_len = 2 * SEQ_LEN
    positions = jnp.arange(SEQ_LEN).astype(jnp.float32)

    def one_group(group_index):
        offset = (group_index * block_width).astype(jnp.int32)
        signal = lax.dynamic_slice_in_dim(gated, offset, block_width, 1).astype(jnp.float32)
        rate_block = lax.dynamic_slice_in_dim(decay, offset, block_width, 1)
        weight_block = lax.dynamic_slice_in_dim(residue, offset, block_width, 1)
        kernel = jnp.zeros((SEQ_LEN, block_width), jnp.float32)
        for order_index in range(MODES):
            kernel = kernel + weight_block[order_index] * jnp.exp(-rate_block[order_index] * positions[:, None])
        spectrum = jnp.fft.rfft(signal, n=padded_len, axis=0) * jnp.fft.rfft(kernel, n=padded_len, axis=0)
        return jnp.fft.irfft(spectrum, n=padded_len, axis=0)[:SEQ_LEN].astype(jnp.float32)

    blocks = lax.map(one_group, jnp.arange(group_count, dtype=jnp.int32))
    convolved = jnp.transpose(blocks, (1, 0, 2)).reshape(SEQ_LEN, CH)
    modulated = (q_gate.astype(jnp.float32) * (convolved + skip * gated.astype(jnp.float32))).astype(jnp.bfloat16)
    projected = jnp.dot(modulated, out_weight, preferred_element_type=jnp.float32) + out_bias
    return projected.astype(jnp.bfloat16)
```

```python
import functools

import jax
import jax.numpy as jnp
from jax import lax
from jax.experimental import pallas as pl
from jax.experimental.pallas import tpu as pltpu
from jax.sharding import PartitionSpec as P

LANES = 128
SUBLANES = 8
STORES = 2
FOLD_COST = 3000000000
NEAR_COST = 3000000000
PART_COST = 1500000000
VMEM_LIMIT = 32 * 1024 * 1024


def row(ref, mode, part):
    return ref[mode : mode + 1, part * LANES : (part + 1) * LANES]


def full(value):
    return jnp.broadcast_to(value, (SUBLANES, LANES))


def tree_sum(terms):
    while len(terms) > 1:
        paired = [a + b for a, b in zip(terms[::2], terms[1::2])]
        terms = paired + ([terms[-1]] if len(terms) % 2 else [])
    return terms[0]


def lane_slice(part):
    return slice(part * LANES, (part + 1) * LANES)


def state_kernel(
    k_hbm, v_hbm, decay_hbm, residue_hbm, skip_hbm, bias_hbm,
    total_ref, chunk_ref, gated_ref, decay_ref, residue_ref, skip_ref, bias_ref,
    k_ref, v_ref, sems,
):
    modes = decay_hbm.shape[0]
    parts = gated_ref.shape[0]
    chunk_len = k_ref.shape[0] // SUBLANES
    pairs = [(decay_hbm, decay_ref)]
    for part in range(parts):
        lanes = pl.ds(part * LANES, LANES)
        pairs += [(k_hbm.at[:, lanes], k_ref.at[:, lanes]), (v_hbm.at[:, lanes], v_ref.at[:, lanes])]
    pairs += [(residue_hbm, residue_ref), (skip_hbm, skip_ref), (bias_hbm, bias_ref)]
    copies = [pltpu.make_async_copy(src, dst, sems.at[i]) for i, (src, dst) in enumerate(pairs)]
    for copy in copies:
        copy.start()
    copies[0].wait()
    later = (SUBLANES - 1 - lax.broadcasted_iota(jnp.int32, (SUBLANES, LANES), 0)) * chunk_len
    later = later.astype(jnp.float32)
    for part in range(parts):
        lanes = lane_slice(part)
        copies[1 + 2 * part].wait()
        copies[2 + 2 * part].wait()
        product = k_ref[:, lanes].astype(jnp.float32) * v_ref[:, lanes].astype(jnp.float32)
        gated_ref[part] = product.astype(jnp.bfloat16).astype(jnp.float32)
        factor = [full(jnp.exp(-row(decay_ref, n, part))) for n in range(modes)]

        def step(t, state):
            x = gated_ref[part, pl.ds(t, SUBLANES, stride=chunk_len), :]
            return tuple(f * h + x for f, h in zip(factor, state))

        zero = jnp.zeros((SUBLANES, LANES), jnp.float32)
        state = lax.fori_loop(0, chunk_len, step, (zero,) * modes, unroll=8)
        for n in range(modes):
            chunk_ref[n, :, lanes] = state[n]
            weight = jnp.exp(-row(decay_ref, n, part) * later)
            total_ref[n : n + 1, lanes] = jnp.sum(weight * state[n], axis=0, keepdims=True)
    for copy in copies[1 + 2 * parts :]:
        copy.wait()


def local_kernel(gated, decay_ref, residue_ref, skip_ref, chunk_ref, local_ref, short_ref):
    modes = decay_ref.shape[0]
    chunk_len = gated.shape[1] // SUBLANES
    index = lax.broadcasted_iota(jnp.int32, (SUBLANES, LANES), 0)
    for part in range(gated.shape[0]):
        lanes = lane_slice(part)
        factor, weight, start = [], [], []
        for n in range(modes):
            rate = row(decay_ref, n, part)
            prefix = chunk_ref[n, :, lanes]
            for shift in (1, 2, 4):
                moved = jnp.where(index >= shift, pltpu.roll(prefix, shift, 0), 0.0)
                prefix = prefix + jnp.exp(-rate * (shift * chunk_len)) * moved
            start.append(jnp.where(index >= 1, pltpu.roll(prefix, 1, 0), 0.0))
            factor.append(full(jnp.exp(-rate)))
            weight.append(full(row(residue_ref, n, part)))
        bypass = full(skip_ref[:, lanes])

        def step(t, state):
            rows = pl.ds(t, SUBLANES, stride=chunk_len)
            x = gated[part, rows, :]
            state = tuple(f * h + x for f, h in zip(factor, state))
            local_ref[part, rows, :] = tree_sum([w * h for w, h in zip(weight, state)] + [bypass * x])
            return state

        lax.fori_loop(0, chunk_len, step, tuple(start), unroll=4)
        short_ref[:, lanes] = local_ref[part].astype(short_ref.dtype)


def fold(rates, inner, total, received, stride, seg_len):
    place = lax.div(lax.axis_index("seq"), 2)
    radix = len(received) + 1
    spot = lax.rem(lax.div(place, stride), radix)
    offset = lax.rem(place, stride)

    def decayed(segments):
        return jnp.exp(-rates * (segments * 2 * seg_len).astype(jnp.float32))

    before = jnp.zeros_like(rates)
    whole = decayed((radix - 1 - spot) * stride) * total
    for i, block in enumerate(received):
        source = spot ^ (i + 1)
        past = source < spot
        gap = jnp.where(past, spot - 1 - source, 0) * stride
        before += jnp.where(past, decayed(gap) * block, 0.0)
        whole += decayed((radix - 1 - source) * stride) * block
    return inner + decayed(offset) * before, whole


def fold_kernel(stride, seg_len, rates_ref, total_ref, *rest):
    inner, rest = (rest[0][...], rest[1:]) if stride > 1 else (0.0, rest)
    received, (inner_out, total_out) = [ref[...] for ref in rest[:-2]], rest[-2:]
    inner_out[...], total_out[...] = fold(
        rates_ref[...], inner, total_ref[...], received, stride, seg_len
    )


def share_kernel(stride, seg_len, rates_ref, residue_ref, own_ref, total_ref, *rest):
    inner, rest = (rest[0][...], rest[1:]) if stride > 1 else (0.0, rest)
    received, (base_ref, extra_ref) = [ref[...] for ref in rest[:-2]], rest[-2:]
    modes = rates_ref.shape[0]
    rates = rates_ref[...]
    before, _ = fold(rates, inner, total_ref[...], received, stride, seg_len)
    before *= residue_ref[...]
    step = jnp.exp(-rates * float(seg_len))
    even = lax.rem(lax.axis_index("seq"), 2) == 0
    base_ref[:modes, :] = step * before
    base_ref[modes:, :] = rates
    extra_ref[...] = jnp.where(even, residue_ref[...] * own_ref[...] + step * step * before, before)


def carry_kernel(first, q_ref, local_ref, base_ref, extra_ref, out_ref):
    modes = extra_ref.shape[0]
    seg_len = q_ref.shape[0]
    block = 2 * SUBLANES
    ahead = (lax.broadcasted_iota(jnp.int32, (SUBLANES, LANES), 0) + 1).astype(jnp.float32)
    for index in range(out_ref.shape[1] // LANES):
        part = first + index
        lanes = lane_slice(part)
        factor, start = [], []
        for n in range(modes):
            rate = row(base_ref, modes + n, part)
            weight = row(base_ref, n, part) + row(extra_ref, n, part)
            start.append(weight * jnp.exp(-rate * ahead))
            factor.append(full(jnp.exp(-rate * SUBLANES)))

        def step(j, state):
            rows = pl.ds(pl.multiple_of(j * block, block), block)
            halves = []
            for _ in range(2):
                halves.append(tree_sum(list(state)))
                state = tuple(f * h for f, h in zip(factor, state))
            local = local_ref[part, rows, :] if len(local_ref.shape) == 3 else local_ref[rows, lanes]
            total = local.astype(jnp.float32) + jnp.concatenate(halves, axis=0)
            out_ref[rows, lane_slice(index)] = (q_ref[rows, lanes].astype(jnp.float32) * total).astype(out_ref.dtype)
            return state

        lax.fori_loop(0, seg_len // block, step, tuple(start), unroll=4)


def project(blocks, weight_ref):
    total = None
    for rank, parts in blocks:
        depth = weight_ref.shape[0] // lax.axis_size("chan")
        offset = pl.multiple_of(rank * depth, depth)
        for block in parts:
            rows = pl.ds(offset, block.shape[1])
            term = jnp.dot(block[...], weight_ref[rows, :], preferred_element_type=jnp.float32)
            total = term if total is None else total + term
            offset = pl.multiple_of(offset + block.shape[1], block.shape[1])
    return total


def near_kernel(weight_ref, bias_ref, *rest):
    blocks, out_ref = rest[:-1], rest[-1]
    rank = lax.axis_index("chan")
    parts = len(blocks) // 3
    blocks = [(rank ^ bit, blocks[i * parts : (i + 1) * parts]) for i, bit in enumerate((0, 2, 3))]
    out_ref[...] = project(blocks, weight_ref) + bias_ref[...]


def last_kernel(near_ref, weight_ref, *rest):
    pair, (out_hbm, out_ref, sems) = rest[:-3], rest[-3:]
    rank = lax.axis_index("chan")
    pieces = sems.shape[0]
    size = out_ref.shape[0] // pieces
    copies = []
    for i in range(pieces):
        rows = pl.ds(i * size, size)
        total = near_ref[rows, :] + project([(rank ^ 1, [ref.at[rows, :] for ref in pair])], weight_ref)
        out_ref[rows, :] = total.astype(out_ref.dtype)
        copies.append(pltpu.make_async_copy(out_ref.at[rows], out_hbm.at[rows], sems.at[i]))
        copies[-1].start()
    for copy in copies:
        copy.wait()


def call(kernel, out, *args, cost=0, scratch=(), ins=pltpu.VMEM, outs=pltpu.VMEM):
    return pl.pallas_call(
        kernel,
        out_shape=out,
        in_specs=[pl.BlockSpec(memory_space=ins)] * len(args),
        out_specs=jax.tree.map(lambda _: pl.BlockSpec(memory_space=outs), out),
        scratch_shapes=list(scratch),
        compiler_params=pltpu.CompilerParams(vmem_limit_bytes=VMEM_LIMIT),
        cost_estimate=pl.CostEstimate(flops=cost, bytes_accessed=0, transcendentals=0),
    )(*args)


def struct(shape, dtype=jnp.float32):
    return jax.ShapeDtypeStruct(shape, dtype)


def swapped(value, bit):
    count = lax.axis_size("chan")
    return lax.ppermute(value, "chan", [(r, r ^ bit) for r in range(count)])


def beside(value, step):
    count = lax.axis_size("seq")
    return lax.ppermute(value, "seq", [(r, r ^ step) for r in range(count)])


def corner(value, step, bit):
    count, width = lax.axis_size("seq"), lax.axis_size("chan")
    pairs = [(r * width + c, (r ^ step) * width + (c ^ bit)) for r in range(count) for c in range(width)]
    return lax.ppermute(value, ("seq", "chan"), pairs)


def carry_shares(total, decay, residue, seg_len, also):
    count = lax.axis_size("seq") // 2
    shape = struct(total.shape)
    own, inner, stride = total, (), 1
    while True:
        radix = min(4, count // stride)
        received = [beside(total, 2 * stride * step) for step in range(1, radix)]
        if stride * radix == count:
            break
        kernel = functools.partial(fold_kernel, stride, seg_len)
        *inner, total = call(kernel, [shape, shape], decay, total, *inner, *received)
        stride *= radix
    received, also = lax.optimization_barrier((received, also))
    kernel = functools.partial(share_kernel, stride, seg_len)
    outs = [struct((2 * total.shape[0], total.shape[1])), shape]
    base, extra = call(kernel, outs, decay, residue, own, total, *inner, *received, cost=FOLD_COST)
    return base, extra, also


def shards(q_gate, k_gate, value, decay, residue, skip, out_weight, out_bias):
    seg_len, channels = value.shape
    modes = decay.shape[0]
    cols = out_weight.shape[1]
    parts = channels // LANES
    tall = pltpu.VMEM((seg_len, channels), jnp.bfloat16)
    short = struct((seg_len, channels), jnp.bfloat16)
    q_across = swapped(q_gate, 2)
    inputs = (k_gate, value, decay, residue, skip.reshape(1, -1), out_bias.reshape(1, -1))
    total, chunks, gated, decay, residue, skip, bias = call(
        state_kernel,
        [
            struct((modes, channels)),
            struct((modes, SUBLANES, channels)),
            struct((parts, seg_len, LANES)),
            struct((modes, channels)),
            struct((modes, channels)),
            struct((1, channels)),
            struct((1, cols)),
        ],
        *(pltpu.with_memory_space_constraint(x, pltpu.HBM) for x in inputs),
        scratch=[tall, tall, pltpu.SemaphoreType.DMA((2 * parts + 4,))],
        ins=pltpu.HBM,
    )
    local, local_short = call(
        local_kernel, [struct((parts, seg_len, LANES)), short], gated, decay, residue, skip, chunks
    )
    local_across = swapped(local_short, 2)
    base, extra, q_across = carry_shares(total, decay, residue, seg_len, q_across)
    extra_corner = corner(extra, 1, 2)
    extra_beside = beside(extra, 1)
    base_across = swapped(base, 2)
    half = struct((seg_len, LANES), jnp.bfloat16)
    across = [
        call(
            functools.partial(carry_kernel, part), half, q_across, local_across, base_across, extra_corner,
            cost=PART_COST,
        )
        for part in range(parts)
    ]
    diagonal = [swapped(block, 1) for block in across]
    (extra_beside, *across) = lax.optimization_barrier((extra_beside, *across))
    own = [
        call(functools.partial(carry_kernel, part), half, q_gate, local, base, extra_beside, cost=PART_COST)
        for part in range(parts)
    ]
    pair = [swapped(block, 1) for block in own]
    near = call(near_kernel, struct((seg_len, cols)), out_weight, bias, *own, *across, *diagonal, cost=NEAR_COST)
    return call(
        last_kernel, struct((seg_len, cols), jnp.bfloat16), near, out_weight, *pair,
        scratch=[pltpu.VMEM((seg_len, cols), jnp.bfloat16), pltpu.SemaphoreType.DMA((STORES,))],
        outs=pltpu.HBM,
    )


def solution(mesh):
    return jax.shard_map(
        shards,
        mesh=mesh,
        in_specs=(
            P("seq", "chan"),
            P("seq", "chan"),
            P("seq", "chan"),
            P(None, "chan"),
            P(None, "chan"),
            P("chan"),
            P(None, "chan"),
            P("chan"),
        ),
        out_specs=P("seq", "chan"),
        check_vma=False,
    )
```

```python
import functools

import jax
import jax.numpy as jnp
from jax import lax
from jax.experimental import pallas as pl
from jax.experimental.pallas import tpu as pltpu
from jax.sharding import PartitionSpec as P

LANES = 128
SUBLANES = 8
STORES = 2
FOLD_COST = 1000000000
TREE_COST = 3000000000
PIECES = 3
PART_COST = 4000000000
VMEM_LIMIT = 32 * 1024 * 1024


def row(ref, mode, part):
    return ref[mode : mode + 1, part * LANES : (part + 1) * LANES]


def full(value):
    return jnp.broadcast_to(value, (SUBLANES, LANES))


def tree_sum(terms):
    while len(terms) > 1:
        paired = [a + b for a, b in zip(terms[::2], terms[1::2])]
        terms = paired + ([terms[-1]] if len(terms) % 2 else [])
    return terms[0]


def lane_slice(part):
    return slice(part * LANES, (part + 1) * LANES)


def state_kernel(
    k_hbm, v_hbm, decay_hbm, residue_hbm, skip_hbm, bias_hbm,
    total_ref, chunk_ref, gated_ref, decay_ref, residue_ref, skip_ref, bias_ref,
    k_ref, v_ref, sems,
):
    modes = decay_hbm.shape[0]
    parts = gated_ref.shape[0]
    chunk_len = k_ref.shape[0] // SUBLANES
    pairs = [(decay_hbm, decay_ref)]
    for part in range(parts):
        lanes = pl.ds(part * LANES, LANES)
        pairs += [(k_hbm.at[:, lanes], k_ref.at[:, lanes]), (v_hbm.at[:, lanes], v_ref.at[:, lanes])]
    pairs += [(residue_hbm, residue_ref), (skip_hbm, skip_ref), (bias_hbm, bias_ref)]
    copies = [pltpu.make_async_copy(src, dst, sems.at[i]) for i, (src, dst) in enumerate(pairs)]
    for copy in copies:
        copy.start()
    copies[0].wait()
    later = (SUBLANES - 1 - lax.broadcasted_iota(jnp.int32, (SUBLANES, LANES), 0)) * chunk_len
    later = later.astype(jnp.float32)
    for part in range(parts):
        lanes = lane_slice(part)
        copies[1 + 2 * part].wait()
        copies[2 + 2 * part].wait()
        product = k_ref[:, lanes].astype(jnp.float32) * v_ref[:, lanes].astype(jnp.float32)
        gated_ref[part] = product.astype(jnp.bfloat16).astype(jnp.float32)
        factor = [full(jnp.exp(-row(decay_ref, n, part))) for n in range(modes)]

        def step(t, state):
            x = gated_ref[part, pl.ds(t, SUBLANES, stride=chunk_len), :]
            return tuple(f * h + x for f, h in zip(factor, state))

        zero = jnp.zeros((SUBLANES, LANES), jnp.float32)
        state = lax.fori_loop(0, chunk_len, step, (zero,) * modes, unroll=8)
        for n in range(modes):
            chunk_ref[n, :, lanes] = state[n]
            weight = jnp.exp(-row(decay_ref, n, part) * later)
            total_ref[n : n + 1, lanes] = jnp.sum(weight * state[n], axis=0, keepdims=True)
    for copy in copies[1 + 2 * parts :]:
        copy.wait()


def local_kernel(gated, decay_ref, residue_ref, skip_ref, chunk_ref, local_ref, short_ref):
    modes = decay_ref.shape[0]
    chunk_len = gated.shape[1] // SUBLANES
    index = lax.broadcasted_iota(jnp.int32, (SUBLANES, LANES), 0)
    for part in range(gated.shape[0]):
        lanes = lane_slice(part)
        factor, weight, start = [], [], []
        for n in range(modes):
            rate = row(decay_ref, n, part)
            prefix = chunk_ref[n, :, lanes]
            for shift in (1, 2, 4):
                moved = jnp.where(index >= shift, pltpu.roll(prefix, shift, 0), 0.0)
                prefix = prefix + jnp.exp(-rate * (shift * chunk_len)) * moved
            start.append(jnp.where(index >= 1, pltpu.roll(prefix, 1, 0), 0.0))
            factor.append(full(jnp.exp(-rate)))
            weight.append(full(row(residue_ref, n, part)))
        bypass = full(skip_ref[:, lanes])

        def step(t, state):
            rows = pl.ds(t, SUBLANES, stride=chunk_len)
            x = gated[part, rows, :]
            state = tuple(f * h + x for f, h in zip(factor, state))
            local_ref[part, rows, :] = tree_sum([w * h for w, h in zip(weight, state)] + [bypass * x])
            return state

        lax.fori_loop(0, chunk_len, step, tuple(start), unroll=4)
        short_ref[: local_ref.shape[1], lanes] = local_ref[part].astype(short_ref.dtype)
    left = decay_ref[...]
    for first in range(local_ref.shape[1], short_ref.shape[0], modes):
        piece = left.astype(short_ref.dtype)
        short_ref[first : first + modes, :] = piece
        left = left - piece.astype(jnp.float32)


def tree_step(rates, before, received, seg_len):
    reach = len(received)
    spot = lax.rem(lax.div(lax.axis_index("seq"), 2), 2 * reach)
    for i, block in enumerate(received):
        weight = jnp.exp(-rates * float(2 * seg_len * i))
        before = before + jnp.where(spot == reach + i, weight * block, 0.0)
    return before


def fold_kernel(seg_len, rates_ref, own_ref, *rest):
    received, (before_ref, total_ref) = [ref[...] for ref in rest[:-2]], rest[-2:]
    before, received = (received[0], received[1:]) if len(received) > 1 else (0.0, received)
    rates = rates_ref[...]
    before = tree_step(rates, before, received, seg_len)
    before_ref[...] = before
    total_ref[...] = own_ref[...] + jnp.exp(-rates * float(2 * seg_len)) * before


def share_kernel(seg_len, rates_ref, residue_ref, own_ref, before_ref, *rest):
    received, (base_ref, extra_ref) = [ref[...] for ref in rest[:-2]], rest[-2:]
    rates, residue = rates_ref[...], residue_ref[...]
    before = residue * tree_step(rates, before_ref[...], received, seg_len)
    step = jnp.exp(-rates * float(seg_len))
    even = lax.rem(lax.axis_index("seq"), 2) == 0
    base_ref[...] = step * before
    extra_ref[...] = jnp.where(even, residue * own_ref[...] + step * step * before, before)


def read_rates(rates_ref, modes):
    if rates_ref.shape[0] == modes:
        return rates_ref[...]
    count = rates_ref.shape[0] // modes
    pieces = [rates_ref[i * modes : (i + 1) * modes, :].astype(jnp.float32) for i in range(count)]
    return (pieces[2] + pieces[1]) + pieces[0]


def carry_kernel(first, q_ref, local_ref, rates_ref, base_ref, extra_ref, out_ref):
    modes = extra_ref.shape[0]
    seg_len = q_ref.shape[0]
    if rates_ref is None:
        rates_ref = local_ref.at[pl.ds(seg_len, PIECES * modes), :]
    rates = read_rates(rates_ref, modes)
    block = 2 * SUBLANES
    ahead = (lax.broadcasted_iota(jnp.int32, (SUBLANES, LANES), 0) + 1).astype(jnp.float32)
    for index in range(out_ref.shape[1] // LANES):
        part = first + index
        lanes = lane_slice(part)
        factor, start = [], []
        for n in range(modes):
            rate = rates[n : n + 1, lanes]
            weight = row(base_ref, n, part) + row(extra_ref, n, part)
            start.append(weight * jnp.exp(-rate * ahead))
            factor.append(full(jnp.exp(-rate * SUBLANES)))

        def step(j, state):
            rows = pl.ds(pl.multiple_of(j * block, block), block)
            halves = []
            for _ in range(2):
                halves.append(tree_sum(list(state)))
                state = tuple(f * h for f, h in zip(factor, state))
            local = local_ref[part, rows, :] if len(local_ref.shape) == 3 else local_ref[rows, lanes]
            total = local.astype(jnp.float32) + jnp.concatenate(halves, axis=0)
            out_ref[rows, lane_slice(index)] = (q_ref[rows, lanes].astype(jnp.float32) * total).astype(out_ref.dtype)
            return state

        lax.fori_loop(0, seg_len // block, step, tuple(start), unroll=4)


def across_kernel(first, q_ref, local_ref, base_ref, extra_ref, out_ref):
    carry_kernel(first, q_ref, local_ref, None, base_ref, extra_ref, out_ref)


def project(blocks, weight_ref):
    total = None
    for rank, parts in blocks:
        depth = weight_ref.shape[0] // lax.axis_size("chan")
        offset = pl.multiple_of(rank * depth, depth)
        for block in parts:
            rows = pl.ds(offset, block.shape[1])
            term = jnp.dot(block[...], weight_ref[rows, :], preferred_element_type=jnp.float32)
            total = term if total is None else total + term
            offset = pl.multiple_of(offset + block.shape[1], block.shape[1])
    return total


def near_kernel(weight_ref, bias_ref, own_ref, pair_ref, *rest):
    across, out_ref = rest[:-1], rest[-1]
    rank = lax.axis_index("chan")
    blocks = [(rank, [own_ref]), (rank ^ 1, [pair_ref]), (rank ^ 2, across)]
    out_ref[...] = project(blocks, weight_ref) + bias_ref[...]


def last_kernel(near_ref, weight_ref, *rest):
    diagonal, (out_hbm, out_ref, sems) = rest[:-3], rest[-3:]
    rank = lax.axis_index("chan")
    pieces = sems.shape[0]
    size = out_ref.shape[0] // pieces
    copies = []
    for i in range(pieces):
        rows = pl.ds(i * size, size)
        total = near_ref[rows, :] + project([(rank ^ 3, [ref.at[rows, :] for ref in diagonal])], weight_ref)
        out_ref[rows, :] = total.astype(out_ref.dtype)
        copies.append(pltpu.make_async_copy(out_ref.at[rows], out_hbm.at[rows], sems.at[i]))
        copies[-1].start()
    for copy in copies:
        copy.wait()


def call(kernel, out, *args, cost=0, scratch=(), ins=pltpu.VMEM, outs=pltpu.VMEM):
    return pl.pallas_call(
        kernel,
        out_shape=out,
        in_specs=[pl.BlockSpec(memory_space=ins)] * len(args),
        out_specs=jax.tree.map(lambda _: pl.BlockSpec(memory_space=outs), out),
        scratch_shapes=list(scratch),
        compiler_params=pltpu.CompilerParams(vmem_limit_bytes=VMEM_LIMIT),
        cost_estimate=pl.CostEstimate(flops=cost, bytes_accessed=0, transcendentals=0),
    )(*args)


def struct(shape, dtype=jnp.float32):
    return jax.ShapeDtypeStruct(shape, dtype)


def swapped(value, bit):
    count = lax.axis_size("chan")
    return lax.ppermute(value, "chan", [(r, r ^ bit) for r in range(count)])


def beside(value):
    count = lax.axis_size("seq")
    return lax.ppermute(value, "seq", [(r, r ^ 1) for r in range(count)])


def tree_sends(value, reach):
    count = lax.axis_size("seq")
    received = []
    for i in reversed(range(reach)):
        target = list(range(count))
        for r in range(count):
            if r // 2 % (2 * reach) == reach - 1:
                other = r + 2 * (i + 1)
                target[r], target[other] = other, r
        received.append(lax.ppermute(value, "seq", list(enumerate(target))))
    return received[::-1]


def corner(value, step, bit):
    count, width = lax.axis_size("seq"), lax.axis_size("chan")
    pairs = [(r * width + c, (r ^ step) * width + (c ^ bit)) for r in range(count) for c in range(width)]
    return lax.ppermute(value, ("seq", "chan"), pairs)


def carry_shares(own, decay, residue, seg_len, also):
    count = lax.axis_size("seq") // 2
    shape = struct(own.shape)
    total, before, reach = own, (), 1
    while 2 * reach < count:
        received = tree_sends(total, reach)
        before, total = call(
            functools.partial(fold_kernel, seg_len), [shape, shape], decay, own, *before, *received, cost=TREE_COST
        )
        before, reach = (before,), 2 * reach
    received, also = lax.optimization_barrier((tree_sends(total, reach), also))
    base, extra = call(
        functools.partial(share_kernel, seg_len), [shape, shape], decay, residue, own, *before, *received,
        cost=FOLD_COST,
    )
    return base, extra, also


def shards(q_gate, k_gate, value, decay, residue, skip, out_weight, out_bias):
    seg_len, channels = value.shape
    modes = decay.shape[0]
    cols = out_weight.shape[1]
    parts = channels // LANES
    tall = pltpu.VMEM((seg_len, channels), jnp.bfloat16)
    short = struct((seg_len, channels), jnp.bfloat16)
    taller = struct((seg_len + PIECES * modes, channels), jnp.bfloat16)
    q_across = swapped(q_gate, 2)
    inputs = (k_gate, value, decay, residue, skip.reshape(1, -1), out_bias.reshape(1, -1))
    total, chunks, gated, decay, residue, skip, bias = call(
        state_kernel,
        [
            struct((modes, channels)),
            struct((modes, SUBLANES, channels)),
            struct((parts, seg_len, LANES)),
            struct((modes, channels)),
            struct((modes, channels)),
            struct((1, channels)),
            struct((1, cols)),
        ],
        *(pltpu.with_memory_space_constraint(x, pltpu.HBM) for x in inputs),
        scratch=[tall, tall, pltpu.SemaphoreType.DMA((2 * parts + 4,))],
        ins=pltpu.HBM,
    )
    local, local_short = call(
        local_kernel, [struct((parts, seg_len, LANES)), taller], gated, decay, residue, skip, chunks
    )
    local_across = swapped(local_short, 2)
    base, extra, q_across = carry_shares(total, decay, residue, seg_len, q_across)
    extra_beside = beside(extra)
    extra_corner = corner(extra, 1, 2)
    base_across = swapped(base, 2)
    own = call(functools.partial(carry_kernel, 0), short, q_gate, local, decay, base, extra_beside)
    pair = swapped(own, 1)
    half = struct((seg_len, LANES), jnp.bfloat16)
    across = [
        call(
            functools.partial(across_kernel, part), half, q_across, local_across, base_across, extra_corner,
            cost=PART_COST,
        )
        for part in range(parts)
    ]
    diagonal = [swapped(block, 1) for block in across]
    near = call(near_kernel, struct((seg_len, cols)), out_weight, bias, own, pair, *across)
    return call(
        last_kernel, struct((seg_len, cols), jnp.bfloat16), near, out_weight, *diagonal,
        scratch=[pltpu.VMEM((seg_len, cols), jnp.bfloat16), pltpu.SemaphoreType.DMA((STORES,))],
        outs=pltpu.HBM,
    )


def solution(mesh):
    return jax.shard_map(
        shards,
        mesh=mesh,
        in_specs=(
            P("seq", "chan"),
            P("seq", "chan"),
            P("seq", "chan"),
            P(None, "chan"),
            P(None, "chan"),
            P("chan"),
            P(None, "chan"),
            P("chan"),
        ),
        out_specs=P("seq", "chan"),
        check_vma=False,
    )
```

```python
import functools

import jax
import jax.numpy as jnp
from jax import lax
from jax.experimental import pallas as pl
from jax.experimental.pallas import tpu as pltpu
from jax.sharding import PartitionSpec as P

LANES = 128
SUBLANES = 8
STORES = 2
FOLD_COST = 3000000000
PIECES = 3
PART_COST = 4000000000
VMEM_LIMIT = 32 * 1024 * 1024


def row(ref, mode, part):
    return ref[mode : mode + 1, part * LANES : (part + 1) * LANES]


def full(value):
    return jnp.broadcast_to(value, (SUBLANES, LANES))


def tree_sum(terms):
    while len(terms) > 1:
        paired = [a + b for a, b in zip(terms[::2], terms[1::2])]
        terms = paired + ([terms[-1]] if len(terms) % 2 else [])
    return terms[0]


def lane_slice(part):
    return slice(part * LANES, (part + 1) * LANES)


def state_kernel(
    k_hbm, v_hbm, decay_hbm, residue_hbm, skip_hbm, bias_hbm,
    total_ref, chunk_ref, gated_ref, local_ref, short_ref, decay_ref, residue_ref, skip_ref, bias_ref,
    k_ref, v_ref, sems,
):
    modes = decay_hbm.shape[0]
    parts = gated_ref.shape[0]
    chunk_len = k_ref.shape[0] // SUBLANES
    pairs = [(decay_hbm, decay_ref)]
    for part in range(parts):
        lanes = pl.ds(part * LANES, LANES)
        pairs += [(k_hbm.at[:, lanes], k_ref.at[:, lanes]), (v_hbm.at[:, lanes], v_ref.at[:, lanes])]
    pairs += [(residue_hbm, residue_ref), (skip_hbm, skip_ref), (bias_hbm, bias_ref)]
    copies = [pltpu.make_async_copy(src, dst, sems.at[i]) for i, (src, dst) in enumerate(pairs)]
    for copy in copies:
        copy.start()
    copies[0].wait()
    later = (SUBLANES - 1 - lax.broadcasted_iota(jnp.int32, (SUBLANES, LANES), 0)) * chunk_len
    later = later.astype(jnp.float32)
    for part in range(parts):
        lanes = lane_slice(part)
        copies[1 + 2 * part].wait()
        copies[2 + 2 * part].wait()
        product = k_ref[:, lanes].astype(jnp.float32) * v_ref[:, lanes].astype(jnp.float32)
        gated_ref[part] = product.astype(jnp.bfloat16).astype(jnp.float32)
        factor = [full(jnp.exp(-row(decay_ref, n, part))) for n in range(modes)]

        def step(t, state):
            x = gated_ref[part, pl.ds(t, SUBLANES, stride=chunk_len), :]
            return tuple(f * h + x for f, h in zip(factor, state))

        zero = jnp.zeros((SUBLANES, LANES), jnp.float32)
        state = lax.fori_loop(0, chunk_len, step, (zero,) * modes, unroll=8)
        for n in range(modes):
            chunk_ref[n, :, lanes] = state[n]
            weight = jnp.exp(-row(decay_ref, n, part) * later)
            total_ref[n : n + 1, lanes] = jnp.sum(weight * state[n], axis=0, keepdims=True)
    for copy in copies[1 + 2 * parts :]:
        copy.wait()

    @pl.when(runs_early())
    def _():
        convolve(gated_ref, decay_ref, residue_ref, skip_ref, chunk_ref, local_ref, short_ref)


def convolve(gated, decay_ref, residue_ref, skip_ref, chunk_ref, local_ref, short_ref):
    modes = decay_ref.shape[0]
    chunk_len = gated.shape[1] // SUBLANES
    index = lax.broadcasted_iota(jnp.int32, (SUBLANES, LANES), 0)
    for part in range(gated.shape[0]):
        lanes = lane_slice(part)
        factor, weight, start = [], [], []
        for n in range(modes):
            rate = row(decay_ref, n, part)
            prefix = chunk_ref[n, :, lanes]
            for shift in (1, 2, 4):
                moved = jnp.where(index >= shift, pltpu.roll(prefix, shift, 0), 0.0)
                prefix = prefix + jnp.exp(-rate * (shift * chunk_len)) * moved
            start.append(jnp.where(index >= 1, pltpu.roll(prefix, 1, 0), 0.0))
            factor.append(full(jnp.exp(-rate)))
            weight.append(full(row(residue_ref, n, part)))
        bypass = full(skip_ref[:, lanes])

        def step(t, state):
            rows = pl.ds(t, SUBLANES, stride=chunk_len)
            x = gated[part, rows, :]
            state = tuple(f * h + x for f, h in zip(factor, state))
            local_ref[part, rows, :] = tree_sum([w * h for w, h in zip(weight, state)] + [bypass * x])
            return state

        lax.fori_loop(0, chunk_len, step, tuple(start), unroll=4)
        short_ref[: local_ref.shape[1], lanes] = local_ref[part].astype(short_ref.dtype)
    left = decay_ref[...]
    for first in range(local_ref.shape[1], short_ref.shape[0], modes):
        piece = left.astype(short_ref.dtype)
        short_ref[first : first + modes, :] = piece
        left = left - piece.astype(jnp.float32)


def runs_early():
    count = lax.axis_size("seq")
    return lax.axis_index("seq") < count - count // 4


def local_kernel(gated, decay_ref, residue_ref, skip_ref, chunk_ref, local_in, short_in, local_ref, short_ref):
    del local_in, short_in

    @pl.when(jnp.logical_not(runs_early()))
    def _():
        convolve(gated, decay_ref, residue_ref, skip_ref, chunk_ref, local_ref, short_ref)


def fold(rates, inner, total, received, stride, seg_len):
    place = lax.div(lax.axis_index("seq"), 2)
    radix = len(received) + 1
    spot = lax.rem(lax.div(place, stride), radix)
    offset = lax.rem(place, stride)

    def decayed(segments):
        return jnp.exp(-rates * (segments * 2 * seg_len).astype(jnp.float32))

    before = jnp.zeros_like(rates)
    whole = decayed((radix - 1 - spot) * stride) * total
    for i, block in enumerate(received):
        source = spot ^ (radix - 1 - i)
        past = source < spot
        gap = jnp.where(past, spot - 1 - source, 0) * stride
        before += jnp.where(past, decayed(gap) * block, 0.0)
        whole += decayed((radix - 1 - source) * stride) * block
    return inner + decayed(offset) * before, whole


def fold_kernel(stride, seg_len, rates_ref, total_ref, *rest):
    inner, rest = (rest[0][...], rest[1:]) if stride > 1 else (0.0, rest)
    received, (inner_out, total_out) = [ref[...] for ref in rest[:-2]], rest[-2:]
    inner_out[...], total_out[...] = fold(
        rates_ref[...], inner, total_ref[...], received, stride, seg_len
    )


def share_kernel(stride, seg_len, rates_ref, residue_ref, own_ref, total_ref, *rest):
    inner, rest = (rest[0][...], rest[1:]) if stride > 1 else (0.0, rest)
    received, (base_ref, extra_ref) = [ref[...] for ref in rest[:-2]], rest[-2:]
    rates = rates_ref[...]
    before, _ = fold(rates, inner, total_ref[...], received, stride, seg_len)
    before *= residue_ref[...]
    step = jnp.exp(-rates * float(seg_len))
    even = lax.rem(lax.axis_index("seq"), 2) == 0
    base_ref[...] = step * before
    extra_ref[...] = jnp.where(even, residue_ref[...] * own_ref[...] + step * step * before, before)


def read_rates(rates_ref, modes):
    if rates_ref.shape[0] == modes:
        return rates_ref[...]
    count = rates_ref.shape[0] // modes
    pieces = [rates_ref[i * modes : (i + 1) * modes, :].astype(jnp.float32) for i in range(count)]
    return (pieces[2] + pieces[1]) + pieces[0]


def carry_kernel(first, q_ref, local_ref, rates_ref, base_ref, extra_ref, out_ref):
    modes = extra_ref.shape[0]
    seg_len = q_ref.shape[0]
    if rates_ref is None:
        rates_ref = local_ref.at[pl.ds(seg_len, PIECES * modes), :]
    rates = read_rates(rates_ref, modes)
    block = 2 * SUBLANES
    ahead = (lax.broadcasted_iota(jnp.int32, (SUBLANES, LANES), 0) + 1).astype(jnp.float32)
    for index in range(out_ref.shape[1] // LANES):
        part = first + index
        lanes = lane_slice(part)
        factor, start = [], []
        for n in range(modes):
            rate = rates[n : n + 1, lanes]
            weight = row(base_ref, n, part) + row(extra_ref, n, part)
            start.append(weight * jnp.exp(-rate * ahead))
            factor.append(full(jnp.exp(-rate * SUBLANES)))

        def step(j, state):
            rows = pl.ds(pl.multiple_of(j * block, block), block)
            halves = []
            for _ in range(2):
                halves.append(tree_sum(list(state)))
                state = tuple(f * h for f, h in zip(factor, state))
            local = local_ref[part, rows, :] if len(local_ref.shape) == 3 else local_ref[rows, lanes]
            total = local.astype(jnp.float32) + jnp.concatenate(halves, axis=0)
            out_ref[rows, lane_slice(index)] = (q_ref[rows, lanes].astype(jnp.float32) * total).astype(out_ref.dtype)
            return state

        lax.fori_loop(0, seg_len // block, step, tuple(start), unroll=4)


def across_kernel(first, extra_ref, base_ref, q_ref, local_ref, out_ref):
    carry_kernel(first, q_ref, local_ref, None, base_ref, extra_ref, out_ref)


def project(blocks, weight_ref):
    total = None
    for rank, parts in blocks:
        depth = weight_ref.shape[0] // lax.axis_size("chan")
        offset = pl.multiple_of(rank * depth, depth)
        for block in parts:
            rows = pl.ds(offset, block.shape[1])
            term = jnp.dot(block[...], weight_ref[rows, :], preferred_element_type=jnp.float32)
            total = term if total is None else total + term
            offset = pl.multiple_of(offset + block.shape[1], block.shape[1])
    return total


def near_kernel(weight_ref, bias_ref, own_ref, pair_ref, *rest):
    across, out_ref = rest[:-1], rest[-1]
    rank = lax.axis_index("chan")
    blocks = [(rank, [own_ref]), (rank ^ 1, [pair_ref]), (rank ^ 2, across)]
    out_ref[...] = project(blocks, weight_ref) + bias_ref[...]


def last_kernel(near_ref, weight_ref, *rest):
    diagonal, (out_hbm, out_ref, sems) = rest[:-3], rest[-3:]
    rank = lax.axis_index("chan")
    pieces = sems.shape[0]
    size = out_ref.shape[0] // pieces
    copies = []
    for i in range(pieces):
        rows = pl.ds(i * size, size)
        total = near_ref[rows, :] + project([(rank ^ 3, [ref.at[rows, :] for ref in diagonal])], weight_ref)
        out_ref[rows, :] = total.astype(out_ref.dtype)
        copies.append(pltpu.make_async_copy(out_ref.at[rows], out_hbm.at[rows], sems.at[i]))
        copies[-1].start()
    for copy in copies:
        copy.wait()


def call(kernel, out, *args, cost=0, aliases=(), scratch=(), ins=pltpu.VMEM, outs=pltpu.VMEM):
    return pl.pallas_call(
        kernel,
        out_shape=out,
        in_specs=[pl.BlockSpec(memory_space=ins)] * len(args),
        out_specs=jax.tree.map(lambda _: pl.BlockSpec(memory_space=outs), out),
        scratch_shapes=list(scratch),
        input_output_aliases=dict(aliases),
        compiler_params=pltpu.CompilerParams(vmem_limit_bytes=VMEM_LIMIT),
        cost_estimate=pl.CostEstimate(flops=cost, bytes_accessed=0, transcendentals=0),
    )(*args)


def struct(shape, dtype=jnp.float32):
    return jax.ShapeDtypeStruct(shape, dtype)


def swapped(value, bit):
    count = lax.axis_size("chan")
    return lax.ppermute(value, "chan", [(r, r ^ bit) for r in range(count)])


def beside(value, step):
    count = lax.axis_size("seq")
    return lax.ppermute(value, "seq", [(r, r ^ step) for r in range(count)])


def corner(value, step, bit):
    count, width = lax.axis_size("seq"), lax.axis_size("chan")
    pairs = [(r * width + c, (r ^ step) * width + (c ^ bit)) for r in range(count) for c in range(width)]
    return lax.ppermute(value, ("seq", "chan"), pairs)


def carry_shares(total, decay, residue, seg_len, also):
    count = lax.axis_size("seq") // 2
    shape = struct(total.shape)
    own, inner, stride = total, (), 1
    while True:
        radix = min(4, count // stride)
        received = [beside(total, 2 * stride * step) for step in reversed(range(1, radix))]
        if stride * radix == count:
            break
        kernel = functools.partial(fold_kernel, stride, seg_len)
        *inner, total = call(kernel, [shape, shape], decay, total, *inner, *received)
        stride *= radix
    received, also = lax.optimization_barrier((received, also))
    kernel = functools.partial(share_kernel, stride, seg_len)
    base, extra = call(kernel, [shape, shape], decay, residue, own, total, *inner, *received, cost=FOLD_COST)
    return base, extra, also


def shards(q_gate, k_gate, value, decay, residue, skip, out_weight, out_bias):
    seg_len, channels = value.shape
    modes = decay.shape[0]
    cols = out_weight.shape[1]
    parts = channels // LANES
    tall = pltpu.VMEM((seg_len, channels), jnp.bfloat16)
    short = struct((seg_len, channels), jnp.bfloat16)
    taller = struct((seg_len + PIECES * modes, channels), jnp.bfloat16)
    q_across = swapped(q_gate, 2)
    inputs = (k_gate, value, decay, residue, skip.reshape(1, -1), out_bias.reshape(1, -1))
    total, chunks, gated, local, local_short, decay, residue, skip, bias = call(
        state_kernel,
        [
            struct((modes, channels)),
            struct((modes, SUBLANES, channels)),
            struct((parts, seg_len, LANES)),
            struct((parts, seg_len, LANES)),
            taller,
            struct((modes, channels)),
            struct((modes, channels)),
            struct((1, channels)),
            struct((1, cols)),
        ],
        *(pltpu.with_memory_space_constraint(x, pltpu.HBM) for x in inputs),
        scratch=[tall, tall, pltpu.SemaphoreType.DMA((2 * parts + 4,))],
        ins=pltpu.HBM,
    )
    local, local_short = call(
        local_kernel,
        [struct((parts, seg_len, LANES)), taller],
        gated, decay, residue, skip, chunks, local, local_short,
        aliases={5: 0, 6: 1},
    )
    local_across = swapped(local_short, 2)
    base, extra, q_across = carry_shares(total, decay, residue, seg_len, q_across)
    extra_beside = beside(extra, 1)
    extra_corner = corner(extra, 1, 2)
    base_across = swapped(base, 2)
    own = call(functools.partial(carry_kernel, 0), short, q_gate, local, decay, base, extra_beside)
    pair = swapped(own, 1)
    half = struct((seg_len, LANES), jnp.bfloat16)
    across = [
        call(
            functools.partial(across_kernel, part), half, extra_corner, base_across, q_across, local_across,
            cost=PART_COST,
        )
        for part in range(parts)
    ]
    diagonal = [swapped(block, 1) for block in across]
    near = call(near_kernel, struct((seg_len, cols)), out_weight, bias, own, pair, *across)
    return call(
        last_kernel, struct((seg_len, cols), jnp.bfloat16), near, out_weight, *diagonal,
        scratch=[pltpu.VMEM((seg_len, cols), jnp.bfloat16), pltpu.SemaphoreType.DMA((STORES,))],
        outs=pltpu.HBM,
    )


def solution(mesh):
    return jax.shard_map(
        shards,
        mesh=mesh,
        in_specs=(
            P("seq", "chan"),
            P("seq", "chan"),
            P("seq", "chan"),
            P(None, "chan"),
            P(None, "chan"),
            P("chan"),
            P(None, "chan"),
            P("chan"),
        ),
        out_specs=P("seq", "chan"),
        check_vma=False,
    )
```

```python
import functools

import jax
import jax.numpy as jnp
from jax import lax
from jax.experimental import pallas as pl
from jax.experimental.pallas import tpu as pltpu
from jax.sharding import PartitionSpec as P

LANES = 128
SUBLANES = 8
STORES = 2
OWN_COST = 1000000000
MORE_COST = 1000000000
FOLD_COST = 500000000
PIECES = 3
INPUTS = 6
KEPT = 6
PART_COST = 4000000000
VMEM_LIMIT = 32 * 1024 * 1024


def row(ref, mode, part):
    return ref[mode : mode + 1, part * LANES : (part + 1) * LANES]


def full(value):
    return jnp.broadcast_to(value, (SUBLANES, LANES))


def tree_sum(terms):
    while len(terms) > 1:
        paired = [a + b for a, b in zip(terms[::2], terms[1::2])]
        terms = paired + ([terms[-1]] if len(terms) % 2 else [])
    return terms[0]


def lane_slice(part):
    return slice(part * LANES, (part + 1) * LANES)


def summarize(
    k_hbm, v_hbm, decay_hbm, residue_hbm, skip_hbm, bias_hbm,
    total_ref, chunk_ref, gated_ref, decay_ref, residue_ref, skip_ref, bias_ref,
    k_ref, v_ref, sems,
):
    modes = decay_hbm.shape[0]
    parts = gated_ref.shape[0]
    chunk_len = k_ref.shape[0] // SUBLANES
    pairs = [(decay_hbm, decay_ref)]
    for part in range(parts):
        lanes = pl.ds(part * LANES, LANES)
        pairs += [(k_hbm.at[:, lanes], k_ref.at[:, lanes]), (v_hbm.at[:, lanes], v_ref.at[:, lanes])]
    pairs += [(residue_hbm, residue_ref), (skip_hbm, skip_ref), (bias_hbm, bias_ref)]
    copies = [pltpu.make_async_copy(src, dst, sems.at[i]) for i, (src, dst) in enumerate(pairs)]
    for copy in copies:
        copy.start()
    copies[0].wait()
    later = (SUBLANES - 1 - lax.broadcasted_iota(jnp.int32, (SUBLANES, LANES), 0)) * chunk_len
    later = later.astype(jnp.float32)
    for part in range(parts):
        lanes = lane_slice(part)
        copies[1 + 2 * part].wait()
        copies[2 + 2 * part].wait()
        product = k_ref[:, lanes].astype(jnp.float32) * v_ref[:, lanes].astype(jnp.float32)
        gated_ref[part] = product.astype(jnp.bfloat16).astype(jnp.float32)
        factor = [full(jnp.exp(-row(decay_ref, n, part))) for n in range(modes)]

        def step(t, state):
            x = gated_ref[part, pl.ds(t, SUBLANES, stride=chunk_len), :]
            return tuple(f * h + x for f, h in zip(factor, state))

        zero = jnp.zeros((SUBLANES, LANES), jnp.float32)
        state = lax.fori_loop(0, chunk_len, step, (zero,) * modes, unroll=8)
        for n in range(modes):
            chunk_ref[n, :, lanes] = state[n]
            weight = jnp.exp(-row(decay_ref, n, part) * later)
            total_ref[n : n + 1, lanes] = jnp.sum(weight * state[n], axis=0, keepdims=True)
    for copy in copies[1 + 2 * parts :]:
        copy.wait()


def is_last():
    count = lax.axis_size("seq")
    return lax.axis_index("seq") >= count - 2


def state_kernel(*refs):
    total_ref = refs[INPUTS]

    @pl.when(jnp.logical_not(is_last()))
    def _():
        summarize(*refs)

    @pl.when(is_last())
    def _():
        total_ref[...] = jnp.zeros_like(total_ref)


def local_kernel(*refs):
    inputs, rest = refs[:INPUTS], refs[INPUTS:]
    total_in, rest = rest[0], rest[1 + KEPT :]
    total_ref, kept, (local_ref, short_ref), scratch = rest[0], rest[1 : 1 + KEPT], rest[1 + KEPT : -3], rest[-3:]
    chunk_ref, gated_ref, decay_ref, residue_ref, skip_ref, _ = kept

    @pl.when(is_last())
    def _():
        summarize(*inputs, total_ref, *kept, *scratch)

    @pl.when(jnp.logical_not(is_last()))
    def _():
        total_ref[...] = total_in[...]

    convolve(0, gated_ref, decay_ref, residue_ref, skip_ref, chunk_ref, local_ref, short_ref)


def convolve(part, gated, decay_ref, residue_ref, skip_ref, chunk_ref, local_ref, short_ref):
    modes = decay_ref.shape[0]
    seg_len = gated.shape[1]
    chunk_len = seg_len // SUBLANES
    index = lax.broadcasted_iota(jnp.int32, (SUBLANES, LANES), 0)
    lanes = lane_slice(part)
    factor, weight, start = [], [], []
    for n in range(modes):
        rate = row(decay_ref, n, part)
        prefix = chunk_ref[n, :, lanes]
        for shift in (1, 2, 4):
            moved = jnp.where(index >= shift, pltpu.roll(prefix, shift, 0), 0.0)
            prefix = prefix + jnp.exp(-rate * (shift * chunk_len)) * moved
        start.append(jnp.where(index >= 1, pltpu.roll(prefix, 1, 0), 0.0))
        factor.append(full(jnp.exp(-rate)))
        weight.append(full(row(residue_ref, n, part)))
    bypass = full(skip_ref[:, lanes])

    def step(t, state):
        rows = pl.ds(t, SUBLANES, stride=chunk_len)
        x = gated[part, rows, :]
        state = tuple(f * h + x for f, h in zip(factor, state))
        local_ref[rows, :] = tree_sum([w * h for w, h in zip(weight, state)] + [bypass * x])
        return state

    lax.fori_loop(0, chunk_len, step, tuple(start), unroll=4)
    short_ref[:seg_len, :] = local_ref[...].astype(short_ref.dtype)
    left = decay_ref[:, lanes]
    for first in range(seg_len, short_ref.shape[0], modes):
        piece = left.astype(short_ref.dtype)
        short_ref[first : first + modes, :] = piece
        left = left - piece.astype(jnp.float32)


def fold(rates, inner, total, received, stride, seg_len):
    place = lax.div(lax.axis_index("seq"), 2)
    radix = len(received) + 1
    spot = lax.rem(lax.div(place, stride), radix)
    offset = lax.rem(place, stride)

    def decayed(segments):
        return jnp.exp(-rates * (segments * 2 * seg_len).astype(jnp.float32))

    before = jnp.zeros_like(rates)
    whole = decayed((radix - 1 - spot) * stride) * total
    for i, block in enumerate(received):
        source = spot ^ (radix - 1 - i)
        past = source < spot
        gap = jnp.where(past, spot - 1 - source, 0) * stride
        before += jnp.where(past, decayed(gap) * block, 0.0)
        whole += decayed((radix - 1 - source) * stride) * block
    return inner + decayed(offset) * before, whole


def fold_kernel(stride, seg_len, rates_ref, total_ref, *rest):
    inner, rest = (rest[0][...], rest[1:]) if stride > 1 else (0.0, rest)
    received, (inner_out, total_out) = [ref[...] for ref in rest[:-2]], rest[-2:]
    inner_out[...], total_out[...] = fold(
        rates_ref[...], inner, total_ref[...], received, stride, seg_len
    )


def share_kernel(stride, seg_len, rates_ref, residue_ref, own_ref, total_ref, *rest):
    inner, rest = (rest[0][...], rest[1:]) if stride > 1 else (0.0, rest)
    received, (base_ref, extra_ref) = [ref[...] for ref in rest[:-2]], rest[-2:]
    rates = rates_ref[...]
    before, _ = fold(rates, inner, total_ref[...], received, stride, seg_len)
    before *= residue_ref[...]
    step = jnp.exp(-rates * float(seg_len))
    even = lax.rem(lax.axis_index("seq"), 2) == 0
    base_ref[...] = step * before
    extra_ref[...] = jnp.where(even, residue_ref[...] * own_ref[...] + step * step * before, before)


def carry(q_ref, local_ref, rates, base_ref, extra_ref, out_ref, part, column):
    modes = rates.shape[0]
    seg_len = q_ref.shape[0]
    block = 2 * SUBLANES
    ahead = (lax.broadcasted_iota(jnp.int32, (SUBLANES, LANES), 0) + 1).astype(jnp.float32)
    lanes = lane_slice(part)
    factor, start = [], []
    for n in range(modes):
        rate = rates[n : n + 1, :]
        weight = row(base_ref, n, part) + row(extra_ref, n, part)
        start.append(weight * jnp.exp(-rate * ahead))
        factor.append(full(jnp.exp(-rate * SUBLANES)))

    def step(j, state):
        rows = pl.ds(pl.multiple_of(j * block, block), block)
        halves = []
        for _ in range(2):
            halves.append(tree_sum(list(state)))
            state = tuple(f * h for f, h in zip(factor, state))
        total = local_ref[rows, :].astype(jnp.float32) + jnp.concatenate(halves, axis=0)
        gate_rows = q_ref[rows, lanes].astype(jnp.float32)
        out_ref[rows, lane_slice(column)] = (gate_rows * total).astype(out_ref.dtype)
        return state

    lax.fori_loop(0, seg_len // block, step, tuple(start), unroll=4)


def own_kernel(q_ref, rates_ref, base_ref, extra_ref, *rest):
    locals_in, out_ref = rest[:-1], rest[-1]
    for part, local_ref in enumerate(locals_in):
        carry(q_ref, local_ref, rates_ref[:, lane_slice(part)], base_ref, extra_ref, out_ref, part, part)


def across_kernel(part, extra_ref, base_ref, q_ref, local_ref, out_ref):
    modes = base_ref.shape[0]
    seg_len = q_ref.shape[0]
    pieces = [
        local_ref[first : first + modes, :].astype(jnp.float32)
        for first in range(seg_len, local_ref.shape[0], modes)
    ]
    rates = (pieces[2] + pieces[1]) + pieces[0]
    carry(q_ref, local_ref, rates, base_ref, extra_ref, out_ref, part, 0)


def project(blocks, weight_ref):
    total = None
    for rank, parts in blocks:
        depth = weight_ref.shape[0] // lax.axis_size("chan")
        offset = pl.multiple_of(rank * depth, depth)
        for block in parts:
            rows = pl.ds(offset, block.shape[1])
            term = jnp.dot(block[...], weight_ref[rows, :], preferred_element_type=jnp.float32)
            total = term if total is None else total + term
            offset = pl.multiple_of(offset + block.shape[1], block.shape[1])
    return total


def near_kernel(weight_ref, bias_ref, own_ref, pair_ref, *rest):
    across, out_ref = rest[:-1], rest[-1]
    rank = lax.axis_index("chan")
    blocks = [(rank, [own_ref]), (rank ^ 1, [pair_ref]), (rank ^ 2, across)]
    out_ref[...] = project(blocks, weight_ref) + bias_ref[...]


def last_kernel(near_ref, weight_ref, *rest):
    diagonal, (out_hbm, out_ref, sems) = rest[:-3], rest[-3:]
    rank = lax.axis_index("chan")
    pieces = sems.shape[0]
    size = out_ref.shape[0] // pieces
    copies = []
    for i in range(pieces):
        rows = pl.ds(i * size, size)
        total = near_ref[rows, :] + project([(rank ^ 3, [ref.at[rows, :] for ref in diagonal])], weight_ref)
        out_ref[rows, :] = total.astype(out_ref.dtype)
        copies.append(pltpu.make_async_copy(out_ref.at[rows], out_hbm.at[rows], sems.at[i]))
        copies[-1].start()
    for copy in copies:
        copy.wait()


def call(kernel, out, *args, cost=0, aliases=(), scratch=(), hbm=0, outs=pltpu.VMEM):
    spaces = [pltpu.HBM] * hbm + [pltpu.VMEM] * (len(args) - hbm)
    return pl.pallas_call(
        kernel,
        out_shape=out,
        in_specs=[pl.BlockSpec(memory_space=space) for space in spaces],
        out_specs=jax.tree.map(lambda _: pl.BlockSpec(memory_space=outs), out),
        scratch_shapes=list(scratch),
        input_output_aliases=dict(aliases),
        compiler_params=pltpu.CompilerParams(vmem_limit_bytes=VMEM_LIMIT),
        cost_estimate=pl.CostEstimate(flops=cost, bytes_accessed=0, transcendentals=0),
    )(*args)


def struct(shape, dtype=jnp.float32):
    return jax.ShapeDtypeStruct(shape, dtype)


def swapped(value, bit):
    count = lax.axis_size("chan")
    return lax.ppermute(value, "chan", [(r, r ^ bit) for r in range(count)])


def beside(value, step):
    count = lax.axis_size("seq")
    return lax.ppermute(value, "seq", [(r, r ^ step) for r in range(count)])


def corner(value, step, bit):
    count, width = lax.axis_size("seq"), lax.axis_size("chan")
    pairs = [(r * width + c, (r ^ step) * width + (c ^ bit)) for r in range(count) for c in range(width)]
    return lax.ppermute(value, ("seq", "chan"), pairs)


def carry_shares(total, own, decay, residue, seg_len, also):
    count = lax.axis_size("seq") // 2
    shape = struct(total.shape)
    inner, stride = (), 1
    while True:
        radix = min(4, count // stride)
        received = [beside(total, 2 * stride * step) for step in reversed(range(1, radix))]
        if stride * radix == count:
            break
        kernel = functools.partial(fold_kernel, stride, seg_len)
        *inner, total = call(kernel, [shape, shape], decay, total, *inner, *received)
        stride *= radix
    received, also = lax.optimization_barrier((received, also))
    kernel = functools.partial(share_kernel, stride, seg_len)
    base, extra = call(kernel, [shape, shape], decay, residue, own, total, *inner, *received, cost=FOLD_COST)
    return base, extra, also


def shards(q_gate, k_gate, value, decay, residue, skip, out_weight, out_bias):
    seg_len, channels = value.shape
    modes = decay.shape[0]
    cols = out_weight.shape[1]
    parts = channels // LANES
    tall = pltpu.VMEM((seg_len, channels), jnp.bfloat16)
    q_across = swapped(q_gate, 2)
    inputs = (k_gate, value, decay, residue, skip.reshape(1, -1), out_bias.reshape(1, -1))
    inputs = [pltpu.with_memory_space_constraint(x, pltpu.HBM) for x in inputs]
    tall = pltpu.VMEM((seg_len, channels), jnp.bfloat16)
    scratch = [tall, tall, pltpu.SemaphoreType.DMA((2 * parts + 4,))]
    few = struct((modes, channels))
    kept = [
        struct((modes, SUBLANES, channels)),
        struct((parts, seg_len, LANES)),
        few,
        few,
        struct((1, channels)),
        struct((1, cols)),
    ]
    thin = [struct((seg_len, LANES)), struct((seg_len + PIECES * modes, LANES), jnp.bfloat16)]
    total, *state = call(state_kernel, [few, *kept], *inputs, scratch=scratch, hbm=INPUTS)
    own_total, *state, first_local, first_short = call(
        local_kernel, [few, *kept, *thin], *inputs, total, *state,
        scratch=scratch, hbm=INPUTS, aliases=[(INPUTS + 1 + i, 1 + i) for i in range(KEPT)],
    )
    chunks, gated, decay, residue, skip, bias = state
    local, short = [first_local], [first_short]
    for part in range(1, parts):
        more = call(functools.partial(convolve, part), thin, gated, decay, residue, skip, chunks, cost=MORE_COST)
        local.append(more[0])
        short.append(more[1])
    local_across = [swapped(block, 2) for block in short]
    base, extra, q_across = carry_shares(total, own_total, decay, residue, seg_len, q_across)
    extra_beside, local_across[0] = lax.optimization_barrier((beside(extra, 1), local_across[0]))
    extra_corner = corner(extra, 1, 2)
    base_across = swapped(base, 2)
    whole = struct((seg_len, channels), jnp.bfloat16)
    own = call(own_kernel, whole, q_gate, decay, base, extra_beside, *local, cost=OWN_COST)
    pair = swapped(own, 1)
    half = struct((seg_len, LANES), jnp.bfloat16)
    across = [
        call(
            functools.partial(across_kernel, part), half, extra_corner, base_across, q_across, local_across[part],
            cost=PART_COST,
        )
        for part in range(parts)
    ]
    diagonal = [swapped(block, 1) for block in across]
    near = call(near_kernel, struct((seg_len, cols)), out_weight, bias, own, pair, *across)
    return call(
        last_kernel, struct((seg_len, cols), jnp.bfloat16), near, out_weight, *diagonal,
        scratch=[pltpu.VMEM((seg_len, cols), jnp.bfloat16), pltpu.SemaphoreType.DMA((STORES,))],
        outs=pltpu.HBM,
    )


def solution(mesh):
    return jax.shard_map(
        shards,
        mesh=mesh,
        in_specs=(
            P("seq", "chan"),
            P("seq", "chan"),
            P("seq", "chan"),
            P(None, "chan"),
            P(None, "chan"),
            P("chan"),
            P(None, "chan"),
            P("chan"),
        ),
        out_specs=P("seq", "chan"),
        check_vma=False,
    )
```

```python
import functools

import jax
import jax.numpy as jnp
from jax import lax
from jax.experimental import pallas as pl
from jax.experimental.pallas import tpu as pltpu
from jax.sharding import PartitionSpec as P

LANES = 128
SUBLANES = 8
STORES = 4
OWN_COST = 0
FOLD_COST = 3000000000
PIECES = 3
INPUTS = 6
KEPT = 6
PART_COST = 0
VMEM_LIMIT = 32 * 1024 * 1024


def row(ref, mode, part):
    return ref[mode : mode + 1, part * LANES : (part + 1) * LANES]


def full(value):
    return jnp.broadcast_to(value, (SUBLANES, LANES))


def tree_sum(terms):
    while len(terms) > 1:
        paired = [a + b for a, b in zip(terms[::2], terms[1::2])]
        terms = paired + ([terms[-1]] if len(terms) % 2 else [])
    return terms[0]


def lane_slice(part):
    return slice(part * LANES, (part + 1) * LANES)


def summarize(
    k_hbm, v_hbm, decay_hbm, residue_hbm, skip_hbm, bias_hbm,
    total_ref, chunk_ref, gated_ref, decay_ref, residue_ref, skip_ref, bias_ref,
    k_ref, v_ref, sems,
):
    modes = decay_hbm.shape[0]
    parts = gated_ref.shape[0]
    chunk_len = k_ref.shape[0] // SUBLANES
    pairs = [(decay_hbm, decay_ref)]
    for part in range(parts):
        lanes = pl.ds(part * LANES, LANES)
        pairs += [(k_hbm.at[:, lanes], k_ref.at[:, lanes]), (v_hbm.at[:, lanes], v_ref.at[:, lanes])]
    pairs += [(residue_hbm, residue_ref), (skip_hbm, skip_ref), (bias_hbm, bias_ref)]
    copies = [pltpu.make_async_copy(src, dst, sems.at[i]) for i, (src, dst) in enumerate(pairs)]
    for copy in copies:
        copy.start()
    copies[0].wait()
    later = (SUBLANES - 1 - lax.broadcasted_iota(jnp.int32, (SUBLANES, LANES), 0)) * chunk_len
    later = later.astype(jnp.float32)
    for part in range(parts):
        lanes = lane_slice(part)
        copies[1 + 2 * part].wait()
        copies[2 + 2 * part].wait()
        product = k_ref[:, lanes].astype(jnp.float32) * v_ref[:, lanes].astype(jnp.float32)
        gated_ref[part] = product.astype(jnp.bfloat16).astype(jnp.float32)
        factor = [full(jnp.exp(-row(decay_ref, n, part))) for n in range(modes)]

        def step(t, state):
            x = gated_ref[part, pl.ds(t, SUBLANES, stride=chunk_len), :]
            return tuple(f * h + x for f, h in zip(factor, state))

        zero = jnp.zeros((SUBLANES, LANES), jnp.float32)
        state = lax.fori_loop(0, chunk_len, step, (zero,) * modes, unroll=8)
        for n in range(modes):
            chunk_ref[n, :, lanes] = state[n]
            weight = jnp.exp(-row(decay_ref, n, part) * later)
            total_ref[n : n + 1, lanes] = jnp.sum(weight * state[n], axis=0, keepdims=True)
    for copy in copies[1 + 2 * parts :]:
        copy.wait()


def is_last():
    count = lax.axis_size("seq")
    return lax.axis_index("seq") >= count - 2


def state_kernel(*refs):
    total_ref = refs[INPUTS]

    @pl.when(jnp.logical_not(is_last()))
    def _():
        summarize(*refs)

    @pl.when(is_last())
    def _():
        total_ref[...] = jnp.zeros_like(total_ref)


def local_kernel(*refs):
    inputs, rest = refs[:INPUTS], refs[INPUTS:]
    total_in, rest = rest[0], rest[1 + KEPT :]
    total_ref, kept, (*locals_out, short_ref), scratch = rest[0], rest[1 : 1 + KEPT], rest[1 + KEPT : -3], rest[-3:]
    chunk_ref, gated_ref, decay_ref, residue_ref, skip_ref, _ = kept

    @pl.when(is_last())
    def _():
        summarize(*inputs, total_ref, *kept, *scratch)

    @pl.when(jnp.logical_not(is_last()))
    def _():
        total_ref[...] = total_in[...]

    for part, local_ref in enumerate(locals_out):
        convolve(part, gated_ref, decay_ref, residue_ref, skip_ref, chunk_ref, local_ref, short_ref)


def convolve(part, gated, decay_ref, residue_ref, skip_ref, chunk_ref, local_ref, short_ref):
    modes = decay_ref.shape[0]
    seg_len = gated.shape[1]
    chunk_len = seg_len // SUBLANES
    index = lax.broadcasted_iota(jnp.int32, (SUBLANES, LANES), 0)
    lanes = lane_slice(part)
    factor, weight, start = [], [], []
    for n in range(modes):
        rate = row(decay_ref, n, part)
        prefix = chunk_ref[n, :, lanes]
        for shift in (1, 2, 4):
            moved = jnp.where(index >= shift, pltpu.roll(prefix, shift, 0), 0.0)
            prefix = prefix + jnp.exp(-rate * (shift * chunk_len)) * moved
        start.append(jnp.where(index >= 1, pltpu.roll(prefix, 1, 0), 0.0))
        factor.append(full(jnp.exp(-rate)))
        weight.append(full(row(residue_ref, n, part)))
    bypass = full(skip_ref[:, lanes])

    def step(t, state):
        rows = pl.ds(t, SUBLANES, stride=chunk_len)
        x = gated[part, rows, :]
        state = tuple(f * h + x for f, h in zip(factor, state))
        local_ref[rows, :] = tree_sum([w * h for w, h in zip(weight, state)] + [bypass * x])
        return state

    lax.fori_loop(0, chunk_len, step, tuple(start), unroll=4)
    short_ref[:seg_len, lanes] = local_ref[...].astype(short_ref.dtype)
    left = decay_ref[:, lanes]
    for first in range(seg_len, short_ref.shape[0], modes):
        piece = left.astype(short_ref.dtype)
        short_ref[first : first + modes, lanes] = piece
        left = left - piece.astype(jnp.float32)


def fold(rates, inner, total, received, stride, seg_len):
    place = lax.div(lax.axis_index("seq"), 2)
    radix = len(received) + 1
    spot = lax.rem(lax.div(place, stride), radix)
    offset = lax.rem(place, stride)

    def decayed(segments):
        return jnp.exp(-rates * (segments * 2 * seg_len).astype(jnp.float32))

    before = jnp.zeros_like(rates)
    whole = decayed((radix - 1 - spot) * stride) * total
    for i, block in enumerate(received):
        source = spot ^ (radix - 1 - i)
        past = source < spot
        gap = jnp.where(past, spot - 1 - source, 0) * stride
        before += jnp.where(past, decayed(gap) * block, 0.0)
        whole += decayed((radix - 1 - source) * stride) * block
    return inner + decayed(offset) * before, whole


def fold_kernel(stride, seg_len, rates_ref, total_ref, *rest):
    inner, rest = (rest[0][...], rest[1:]) if stride > 1 else (0.0, rest)
    received, (inner_out, total_out) = [ref[...] for ref in rest[:-2]], rest[-2:]
    inner_out[...], total_out[...] = fold(
        rates_ref[...], inner, total_ref[...], received, stride, seg_len
    )


def share_kernel(stride, seg_len, rates_ref, residue_ref, own_ref, total_ref, *rest):
    inner, rest = (rest[0][...], rest[1:]) if stride > 1 else (0.0, rest)
    received, (base_ref, extra_ref) = [ref[...] for ref in rest[:-2]], rest[-2:]
    rates = rates_ref[...]
    before, _ = fold(rates, inner, total_ref[...], received, stride, seg_len)
    before *= residue_ref[...]
    step = jnp.exp(-rates * float(seg_len))
    even = lax.rem(lax.axis_index("seq"), 2) == 0
    base_ref[...] = step * before
    extra_ref[...] = jnp.where(even, residue_ref[...] * own_ref[...] + step * step * before, before)


def carry(q_ref, local_ref, rates, base_ref, extra_ref, out_ref, part, column):
    modes = rates.shape[0]
    seg_len = q_ref.shape[0]
    block = 2 * SUBLANES
    ahead = (lax.broadcasted_iota(jnp.int32, (SUBLANES, LANES), 0) + 1).astype(jnp.float32)
    lanes = lane_slice(part)
    factor, start = [], []
    for n in range(modes):
        rate = rates[n : n + 1, :]
        weight = row(base_ref, n, part) + row(extra_ref, n, part)
        start.append(weight * jnp.exp(-rate * ahead))
        factor.append(full(jnp.exp(-rate * SUBLANES)))

    def step(j, state):
        rows = pl.ds(pl.multiple_of(j * block, block), block)
        halves = []
        for _ in range(2):
            halves.append(tree_sum(list(state)))
            state = tuple(f * h for f, h in zip(factor, state))
        total = local_ref[rows, :].astype(jnp.float32) + jnp.concatenate(halves, axis=0)
        gate_rows = q_ref[rows, lanes].astype(jnp.float32)
        out_ref[rows, lane_slice(column)] = (gate_rows * total).astype(out_ref.dtype)
        return state

    lax.fori_loop(0, seg_len // block, step, tuple(start), unroll=4)


def own_kernel(q_ref, rates_ref, base_ref, extra_ref, *rest):
    locals_in, out_ref = rest[:-1], rest[-1]
    for part, local_ref in enumerate(locals_in):
        carry(q_ref, local_ref, rates_ref[:, lane_slice(part)], base_ref, extra_ref, out_ref, part, part)


def across_kernel(extra_ref, base_ref, q_ref, local_ref, out_ref):
    modes = base_ref.shape[0]
    seg_len = q_ref.shape[0]
    pieces = [
        local_ref[first : first + modes, :].astype(jnp.float32)
        for first in range(seg_len, local_ref.shape[0], modes)
    ]
    rates = (pieces[2] + pieces[1]) + pieces[0]
    for part in range(q_ref.shape[1] // LANES):
        lanes = lane_slice(part)
        carry(q_ref, local_ref.at[:, lanes], rates[:, lanes], base_ref, extra_ref, out_ref, part, part)


def project(blocks, weight_ref):
    total = None
    for rank, parts in blocks:
        depth = weight_ref.shape[0] // lax.axis_size("chan")
        offset = pl.multiple_of(rank * depth, depth)
        for block in parts:
            rows = pl.ds(offset, block.shape[1])
            term = jnp.dot(block[...], weight_ref[rows, :], preferred_element_type=jnp.float32)
            total = term if total is None else total + term
            offset = pl.multiple_of(offset + block.shape[1], block.shape[1])
    return total


def near_kernel(weight_ref, bias_ref, own_ref, pair_ref, *rest):
    across, out_ref = rest[:-1], rest[-1]
    rank = lax.axis_index("chan")
    blocks = [(rank, [own_ref]), (rank ^ 1, [pair_ref]), (rank ^ 2, across)]
    out_ref[...] = project(blocks, weight_ref) + bias_ref[...]


def last_kernel(near_ref, weight_ref, *rest):
    diagonal, (out_hbm, out_ref, sems) = rest[:-3], rest[-3:]
    rank = lax.axis_index("chan")
    pieces = sems.shape[0]
    size = out_ref.shape[0] // pieces
    copies = []
    for i in range(pieces):
        rows = pl.ds(i * size, size)
        total = near_ref[rows, :] + project([(rank ^ 3, [ref.at[rows, :] for ref in diagonal])], weight_ref)
        out_ref[rows, :] = total.astype(out_ref.dtype)
        copies.append(pltpu.make_async_copy(out_ref.at[rows], out_hbm.at[rows], sems.at[i]))
        copies[-1].start()
    for copy in copies:
        copy.wait()


def call(kernel, out, *args, cost=0, aliases=(), scratch=(), hbm=0, outs=pltpu.VMEM):
    spaces = [pltpu.HBM] * hbm + [pltpu.VMEM] * (len(args) - hbm)
    return pl.pallas_call(
        kernel,
        out_shape=out,
        in_specs=[pl.BlockSpec(memory_space=space) for space in spaces],
        out_specs=jax.tree.map(lambda _: pl.BlockSpec(memory_space=outs), out),
        scratch_shapes=list(scratch),
        input_output_aliases=dict(aliases),
        compiler_params=pltpu.CompilerParams(vmem_limit_bytes=VMEM_LIMIT),
        cost_estimate=pl.CostEstimate(flops=cost, bytes_accessed=0, transcendentals=0),
    )(*args)


def struct(shape, dtype=jnp.float32):
    return jax.ShapeDtypeStruct(shape, dtype)


def swapped(value, bit):
    count = lax.axis_size("chan")
    return lax.ppermute(value, "chan", [(r, r ^ bit) for r in range(count)])


def beside(value, step):
    count = lax.axis_size("seq")
    return lax.ppermute(value, "seq", [(r, r ^ step) for r in range(count)])


def corner(value, step, bit):
    count, width = lax.axis_size("seq"), lax.axis_size("chan")
    pairs = [(r * width + c, (r ^ step) * width + (c ^ bit)) for r in range(count) for c in range(width)]
    return lax.ppermute(value, ("seq", "chan"), pairs)


def carry_shares(total, own, decay, residue, seg_len, also):
    count = lax.axis_size("seq") // 2
    shape = struct(total.shape)
    inner, stride = (), 1
    while True:
        radix = min(4, count // stride)
        received = [beside(total, 2 * stride * step) for step in reversed(range(1, radix))]
        if stride * radix == count:
            break
        kernel = functools.partial(fold_kernel, stride, seg_len)
        *inner, total = call(kernel, [shape, shape], decay, total, *inner, *received)
        stride *= radix
    received, also = lax.optimization_barrier((received, also))
    kernel = functools.partial(share_kernel, stride, seg_len)
    base, extra = call(kernel, [shape, shape], decay, residue, own, total, *inner, *received, cost=FOLD_COST)
    return base, extra, also


def shards(q_gate, k_gate, value, decay, residue, skip, out_weight, out_bias):
    seg_len, channels = value.shape
    modes = decay.shape[0]
    cols = out_weight.shape[1]
    parts = channels // LANES
    tall = pltpu.VMEM((seg_len, channels), jnp.bfloat16)
    q_across = swapped(q_gate, 2)
    inputs = (k_gate, value, decay, residue, skip.reshape(1, -1), out_bias.reshape(1, -1))
    inputs = [pltpu.with_memory_space_constraint(x, pltpu.HBM) for x in inputs]
    tall = pltpu.VMEM((seg_len, channels), jnp.bfloat16)
    scratch = [tall, tall, pltpu.SemaphoreType.DMA((2 * parts + 4,))]
    few = struct((modes, channels))
    kept = [
        struct((modes, SUBLANES, channels)),
        struct((parts, seg_len, LANES)),
        few,
        few,
        struct((1, channels)),
        struct((1, cols)),
    ]
    thin = struct((seg_len, LANES))
    short = struct((seg_len + PIECES * modes, channels), jnp.bfloat16)
    total, *state = call(state_kernel, [few, *kept], *inputs, scratch=scratch, hbm=INPUTS)
    own_total, *state = call(
        local_kernel, [few, *kept, *[thin] * parts, short], *inputs, total, *state,
        scratch=scratch, hbm=INPUTS, aliases=[(INPUTS + 1 + i, 1 + i) for i in range(KEPT)],
    )
    _, _, decay, residue, _, bias, *local, local_short = state
    local_across = swapped(local_short, 2)
    base, extra, q_across = carry_shares(total, own_total, decay, residue, seg_len, q_across)
    extra_beside = beside(extra, 1)
    extra_corner = corner(extra, 1, 2)
    base_across = swapped(base, 2)
    whole = struct((seg_len, channels), jnp.bfloat16)
    own = call(own_kernel, whole, q_gate, decay, base, extra_beside, *local, cost=OWN_COST)
    pair = swapped(own, 1)
    across = call(
        across_kernel, whole, extra_corner, base_across, q_across, local_across, cost=PART_COST
    )
    diagonal = swapped(across, 1)
    near = call(near_kernel, struct((seg_len, cols)), out_weight, bias, own, pair, across)
    return call(
        last_kernel, struct((seg_len, cols), jnp.bfloat16), near, out_weight, diagonal,
        scratch=[pltpu.VMEM((seg_len, cols), jnp.bfloat16), pltpu.SemaphoreType.DMA((STORES,))],
        outs=pltpu.HBM,
    )


def solution(mesh):
    return jax.shard_map(
        shards,
        mesh=mesh,
        in_specs=(
            P("seq", "chan"),
            P("seq", "chan"),
            P("seq", "chan"),
            P(None, "chan"),
            P(None, "chan"),
            P("chan"),
            P(None, "chan"),
            P("chan"),
        ),
        out_specs=P("seq", "chan"),
        check_vma=False,
    )
```

```python
import functools

import jax
import jax.numpy as jnp
from jax import lax
from jax.experimental import pallas as pl
from jax.experimental.pallas import tpu as pltpu
from jax.sharding import PartitionSpec as P

LANES = 128
SUBLANES = 8
STORES = 4
OWN_COST = 0
FOLD_COST = 3000000000
PIECES = 3
ROUTES = {2: [(1, 0)], 4: [(3, 2, 1, 0), (2, 0, 3, 1), (1, 3, 0, 2)]}
INPUTS = 6
KEPT = 6
PART_COST = 0
VMEM_LIMIT = 32 * 1024 * 1024


def row(ref, mode, part):
    return ref[mode : mode + 1, part * LANES : (part + 1) * LANES]


def full(value):
    return jnp.broadcast_to(value, (SUBLANES, LANES))


def tree_sum(terms):
    while len(terms) > 1:
        paired = [a + b for a, b in zip(terms[::2], terms[1::2])]
        terms = paired + ([terms[-1]] if len(terms) % 2 else [])
    return terms[0]


def lane_slice(part):
    return slice(part * LANES, (part + 1) * LANES)


def summarize(
    k_hbm, v_hbm, decay_hbm, residue_hbm, skip_hbm, bias_hbm,
    total_ref, chunk_ref, gated_ref, decay_ref, residue_ref, skip_ref, bias_ref,
    k_ref, v_ref, sems,
):
    modes = decay_hbm.shape[0]
    parts = gated_ref.shape[0]
    chunk_len = k_ref.shape[0] // SUBLANES
    pairs = [(decay_hbm, decay_ref)]
    for part in range(parts):
        lanes = pl.ds(part * LANES, LANES)
        pairs += [(k_hbm.at[:, lanes], k_ref.at[:, lanes]), (v_hbm.at[:, lanes], v_ref.at[:, lanes])]
    pairs += [(residue_hbm, residue_ref), (skip_hbm, skip_ref), (bias_hbm, bias_ref)]
    copies = [pltpu.make_async_copy(src, dst, sems.at[i]) for i, (src, dst) in enumerate(pairs)]
    for copy in copies:
        copy.start()
    copies[0].wait()
    later = (SUBLANES - 1 - lax.broadcasted_iota(jnp.int32, (SUBLANES, LANES), 0)) * chunk_len
    later = later.astype(jnp.float32)
    for part in range(parts):
        lanes = lane_slice(part)
        copies[1 + 2 * part].wait()
        copies[2 + 2 * part].wait()
        product = k_ref[:, lanes].astype(jnp.float32) * v_ref[:, lanes].astype(jnp.float32)
        gated_ref[part] = product.astype(jnp.bfloat16).astype(jnp.float32)
        factor = [full(jnp.exp(-row(decay_ref, n, part))) for n in range(modes)]

        def step(t, state):
            x = gated_ref[part, pl.ds(t, SUBLANES, stride=chunk_len), :]
            return tuple(f * h + x for f, h in zip(factor, state))

        zero = jnp.zeros((SUBLANES, LANES), jnp.float32)
        state = lax.fori_loop(0, chunk_len, step, (zero,) * modes, unroll=8)
        for n in range(modes):
            chunk_ref[n, :, lanes] = state[n]
            weight = jnp.exp(-row(decay_ref, n, part) * later)
            total_ref[n : n + 1, lanes] = jnp.sum(weight * state[n], axis=0, keepdims=True)
    for copy in copies[1 + 2 * parts :]:
        copy.wait()


def is_last():
    count = lax.axis_size("seq")
    return lax.axis_index("seq") >= count - 2


def state_kernel(*refs):
    total_ref = refs[INPUTS]

    @pl.when(jnp.logical_not(is_last()))
    def _():
        summarize(*refs)

    @pl.when(is_last())
    def _():
        total_ref[...] = jnp.zeros_like(total_ref)


def local_kernel(*refs):
    inputs, rest = refs[:INPUTS], refs[INPUTS:]
    total_in, rest = rest[0], rest[1 + KEPT :]
    total_ref, kept, (*locals_out, short_ref), scratch = rest[0], rest[1 : 1 + KEPT], rest[1 + KEPT : -3], rest[-3:]
    chunk_ref, gated_ref, decay_ref, residue_ref, skip_ref, _ = kept

    @pl.when(is_last())
    def _():
        summarize(*inputs, total_ref, *kept, *scratch)

    @pl.when(jnp.logical_not(is_last()))
    def _():
        total_ref[...] = total_in[...]

    for part, local_ref in enumerate(locals_out):
        convolve(part, gated_ref, decay_ref, residue_ref, skip_ref, chunk_ref, local_ref, short_ref)


def convolve(part, gated, decay_ref, residue_ref, skip_ref, chunk_ref, local_ref, short_ref):
    modes = decay_ref.shape[0]
    seg_len = gated.shape[1]
    chunk_len = seg_len // SUBLANES
    index = lax.broadcasted_iota(jnp.int32, (SUBLANES, LANES), 0)
    lanes = lane_slice(part)
    factor, weight, start = [], [], []
    for n in range(modes):
        rate = row(decay_ref, n, part)
        prefix = chunk_ref[n, :, lanes]
        for shift in (1, 2, 4):
            moved = jnp.where(index >= shift, pltpu.roll(prefix, shift, 0), 0.0)
            prefix = prefix + jnp.exp(-rate * (shift * chunk_len)) * moved
        start.append(jnp.where(index >= 1, pltpu.roll(prefix, 1, 0), 0.0))
        factor.append(full(jnp.exp(-rate)))
        weight.append(full(row(residue_ref, n, part)))
    bypass = full(skip_ref[:, lanes])

    def step(t, state):
        rows = pl.ds(t, SUBLANES, stride=chunk_len)
        x = gated[part, rows, :]
        state = tuple(f * h + x for f, h in zip(factor, state))
        local_ref[rows, :] = tree_sum([w * h for w, h in zip(weight, state)] + [bypass * x])
        return state

    lax.fori_loop(0, chunk_len, step, tuple(start), unroll=4)
    short_ref[:seg_len, lanes] = local_ref[...].astype(short_ref.dtype)
    left = decay_ref[:, lanes]
    for first in range(seg_len, short_ref.shape[0], modes):
        piece = left.astype(short_ref.dtype)
        short_ref[first : first + modes, lanes] = piece
        left = left - piece.astype(jnp.float32)


def lookup(spot, table):
    found = table[0]
    for i, entry in enumerate(table[1:]):
        found = jnp.where(spot == i + 1, entry, found)
    return found


def fold(rates, inner, total, received, stride, seg_len):
    place = lax.div(lax.axis_index("seq"), 2)
    radix = len(received) + 1
    spot = lax.rem(lax.div(place, stride), radix)
    offset = lax.rem(place, stride)

    def decayed(segments):
        return jnp.exp(-rates * (segments * 2 * seg_len).astype(jnp.float32))

    before = jnp.zeros_like(rates)
    whole = decayed((radix - 1 - spot) * stride) * total
    for route, block in zip(ROUTES[radix], received):
        source = lookup(spot, [route.index(i) for i in range(radix)])
        past = source < spot
        gap = jnp.where(past, spot - 1 - source, 0) * stride
        before += jnp.where(past, decayed(gap) * block, 0.0)
        whole += decayed((radix - 1 - source) * stride) * block
    return inner + decayed(offset) * before, whole


def fold_kernel(stride, seg_len, rates_ref, total_ref, *rest):
    inner, rest = (rest[0][...], rest[1:]) if stride > 1 else (0.0, rest)
    received, (inner_out, total_out) = [ref[...] for ref in rest[:-2]], rest[-2:]
    inner_out[...], total_out[...] = fold(
        rates_ref[...], inner, total_ref[...], received, stride, seg_len
    )


def share_kernel(stride, seg_len, rates_ref, residue_ref, own_ref, total_ref, *rest):
    inner, rest = (rest[0][...], rest[1:]) if stride > 1 else (0.0, rest)
    received, (base_ref, extra_ref) = [ref[...] for ref in rest[:-2]], rest[-2:]
    rates = rates_ref[...]
    before, _ = fold(rates, inner, total_ref[...], received, stride, seg_len)
    before *= residue_ref[...]
    step = jnp.exp(-rates * float(seg_len))
    even = lax.rem(lax.axis_index("seq"), 2) == 0
    base_ref[...] = step * before
    extra_ref[...] = jnp.where(even, residue_ref[...] * own_ref[...] + step * step * before, before)


def carry(q_ref, local_ref, rates, base_ref, extra_ref, out_ref, part, column):
    modes = rates.shape[0]
    seg_len = q_ref.shape[0]
    block = 2 * SUBLANES
    ahead = (lax.broadcasted_iota(jnp.int32, (SUBLANES, LANES), 0) + 1).astype(jnp.float32)
    lanes = lane_slice(part)
    factor, start = [], []
    for n in range(modes):
        rate = rates[n : n + 1, :]
        weight = row(base_ref, n, part) + row(extra_ref, n, part)
        start.append(weight * jnp.exp(-rate * ahead))
        factor.append(full(jnp.exp(-rate * SUBLANES)))

    def step(j, state):
        rows = pl.ds(pl.multiple_of(j * block, block), block)
        halves = []
        for _ in range(2):
            halves.append(tree_sum(list(state)))
            state = tuple(f * h for f, h in zip(factor, state))
        total = local_ref[rows, :].astype(jnp.float32) + jnp.concatenate(halves, axis=0)
        gate_rows = q_ref[rows, lanes].astype(jnp.float32)
        out_ref[rows, lane_slice(column)] = (gate_rows * total).astype(out_ref.dtype)
        return state

    lax.fori_loop(0, seg_len // block, step, tuple(start), unroll=4)


def own_kernel(q_ref, rates_ref, base_ref, extra_ref, *rest):
    locals_in, out_ref = rest[:-1], rest[-1]
    for part, local_ref in enumerate(locals_in):
        carry(q_ref, local_ref, rates_ref[:, lane_slice(part)], base_ref, extra_ref, out_ref, part, part)


def across_kernel(extra_ref, base_ref, q_ref, local_ref, out_ref):
    modes = base_ref.shape[0]
    seg_len = q_ref.shape[0]
    pieces = [
        local_ref[first : first + modes, :].astype(jnp.float32)
        for first in range(seg_len, local_ref.shape[0], modes)
    ]
    rates = (pieces[2] + pieces[1]) + pieces[0]
    for part in range(q_ref.shape[1] // LANES):
        lanes = lane_slice(part)
        carry(q_ref, local_ref.at[:, lanes], rates[:, lanes], base_ref, extra_ref, out_ref, part, part)


def project(blocks, weight_ref):
    total = None
    for rank, parts in blocks:
        depth = weight_ref.shape[0] // lax.axis_size("chan")
        offset = pl.multiple_of(rank * depth, depth)
        for block in parts:
            rows = pl.ds(offset, block.shape[1])
            term = jnp.dot(block[...], weight_ref[rows, :], preferred_element_type=jnp.float32)
            total = term if total is None else total + term
            offset = pl.multiple_of(offset + block.shape[1], block.shape[1])
    return total


def near_kernel(weight_ref, bias_ref, own_ref, pair_ref, *rest):
    across, out_ref = rest[:-1], rest[-1]
    rank = lax.axis_index("chan")
    blocks = [(rank, [own_ref]), (rank ^ 1, [pair_ref]), (rank ^ 2, across)]
    out_ref[...] = project(blocks, weight_ref) + bias_ref[...]


def last_kernel(near_ref, weight_ref, *rest):
    diagonal, (out_hbm, out_ref, sems) = rest[:-3], rest[-3:]
    rank = lax.axis_index("chan")
    pieces = sems.shape[0]
    size = out_ref.shape[0] // pieces
    copies = []
    for i in range(pieces):
        rows = pl.ds(i * size, size)
        total = near_ref[rows, :] + project([(rank ^ 3, [ref.at[rows, :] for ref in diagonal])], weight_ref)
        out_ref[rows, :] = total.astype(out_ref.dtype)
        copies.append(pltpu.make_async_copy(out_ref.at[rows], out_hbm.at[rows], sems.at[i]))
        copies[-1].start()
    for copy in copies:
        copy.wait()


def call(kernel, out, *args, cost=0, aliases=(), scratch=(), hbm=0, outs=pltpu.VMEM):
    spaces = [pltpu.HBM] * hbm + [pltpu.VMEM] * (len(args) - hbm)
    return pl.pallas_call(
        kernel,
        out_shape=out,
        in_specs=[pl.BlockSpec(memory_space=space) for space in spaces],
        out_specs=jax.tree.map(lambda _: pl.BlockSpec(memory_space=outs), out),
        scratch_shapes=list(scratch),
        input_output_aliases=dict(aliases),
        compiler_params=pltpu.CompilerParams(vmem_limit_bytes=VMEM_LIMIT),
        cost_estimate=pl.CostEstimate(flops=cost, bytes_accessed=0, transcendentals=0),
    )(*args)


def struct(shape, dtype=jnp.float32):
    return jax.ShapeDtypeStruct(shape, dtype)


def swapped(value, bit):
    count = lax.axis_size("chan")
    return lax.ppermute(value, "chan", [(r, r ^ bit) for r in range(count)])


def beside(value):
    count = lax.axis_size("seq")
    return lax.ppermute(value, "seq", [(r, r ^ 1) for r in range(count)])


def along(value, stride, route):
    count, radix = lax.axis_size("seq"), len(route)

    def target(r):
        spot = r // stride % radix
        return r + (route[spot] - spot) * stride

    return lax.ppermute(value, "seq", [(r, target(r)) for r in range(count)])


def corner(value, step, bit):
    count, width = lax.axis_size("seq"), lax.axis_size("chan")
    pairs = [(r * width + c, (r ^ step) * width + (c ^ bit)) for r in range(count) for c in range(width)]
    return lax.ppermute(value, ("seq", "chan"), pairs)


def carry_shares(total, own, decay, residue, seg_len, also):
    count = lax.axis_size("seq") // 2
    shape = struct(total.shape)
    inner, stride = (), 1
    while True:
        radix = min(4, count // stride)
        received = [along(total, 2 * stride, route) for route in ROUTES[radix]]
        if stride * radix == count:
            break
        kernel = functools.partial(fold_kernel, stride, seg_len)
        *inner, total = call(kernel, [shape, shape], decay, total, *inner, *received)
        stride *= radix
    received, also = lax.optimization_barrier((received, also))
    kernel = functools.partial(share_kernel, stride, seg_len)
    base, extra = call(kernel, [shape, shape], decay, residue, own, total, *inner, *received, cost=FOLD_COST)
    return base, extra, also


def shards(q_gate, k_gate, value, decay, residue, skip, out_weight, out_bias):
    seg_len, channels = value.shape
    modes = decay.shape[0]
    cols = out_weight.shape[1]
    parts = channels // LANES
    tall = pltpu.VMEM((seg_len, channels), jnp.bfloat16)
    q_across = swapped(q_gate, 2)
    inputs = (k_gate, value, decay, residue, skip.reshape(1, -1), out_bias.reshape(1, -1))
    inputs = [pltpu.with_memory_space_constraint(x, pltpu.HBM) for x in inputs]
    tall = pltpu.VMEM((seg_len, channels), jnp.bfloat16)
    scratch = [tall, tall, pltpu.SemaphoreType.DMA((2 * parts + 4,))]
    few = struct((modes, channels))
    kept = [
        struct((modes, SUBLANES, channels)),
        struct((parts, seg_len, LANES)),
        few,
        few,
        struct((1, channels)),
        struct((1, cols)),
    ]
    thin = struct((seg_len, LANES))
    short = struct((seg_len + PIECES * modes, channels), jnp.bfloat16)
    total, *state = call(state_kernel, [few, *kept], *inputs, scratch=scratch, hbm=INPUTS)
    own_total, *state = call(
        local_kernel, [few, *kept, *[thin] * parts, short], *inputs, total, *state,
        scratch=scratch, hbm=INPUTS, aliases=[(INPUTS + 1 + i, 1 + i) for i in range(KEPT)],
    )
    _, _, decay, residue, _, bias, *local, local_short = state
    local_across = swapped(local_short, 2)
    base, extra, q_across = carry_shares(total, own_total, decay, residue, seg_len, q_across)
    extra_beside = beside(extra)
    extra_corner = corner(extra, 1, 2)
    base_across = swapped(base, 2)
    whole = struct((seg_len, channels), jnp.bfloat16)
    own = call(own_kernel, whole, q_gate, decay, base, extra_beside, *local, cost=OWN_COST)
    pair = swapped(own, 1)
    across = call(
        across_kernel, whole, extra_corner, base_across, q_across, local_across, cost=PART_COST
    )
    diagonal = swapped(across, 1)
    near = call(near_kernel, struct((seg_len, cols)), out_weight, bias, own, pair, across)
    return call(
        last_kernel, struct((seg_len, cols), jnp.bfloat16), near, out_weight, diagonal,
        scratch=[pltpu.VMEM((seg_len, cols), jnp.bfloat16), pltpu.SemaphoreType.DMA((STORES,))],
        outs=pltpu.HBM,
    )


def solution(mesh):
    return jax.shard_map(
        shards,
        mesh=mesh,
        in_specs=(
            P("seq", "chan"),
            P("seq", "chan"),
            P("seq", "chan"),
            P(None, "chan"),
            P(None, "chan"),
            P("chan"),
            P(None, "chan"),
            P("chan"),
        ),
        out_specs=P("seq", "chan"),
        check_vma=False,
    )
```

```python
import functools

import jax
import jax.numpy as jnp
from jax import lax
from jax.experimental import pallas as pl
from jax.experimental.pallas import tpu as pltpu
from jax.sharding import PartitionSpec as P

LANES = 128
SUBLANES = 8
STORES = 4
OWN_COST = 0
FOLD_COST = 3000000000
PIECES = 3
ROUTES = {2: [(1, 0)], 4: [(3, 2, 0, 1), (2, 3, 0, 1), (1, 0, 3, 2)]}
INPUTS = 6
KEPT = 8
PART_COST = 0
VMEM_LIMIT = 32 * 1024 * 1024


def row(ref, mode, part):
    return ref[mode : mode + 1, part * LANES : (part + 1) * LANES]


def full(value):
    return jnp.broadcast_to(value, (SUBLANES, LANES))


def lane_slice(part):
    return slice(part * LANES, (part + 1) * LANES)


def summarize(
    k_hbm, v_hbm, decay_hbm, residue_hbm, skip_hbm, bias_hbm,
    total_ref, chunk_ref, gated_ref, decay_ref, residue_ref, skip_ref, bias_ref,
    k_ref, v_ref, sems,
):
    modes = decay_hbm.shape[0]
    parts = gated_ref.shape[0]
    chunk_len = k_ref.shape[0] // SUBLANES
    pairs = [(decay_hbm, decay_ref)]
    for part in range(parts):
        lanes = pl.ds(part * LANES, LANES)
        pairs += [(k_hbm.at[:, lanes], k_ref.at[:, lanes]), (v_hbm.at[:, lanes], v_ref.at[:, lanes])]
    pairs += [(residue_hbm, residue_ref), (skip_hbm, skip_ref), (bias_hbm, bias_ref)]
    copies = [pltpu.make_async_copy(src, dst, sems.at[i]) for i, (src, dst) in enumerate(pairs)]
    for copy in copies:
        copy.start()
    copies[0].wait()
    later = (SUBLANES - 1 - lax.broadcasted_iota(jnp.int32, (SUBLANES, LANES), 0)) * chunk_len
    later = later.astype(jnp.float32)
    for part in range(parts):
        lanes = lane_slice(part)
        copies[1 + 2 * part].wait()
        copies[2 + 2 * part].wait()
        product = k_ref[:, lanes].astype(jnp.float32) * v_ref[:, lanes].astype(jnp.float32)
        gated_ref[part] = product.astype(jnp.bfloat16).astype(jnp.float32)
        factor = [full(jnp.exp(-row(decay_ref, n, part))) for n in range(modes)]
        square = [f * f for f in factor]

        def step(t, state):
            x = gated_ref[part, pl.ds(2 * t, SUBLANES, stride=chunk_len), :]
            y = gated_ref[part, pl.ds(2 * t + 1, SUBLANES, stride=chunk_len), :]
            return tuple(g * h + (f * x + y) for f, g, h in zip(factor, square, state))

        zero = jnp.zeros((SUBLANES, LANES), jnp.float32)
        state = lax.fori_loop(0, chunk_len // 2, step, (zero,) * modes, unroll=4)
        for n in range(modes):
            chunk_ref[n, :, lanes] = state[n]
            weight = jnp.exp(-row(decay_ref, n, part) * later)
            total_ref[n : n + 1, lanes] = jnp.sum(weight * state[n], axis=0, keepdims=True)
    for copy in copies[1 + 2 * parts :]:
        copy.wait()


def is_last():
    count = lax.axis_size("seq")
    return lax.axis_index("seq") >= count - 2


def is_first():
    return lax.axis_index("seq") < 2


def state_kernel(*refs):
    inputs, total_ref, kept = refs[:INPUTS], refs[INPUTS], refs[INPUTS + 1 : INPUTS + 1 + KEPT]
    scratch, weights = refs[-4:-1], refs[-1]
    state, (local_ref, short_ref) = kept[:-2], kept[-2:]
    chunk_ref, gated_ref, decay_ref, residue_ref, skip_ref, _ = state

    @pl.when(jnp.logical_not(is_last()))
    def _():
        summarize(*inputs, total_ref, *state, *scratch)

    @pl.when(is_last())
    def _():
        total_ref[...] = jnp.zeros_like(total_ref)

    @pl.when(is_first())
    def _():
        convolve(0, gated_ref, decay_ref, residue_ref, skip_ref, chunk_ref, local_ref, short_ref, weights)


def local_kernel(*refs):
    inputs, total_in, rest = refs[:INPUTS], refs[INPUTS], refs[INPUTS + 1 + KEPT :]
    total_ref, kept, more, scratch, weights = rest[0], rest[1 : 1 + KEPT], rest[1 + KEPT : -4], rest[-4:-1], rest[-1]
    state, (local_ref, short_ref) = kept[:-2], kept[-2:]
    chunk_ref, gated_ref, decay_ref, residue_ref, skip_ref, _ = state

    @pl.when(is_last())
    def _():
        summarize(*inputs, total_ref, *state, *scratch)

    @pl.when(jnp.logical_not(is_last()))
    def _():
        total_ref[...] = total_in[...]

    @pl.when(jnp.logical_not(is_first()))
    def _():
        convolve(0, gated_ref, decay_ref, residue_ref, skip_ref, chunk_ref, local_ref, short_ref, weights)

    for i, more_ref in enumerate(more):
        convolve(i + 1, gated_ref, decay_ref, residue_ref, skip_ref, chunk_ref, more_ref, short_ref, weights)


def convolve(part, gated, decay_ref, residue_ref, skip_ref, chunk_ref, local_ref, short_ref, weights):
    modes = decay_ref.shape[0]
    seg_len = gated.shape[1]
    chunk_len = seg_len // SUBLANES
    index = lax.broadcasted_iota(jnp.int32, (SUBLANES, LANES), 0)
    lanes = lane_slice(part)
    factor, start = [], []
    for n in range(modes):
        rate = row(decay_ref, n, part)
        prefix = chunk_ref[n, :, lanes]
        for shift in (1, 2, 4):
            moved = jnp.where(index >= shift, pltpu.roll(prefix, shift, 0), 0.0)
            prefix = prefix + jnp.exp(-rate * (shift * chunk_len)) * moved
        start.append(jnp.where(index >= 1, pltpu.roll(prefix, 1, 0), 0.0))
        factor.append(full(jnp.exp(-rate)))
        weights[n] = full(row(residue_ref, n, part))
    bypass = full(skip_ref[:, lanes])

    def step(t, state):
        rows = pl.ds(t, SUBLANES, stride=chunk_len)
        x = gated[part, rows, :]
        state = tuple(f * h + x for f, h in zip(factor, state))
        sums = [bypass * x] + [None] * 3
        for n, h in enumerate(state):
            term = weights[n] * h
            sums[n % 4] = term if sums[n % 4] is None else sums[n % 4] + term
        local_ref[rows, :] = (sums[0] + sums[1]) + (sums[2] + sums[3])
        return state

    lax.fori_loop(0, chunk_len, step, tuple(start), unroll=4)
    short_ref[:seg_len, lanes] = local_ref[...].astype(short_ref.dtype)
    left = decay_ref[:, lanes]
    for first in range(seg_len, short_ref.shape[0], modes):
        piece = left.astype(short_ref.dtype)
        short_ref[first : first + modes, lanes] = piece
        left = left - piece.astype(jnp.float32)


def lookup(spot, table):
    found = table[0]
    for i, entry in enumerate(table[1:]):
        found = jnp.where(spot == i + 1, entry, found)
    return found


def fold(rates, inner, total, received, stride, seg_len):
    place = lax.div(lax.axis_index("seq"), 2)
    radix = len(received) + 1
    spot = lax.rem(lax.div(place, stride), radix)
    offset = lax.rem(place, stride)

    def decayed(segments):
        return jnp.exp(-rates * (segments * 2 * seg_len).astype(jnp.float32))

    before = jnp.zeros_like(rates)
    whole = decayed((radix - 1 - spot) * stride) * total
    for route, block in zip(ROUTES[radix], received):
        source = lookup(spot, [route.index(i) for i in range(radix)])
        past = source < spot
        gap = jnp.where(past, spot - 1 - source, 0) * stride
        before += jnp.where(past, decayed(gap) * block, 0.0)
        whole += decayed((radix - 1 - source) * stride) * block
    return inner + decayed(offset) * before, whole


def fold_kernel(stride, seg_len, rates_ref, total_ref, *rest):
    inner, rest = (rest[0][...], rest[1:]) if stride > 1 else (0.0, rest)
    received, (inner_out, total_out) = [ref[...] for ref in rest[:-2]], rest[-2:]
    inner_out[...], total_out[...] = fold(
        rates_ref[...], inner, total_ref[...], received, stride, seg_len
    )


def share_kernel(stride, seg_len, rates_ref, residue_ref, own_ref, total_ref, *rest):
    inner, rest = (rest[0][...], rest[1:]) if stride > 1 else (0.0, rest)
    received, (base_ref, extra_ref) = [ref[...] for ref in rest[:-2]], rest[-2:]
    rates = rates_ref[...]
    before, _ = fold(rates, inner, total_ref[...], received, stride, seg_len)
    before *= residue_ref[...]
    step = jnp.exp(-rates * float(seg_len))
    even = lax.rem(lax.axis_index("seq"), 2) == 0
    base_ref[...] = step * before
    extra_ref[...] = jnp.where(even, residue_ref[...] * own_ref[...] + step * step * before, before)


def carry(q_ref, local_ref, rates, base_ref, extra_ref, out_ref, part, column):
    modes = rates.shape[0]
    seg_len = q_ref.shape[0]
    block = 2 * SUBLANES
    ahead = (lax.broadcasted_iota(jnp.int32, (SUBLANES, LANES), 0) + 1).astype(jnp.float32)
    lanes = lane_slice(part)
    factor, start = [], []
    for n in range(modes):
        rate = rates[n : n + 1, :]
        weight = row(base_ref, n, part) + row(extra_ref, n, part)
        start.append(weight * jnp.exp(-rate * ahead))
        factor.append(full(jnp.exp(-rate * SUBLANES)))

    def step(j, state):
        rows = pl.ds(pl.multiple_of(j * block, block), block)
        halves = []
        for _ in range(2):
            sums = list(state[:4])
            for n, h in enumerate(state[4:]):
                sums[n % 4] = sums[n % 4] + h
            halves.append((sums[0] + sums[1]) + (sums[2] + sums[3]))
            state = tuple(f * h for f, h in zip(factor, state))
        total = local_ref[rows, :].astype(jnp.float32) + jnp.concatenate(halves, axis=0)
        gate_rows = q_ref[rows, lanes].astype(jnp.float32)
        out_ref[rows, lane_slice(column)] = (gate_rows * total).astype(out_ref.dtype)
        return state

    lax.fori_loop(0, seg_len // block, step, tuple(start), unroll=4)


def own_kernel(q_ref, rates_ref, base_ref, extra_ref, *rest):
    locals_in, out_ref = rest[:-1], rest[-1]
    for part, local_ref in enumerate(locals_in):
        carry(q_ref, local_ref, rates_ref[:, lane_slice(part)], base_ref, extra_ref, out_ref, part, part)


def across_kernel(extra_ref, base_ref, q_ref, local_ref, out_ref):
    modes = base_ref.shape[0]
    seg_len = q_ref.shape[0]
    pieces = [
        local_ref[first : first + modes, :].astype(jnp.float32)
        for first in range(seg_len, local_ref.shape[0], modes)
    ]
    rates = (pieces[2] + pieces[1]) + pieces[0]
    for part in range(q_ref.shape[1] // LANES):
        lanes = lane_slice(part)
        carry(q_ref, local_ref.at[:, lanes], rates[:, lanes], base_ref, extra_ref, out_ref, part, part)


def project(blocks, weight_ref):
    total = None
    for rank, parts in blocks:
        depth = weight_ref.shape[0] // lax.axis_size("chan")
        offset = pl.multiple_of(rank * depth, depth)
        for block in parts:
            rows = pl.ds(offset, block.shape[1])
            term = jnp.dot(block[...], weight_ref[rows, :], preferred_element_type=jnp.float32)
            total = term if total is None else total + term
            offset = pl.multiple_of(offset + block.shape[1], block.shape[1])
    return total


def near_kernel(weight_ref, bias_ref, own_ref, pair_ref, *rest):
    across, out_ref = rest[:-1], rest[-1]
    rank = lax.axis_index("chan")
    blocks = [(rank, [own_ref]), (rank ^ 1, [pair_ref]), (rank ^ 2, across)]
    out_ref[...] = project(blocks, weight_ref) + bias_ref[...]


def last_kernel(near_ref, weight_ref, *rest):
    diagonal, (out_hbm, out_ref, sems) = rest[:-3], rest[-3:]
    rank = lax.axis_index("chan")
    pieces = sems.shape[0]
    size = out_ref.shape[0] // pieces
    copies = []
    for i in range(pieces):
        rows = pl.ds(i * size, size)
        total = near_ref[rows, :] + project([(rank ^ 3, [ref.at[rows, :] for ref in diagonal])], weight_ref)
        out_ref[rows, :] = total.astype(out_ref.dtype)
        copies.append(pltpu.make_async_copy(out_ref.at[rows], out_hbm.at[rows], sems.at[i]))
        copies[-1].start()
    for copy in copies:
        copy.wait()


def call(kernel, out, *args, cost=0, aliases=(), scratch=(), hbm=0, outs=pltpu.VMEM):
    spaces = [pltpu.HBM] * hbm + [pltpu.VMEM] * (len(args) - hbm)
    return pl.pallas_call(
        kernel,
        out_shape=out,
        in_specs=[pl.BlockSpec(memory_space=space) for space in spaces],
        out_specs=jax.tree.map(lambda _: pl.BlockSpec(memory_space=outs), out),
        scratch_shapes=list(scratch),
        input_output_aliases=dict(aliases),
        compiler_params=pltpu.CompilerParams(vmem_limit_bytes=VMEM_LIMIT),
        cost_estimate=pl.CostEstimate(flops=cost, bytes_accessed=0, transcendentals=0),
    )(*args)


def struct(shape, dtype=jnp.float32):
    return jax.ShapeDtypeStruct(shape, dtype)


def swapped(value, bit):
    count = lax.axis_size("chan")
    return lax.ppermute(value, "chan", [(r, r ^ bit) for r in range(count)])


def beside(value):
    count = lax.axis_size("seq")
    return lax.ppermute(value, "seq", [(r, r ^ 1) for r in range(count)])


def along(value, stride, route):
    count, radix = lax.axis_size("seq"), len(route)

    def target(r):
        spot = r // stride % radix
        return r + (route[spot] - spot) * stride

    return lax.ppermute(value, "seq", [(r, target(r)) for r in range(count)])


def corner(value, step, bit):
    count, width = lax.axis_size("seq"), lax.axis_size("chan")
    pairs = [(r * width + c, (r ^ step) * width + (c ^ bit)) for r in range(count) for c in range(width)]
    return lax.ppermute(value, ("seq", "chan"), pairs)


def carry_shares(total, own, decay, residue, seg_len, also):
    count = lax.axis_size("seq") // 2
    shape = struct(total.shape)
    inner, stride = (), 1
    while True:
        radix = min(4, count // stride)
        received = [along(total, 2 * stride, route) for route in ROUTES[radix]]
        if stride * radix == count:
            break
        kernel = functools.partial(fold_kernel, stride, seg_len)
        *inner, total = call(kernel, [shape, shape], decay, total, *inner, *received)
        stride *= radix
    received, also = lax.optimization_barrier((received, also))
    kernel = functools.partial(share_kernel, stride, seg_len)
    base, extra = call(kernel, [shape, shape], decay, residue, own, total, *inner, *received, cost=FOLD_COST)
    return base, extra, also


def shards(q_gate, k_gate, value, decay, residue, skip, out_weight, out_bias):
    seg_len, channels = value.shape
    modes = decay.shape[0]
    cols = out_weight.shape[1]
    parts = channels // LANES
    tall = pltpu.VMEM((seg_len, channels), jnp.bfloat16)
    q_across = swapped(q_gate, 2)
    inputs = (k_gate, value, decay, residue, skip.reshape(1, -1), out_bias.reshape(1, -1))
    inputs = [pltpu.with_memory_space_constraint(x, pltpu.HBM) for x in inputs]
    tall = pltpu.VMEM((seg_len, channels), jnp.bfloat16)
    scratch = [tall, tall, pltpu.SemaphoreType.DMA((2 * parts + 4,))]
    few = struct((modes, channels))
    kept = [
        struct((modes, SUBLANES, channels)),
        struct((parts, seg_len, LANES)),
        few,
        few,
        struct((1, channels)),
        struct((1, cols)),
        struct((seg_len, LANES)),
        struct((seg_len + PIECES * modes, channels), jnp.bfloat16),
    ]
    scratch += [pltpu.VMEM((modes, SUBLANES, LANES), jnp.float32)]
    total, *state = call(state_kernel, [few, *kept], *inputs, scratch=scratch, hbm=INPUTS)
    more = [struct((seg_len, LANES))] * (parts - 1)
    own_total, *state = call(
        local_kernel, [few, *kept, *more], *inputs, total, *state,
        scratch=scratch, hbm=INPUTS, aliases=[(INPUTS + 1 + i, 1 + i) for i in range(KEPT)],
    )
    _, _, decay, residue, _, bias, first_local, local_short, *more = state
    local = [first_local, *more]
    local_across = swapped(local_short, 2)
    base, extra, q_across = carry_shares(total, own_total, decay, residue, seg_len, q_across)
    extra_beside = beside(extra)
    extra_corner = corner(extra, 1, 2)
    base_across = swapped(base, 2)
    whole = struct((seg_len, channels), jnp.bfloat16)
    own = call(own_kernel, whole, q_gate, decay, base, extra_beside, *local, cost=OWN_COST)
    pair = swapped(own, 1)
    across = call(
        across_kernel, whole, extra_corner, base_across, q_across, local_across, cost=PART_COST
    )
    diagonal = swapped(across, 1)
    near = call(near_kernel, struct((seg_len, cols)), out_weight, bias, own, pair, across)
    return call(
        last_kernel, struct((seg_len, cols), jnp.bfloat16), near, out_weight, diagonal,
        scratch=[pltpu.VMEM((seg_len, cols), jnp.bfloat16), pltpu.SemaphoreType.DMA((STORES,))],
        outs=pltpu.HBM,
    )


def solution(mesh):
    return jax.shard_map(
        shards,
        mesh=mesh,
        in_specs=(
            P("seq", "chan"),
            P("seq", "chan"),
            P("seq", "chan"),
            P(None, "chan"),
            P(None, "chan"),
            P("chan"),
            P(None, "chan"),
            P("chan"),
        ),
        out_specs=P("seq", "chan"),
        check_vma=False,
    )
```

```python
import functools

import jax
import jax.numpy as jnp
from jax import lax
from jax.experimental import pallas as pl
from jax.experimental.pallas import tpu as pltpu
from jax.sharding import PartitionSpec as P

LANES = 128
SUBLANES = 8
STORES = 4
OWN_COST = 0
FOLD_COST = 3000000000
PIECES = 3
ROUTES = {2: [(1, 0)], 4: [(3, 2, 0, 1), (2, 3, 0, 1), (1, 0, 3, 2)]}
FIRST_COST = 30000000000
PART_COST = 0
VMEM_LIMIT = 32 * 1024 * 1024


def row(ref, mode, part):
    return ref[mode : mode + 1, part * LANES : (part + 1) * LANES]


def full(value):
    return jnp.broadcast_to(value, (SUBLANES, LANES))


def lane_slice(part):
    return slice(part * LANES, (part + 1) * LANES)


def summarize(zero, k_ref, v_ref, decay_ref, total_ref, chunk_ref, gated_ref):
    modes = decay_ref.shape[0]
    chunk_len = k_ref.shape[0] // SUBLANES
    later = (SUBLANES - 1 - lax.broadcasted_iota(jnp.int32, (SUBLANES, LANES), 0)) * chunk_len
    later = later.astype(jnp.float32)
    for part in range(gated_ref.shape[0]):
        lanes = lane_slice(part)
        product = k_ref[:, lanes].astype(jnp.float32) * v_ref[:, lanes].astype(jnp.float32)
        gated_ref[part] = product.astype(jnp.bfloat16).astype(jnp.float32)
        factor = [full(jnp.exp(-row(decay_ref, n, part))) for n in range(modes)]
        square = [f * f for f in factor]

        def step(t, state):
            x = gated_ref[part, pl.ds(2 * t, SUBLANES, stride=chunk_len), :]
            y = gated_ref[part, pl.ds(2 * t + 1, SUBLANES, stride=chunk_len), :]
            return tuple(g * h + (f * x + y) for f, g, h in zip(factor, square, state))

        state = lax.fori_loop(0, chunk_len // 2, step, (zero,) * modes, unroll=4)
        for n in range(modes):
            chunk_ref[n, :, lanes] = state[n]
            weight = jnp.exp(-row(decay_ref, n, part) * later)
            total_ref[n : n + 1, lanes] = jnp.sum(weight * state[n], axis=0, keepdims=True)


def is_last():
    count = lax.axis_size("seq")
    return lax.axis_index("seq") >= count - 2


def is_first():
    return lax.axis_index("seq") < 2


def first_kernel(out_ref):
    out_ref[...] = jnp.zeros_like(out_ref)


def state_kernel(
    zero_ref, k_ref, v_ref, decay_ref, residue_ref, skip_hbm,
    total_ref, chunk_ref, gated_ref, skip_ref, local_ref, short_ref, weights, sem,
):
    @pl.when(jnp.logical_not(is_last()))
    def _():
        copy = pltpu.make_async_copy(skip_hbm, skip_ref, sem)
        copy.start()
        summarize(zero_ref[...], k_ref, v_ref, decay_ref, total_ref, chunk_ref, gated_ref)
        copy.wait()

    @pl.when(is_last())
    def _():
        total_ref[...] = jnp.zeros_like(total_ref)

    @pl.when(is_first())
    def _():
        convolve(0, gated_ref, decay_ref, residue_ref, skip_ref, chunk_ref, local_ref, short_ref, weights)


def local_kernel(
    zero_ref, k_ref, v_ref, decay_ref, residue_ref, skip_hbm,
    total_in, chunk_in, gated_in, skip_in, local_in, short_in,
    total_ref, short_ref, *rest,
):
    locals_out, (chunk_ref, gated_ref, skip_ref, weights, sem) = rest[:-5], rest[-5:]

    def part_of(part, gated, skip, chunk):
        convolve(part, gated, decay_ref, residue_ref, skip, chunk, locals_out[part], short_ref, weights)

    @pl.when(is_last())
    def _():
        copy = pltpu.make_async_copy(skip_hbm, skip_ref, sem)
        copy.start()
        summarize(zero_ref[...], k_ref, v_ref, decay_ref, total_ref, chunk_ref, gated_ref)
        copy.wait()
        for part in range(len(locals_out)):
            part_of(part, gated_ref, skip_ref, chunk_ref)

    @pl.when(jnp.logical_not(is_last()))
    def _():
        total_ref[...] = total_in[...]
        for part in range(1, len(locals_out)):
            part_of(part, gated_in, skip_in, chunk_in)

    @pl.when(is_first())
    def _():
        locals_out[0][...] = local_in[...]
        short_ref[:, lane_slice(0)] = short_in[...]

    @pl.when(jnp.logical_not(jnp.logical_or(is_first(), is_last())))
    def _():
        part_of(0, gated_in, skip_in, chunk_in)


def convolve(part, gated, decay_ref, residue_ref, skip_ref, chunk_ref, local_ref, short_ref, weights):
    modes = decay_ref.shape[0]
    seg_len = gated.shape[1]
    chunk_len = seg_len // SUBLANES
    index = lax.broadcasted_iota(jnp.int32, (SUBLANES, LANES), 0)
    lanes = lane_slice(part)
    factor, start = [], []
    for n in range(modes):
        rate = row(decay_ref, n, part)
        prefix = chunk_ref[n, :, lanes]
        for shift in (1, 2, 4):
            moved = jnp.where(index >= shift, pltpu.roll(prefix, shift, 0), 0.0)
            prefix = prefix + jnp.exp(-rate * (shift * chunk_len)) * moved
        start.append(jnp.where(index >= 1, pltpu.roll(prefix, 1, 0), 0.0))
        factor.append(full(jnp.exp(-rate)))
        weights[n] = full(row(residue_ref, n, part))
    bypass = full(skip_ref[:, lanes])

    def step(t, state):
        rows = pl.ds(t, SUBLANES, stride=chunk_len)
        x = gated[part, rows, :]
        state = tuple(f * h + x for f, h in zip(factor, state))
        sums = [bypass * x] + [None] * 3
        for n, h in enumerate(state):
            term = weights[n] * h
            sums[n % 4] = term if sums[n % 4] is None else sums[n % 4] + term
        local_ref[rows, :] = (sums[0] + sums[1]) + (sums[2] + sums[3])
        return state

    lax.fori_loop(0, chunk_len, step, tuple(start), unroll=4)
    spot = lanes if short_ref.shape[1] > LANES else slice(None)
    short_ref[:seg_len, spot] = local_ref[...].astype(short_ref.dtype)
    left = decay_ref[:, lanes]
    for first in range(seg_len, short_ref.shape[0], modes):
        piece = left.astype(short_ref.dtype)
        short_ref[first : first + modes, spot] = piece
        left = left - piece.astype(jnp.float32)


def lookup(spot, table):
    found = table[0]
    for i, entry in enumerate(table[1:]):
        found = jnp.where(spot == i + 1, entry, found)
    return found


def fold(rates, inner, total, received, stride, seg_len):
    place = lax.div(lax.axis_index("seq"), 2)
    radix = len(received) + 1
    spot = lax.rem(lax.div(place, stride), radix)
    offset = lax.rem(place, stride)

    def decayed(segments):
        return jnp.exp(-rates * (segments * 2 * seg_len).astype(jnp.float32))

    before = jnp.zeros_like(rates)
    whole = decayed((radix - 1 - spot) * stride) * total
    for route, block in zip(ROUTES[radix], received):
        source = lookup(spot, [route.index(i) for i in range(radix)])
        past = source < spot
        gap = jnp.where(past, spot - 1 - source, 0) * stride
        before += jnp.where(past, decayed(gap) * block, 0.0)
        whole += decayed((radix - 1 - source) * stride) * block
    return inner + decayed(offset) * before, whole


def fold_kernel(stride, seg_len, rates_ref, total_ref, *rest):
    inner, rest = (rest[0][...], rest[1:]) if stride > 1 else (0.0, rest)
    received, (inner_out, total_out) = [ref[...] for ref in rest[:-2]], rest[-2:]
    inner_out[...], total_out[...] = fold(
        rates_ref[...], inner, total_ref[...], received, stride, seg_len
    )


def share_kernel(stride, seg_len, rates_ref, residue_ref, own_ref, total_ref, *rest):
    inner, rest = (rest[0][...], rest[1:]) if stride > 1 else (0.0, rest)
    received, (base_ref, extra_ref) = [ref[...] for ref in rest[:-2]], rest[-2:]
    rates = rates_ref[...]
    before, _ = fold(rates, inner, total_ref[...], received, stride, seg_len)
    before *= residue_ref[...]
    step = jnp.exp(-rates * float(seg_len))
    even = lax.rem(lax.axis_index("seq"), 2) == 0
    base_ref[...] = step * before
    extra_ref[...] = jnp.where(even, residue_ref[...] * own_ref[...] + step * step * before, before)


def carry(q_ref, local_ref, rates, base_ref, extra_ref, out_ref, part, column):
    modes = rates.shape[0]
    seg_len = q_ref.shape[0]
    block = 2 * SUBLANES
    ahead = (lax.broadcasted_iota(jnp.int32, (SUBLANES, LANES), 0) + 1).astype(jnp.float32)
    lanes = lane_slice(part)
    factor, start = [], []
    for n in range(modes):
        rate = rates[n : n + 1, :]
        weight = row(base_ref, n, part) + row(extra_ref, n, part)
        start.append(weight * jnp.exp(-rate * ahead))
        factor.append(full(jnp.exp(-rate * SUBLANES)))

    def step(j, state):
        rows = pl.ds(pl.multiple_of(j * block, block), block)
        halves = []
        for _ in range(2):
            sums = list(state[:4])
            for n, h in enumerate(state[4:]):
                sums[n % 4] = sums[n % 4] + h
            halves.append((sums[0] + sums[1]) + (sums[2] + sums[3]))
            state = tuple(f * h for f, h in zip(factor, state))
        total = local_ref[rows, :].astype(jnp.float32) + jnp.concatenate(halves, axis=0)
        gate_rows = q_ref[rows, lanes].astype(jnp.float32)
        out_ref[rows, lane_slice(column)] = (gate_rows * total).astype(out_ref.dtype)
        return state

    lax.fori_loop(0, seg_len // block, step, tuple(start), unroll=4)


def own_kernel(q_ref, rates_ref, base_ref, extra_ref, *rest):
    locals_in, out_ref = rest[:-1], rest[-1]
    for part, local_ref in enumerate(locals_in):
        carry(q_ref, local_ref, rates_ref[:, lane_slice(part)], base_ref, extra_ref, out_ref, part, part)


def across_kernel(extra_ref, base_ref, q_ref, local_ref, out_ref):
    modes = base_ref.shape[0]
    seg_len = q_ref.shape[0]
    pieces = [
        local_ref[first : first + modes, :].astype(jnp.float32)
        for first in range(seg_len, local_ref.shape[0], modes)
    ]
    rates = (pieces[2] + pieces[1]) + pieces[0]
    for part in range(q_ref.shape[1] // LANES):
        lanes = lane_slice(part)
        carry(q_ref, local_ref.at[:, lanes], rates[:, lanes], base_ref, extra_ref, out_ref, part, part)


def project(blocks, weight_ref):
    total = None
    for rank, parts in blocks:
        depth = weight_ref.shape[0] // lax.axis_size("chan")
        offset = pl.multiple_of(rank * depth, depth)
        for block in parts:
            rows = pl.ds(offset, block.shape[1])
            term = jnp.dot(block[...], weight_ref[rows, :], preferred_element_type=jnp.float32)
            total = term if total is None else total + term
            offset = pl.multiple_of(offset + block.shape[1], block.shape[1])
    return total


def near_kernel(weight_ref, bias_ref, own_ref, pair_ref, *rest):
    across, out_ref = rest[:-1], rest[-1]
    rank = lax.axis_index("chan")
    blocks = [(rank, [own_ref]), (rank ^ 1, [pair_ref]), (rank ^ 2, across)]
    out_ref[...] = project(blocks, weight_ref) + bias_ref[...]


def last_kernel(near_ref, weight_ref, *rest):
    diagonal, (out_hbm, out_ref, sems) = rest[:-3], rest[-3:]
    rank = lax.axis_index("chan")
    pieces = sems.shape[0]
    size = out_ref.shape[0] // pieces
    copies = []
    for i in range(pieces):
        rows = pl.ds(i * size, size)
        total = near_ref[rows, :] + project([(rank ^ 3, [ref.at[rows, :] for ref in diagonal])], weight_ref)
        out_ref[rows, :] = total.astype(out_ref.dtype)
        copies.append(pltpu.make_async_copy(out_ref.at[rows], out_hbm.at[rows], sems.at[i]))
        copies[-1].start()
    for copy in copies:
        copy.wait()


def call(kernel, out, *args, cost=0, scratch=(), hbm=(), outs=pltpu.VMEM):
    return pl.pallas_call(
        kernel,
        out_shape=out,
        in_specs=[pl.BlockSpec(memory_space=pltpu.HBM if i in hbm else pltpu.VMEM) for i in range(len(args))],
        out_specs=jax.tree.map(lambda _: pl.BlockSpec(memory_space=outs), out),
        scratch_shapes=list(scratch),
        compiler_params=pltpu.CompilerParams(vmem_limit_bytes=VMEM_LIMIT),
        cost_estimate=pl.CostEstimate(flops=cost, bytes_accessed=0, transcendentals=0),
    )(*args)


def struct(shape, dtype=jnp.float32):
    return jax.ShapeDtypeStruct(shape, dtype)


def swapped(value, bit):
    count = lax.axis_size("chan")
    return lax.ppermute(value, "chan", [(r, r ^ bit) for r in range(count)])


def beside(value):
    count = lax.axis_size("seq")
    return lax.ppermute(value, "seq", [(r, r ^ 1) for r in range(count)])


def along(value, stride, route):
    count, radix = lax.axis_size("seq"), len(route)

    def target(r):
        spot = r // stride % radix
        return r + (route[spot] - spot) * stride

    return lax.ppermute(value, "seq", [(r, target(r)) for r in range(count)])


def corner(value, step, bit):
    count, width = lax.axis_size("seq"), lax.axis_size("chan")
    pairs = [(r * width + c, (r ^ step) * width + (c ^ bit)) for r in range(count) for c in range(width)]
    return lax.ppermute(value, ("seq", "chan"), pairs)


def carry_shares(total, own, decay, residue, seg_len, also):
    count = lax.axis_size("seq") // 2
    shape = struct(total.shape)
    inner, stride = (), 1
    while True:
        radix = min(4, count // stride)
        received = [along(total, 2 * stride, route) for route in ROUTES[radix]]
        if stride * radix == count:
            break
        kernel = functools.partial(fold_kernel, stride, seg_len)
        *inner, total = call(kernel, [shape, shape], decay, total, *inner, *received)
        stride *= radix
    received, also = lax.optimization_barrier((received, also))
    kernel = functools.partial(share_kernel, stride, seg_len)
    base, extra = call(kernel, [shape, shape], decay, residue, own, total, *inner, *received, cost=FOLD_COST)
    return base, extra, also


def shards(q_gate, k_gate, value, decay, residue, skip, out_weight, out_bias):
    seg_len, channels = value.shape
    modes = decay.shape[0]
    cols = out_weight.shape[1]
    parts = channels // LANES
    bias = out_bias.reshape(1, -1)
    zero = call(first_kernel, struct((SUBLANES, LANES)), cost=FIRST_COST)
    q_across = swapped(q_gate, 2)
    few = struct((modes, channels))
    chunks, gated, bypass = (modes, SUBLANES, channels), (parts, seg_len, LANES), (1, channels)
    thin = struct((seg_len, LANES))
    tall = seg_len + PIECES * modes
    skip = pltpu.with_memory_space_constraint(skip.reshape(1, -1), pltpu.HBM)
    inputs = (zero, k_gate, value, decay, residue, skip)
    scratch = [pltpu.VMEM((modes, SUBLANES, LANES), jnp.float32), pltpu.SemaphoreType.DMA]
    total, *state = call(
        state_kernel,
        [few, struct(chunks), struct(gated), struct(bypass), thin, struct((tall, LANES), jnp.bfloat16)],
        *inputs,
        scratch=scratch, hbm=(5,),
    )
    own_total, local_short, *local = call(
        local_kernel,
        [few, struct((tall, channels), jnp.bfloat16), *[thin] * parts],
        *inputs, total, *state,
        scratch=[pltpu.VMEM(shape, jnp.float32) for shape in (chunks, gated, bypass)] + scratch, hbm=(5,),
    )
    local_across = swapped(local_short, 2)
    base, extra, q_across = carry_shares(total, own_total, decay, residue, seg_len, q_across)
    extra_beside = beside(extra)
    extra_corner = corner(extra, 1, 2)
    base_across = swapped(base, 2)
    whole = struct((seg_len, channels), jnp.bfloat16)
    own = call(own_kernel, whole, q_gate, decay, base, extra_beside, *local, cost=OWN_COST)
    pair = swapped(own, 1)
    across = call(
        across_kernel, whole, extra_corner, base_across, q_across, local_across, cost=PART_COST
    )
    diagonal = swapped(across, 1)
    near = call(near_kernel, struct((seg_len, cols)), out_weight, bias, own, pair, across)
    return call(
        last_kernel, struct((seg_len, cols), jnp.bfloat16), near, out_weight, diagonal,
        scratch=[pltpu.VMEM((seg_len, cols), jnp.bfloat16), pltpu.SemaphoreType.DMA((STORES,))],
        outs=pltpu.HBM,
    )


def solution(mesh):
    return jax.shard_map(
        shards,
        mesh=mesh,
        in_specs=(
            P("seq", "chan"),
            P("seq", "chan"),
            P("seq", "chan"),
            P(None, "chan"),
            P(None, "chan"),
            P("chan"),
            P(None, "chan"),
            P("chan"),
        ),
        out_specs=P("seq", "chan"),
        check_vma=False,
    )
```

```python
import functools

import jax
import jax.numpy as jnp
from jax import lax
from jax.experimental import pallas as pl
from jax.experimental.pallas import tpu as pltpu
from jax.sharding import PartitionSpec as P

LANES = 128
SUBLANES = 8
STORES = 4
OWN_COST = 3000000000
FOLD_COST = 500000000
PIECES = 2
ROUTES = {2: [(1, 0)], 4: [(3, 2, 0, 1), (2, 3, 0, 1), (1, 0, 3, 2)]}
MORE_COST = 1000000000
FIRST_COST = 30000000000
NEAR_COST = 3000000000
PART_COST = 1000000000
VMEM_LIMIT = 32 * 1024 * 1024


def row(ref, mode, part):
    return ref[mode : mode + 1, part * LANES : (part + 1) * LANES]


def full(value):
    return jnp.broadcast_to(value, (SUBLANES, LANES))


def lane_slice(part):
    return slice(part * LANES, (part + 1) * LANES)


def summarize(zero, k_ref, v_ref, decay_ref, total_ref, chunk_ref, gated_ref):
    modes = decay_ref.shape[0]
    chunk_len = k_ref.shape[0] // SUBLANES
    later = (SUBLANES - 1 - lax.broadcasted_iota(jnp.int32, (SUBLANES, LANES), 0)) * chunk_len
    later = later.astype(jnp.float32)
    for part in range(gated_ref.shape[0]):
        lanes = lane_slice(part)
        product = k_ref[:, lanes].astype(jnp.float32) * v_ref[:, lanes].astype(jnp.float32)
        gated_ref[part] = product.astype(jnp.bfloat16).astype(jnp.float32)
        factor = [full(jnp.exp(-row(decay_ref, n, part))) for n in range(modes)]
        square = [f * f for f in factor]

        def step(t, state):
            x = gated_ref[part, pl.ds(2 * t, SUBLANES, stride=chunk_len), :]
            y = gated_ref[part, pl.ds(2 * t + 1, SUBLANES, stride=chunk_len), :]
            return tuple(g * h + (f * x + y) for f, g, h in zip(factor, square, state))

        state = lax.fori_loop(0, chunk_len // 2, step, (zero,) * modes, unroll=4)
        for n in range(modes):
            chunk_ref[n, :, lanes] = state[n]
            weight = jnp.exp(-row(decay_ref, n, part) * later)
            total_ref[n : n + 1, lanes] = jnp.sum(weight * state[n], axis=0, keepdims=True)


def is_last():
    count = lax.axis_size("seq")
    return lax.axis_index("seq") >= count - 2


def is_first():
    return lax.axis_index("seq") < 2


def first_kernel(out_ref):
    out_ref[...] = jnp.zeros_like(out_ref)


def state_kernel(
    zero_ref, k_ref, v_ref, decay_ref, residue_ref, skip_hbm,
    total_ref, chunk_ref, gated_ref, skip_ref, local_ref, short_ref, weights, sem,
):
    @pl.when(jnp.logical_not(is_last()))
    def _():
        copy = pltpu.make_async_copy(skip_hbm, skip_ref, sem)
        copy.start()
        summarize(zero_ref[...], k_ref, v_ref, decay_ref, total_ref, chunk_ref, gated_ref)
        copy.wait()

    @pl.when(is_last())
    def _():
        total_ref[...] = jnp.zeros_like(total_ref)

    @pl.when(is_first())
    def _():
        convolve(0, gated_ref, decay_ref, residue_ref, skip_ref, chunk_ref, local_ref, short_ref, weights)


def first_part_kernel(
    zero_ref, k_ref, v_ref, decay_ref, residue_ref, skip_hbm,
    total_in, chunk_in, gated_in, skip_in, local_in, short_in,
    total_ref, chunk_ref, gated_ref, skip_ref, local_ref, short_ref, weights, sem,
):
    @pl.when(is_last())
    def _():
        copy = pltpu.make_async_copy(skip_hbm, skip_ref, sem)
        copy.start()
        summarize(zero_ref[...], k_ref, v_ref, decay_ref, total_ref, chunk_ref, gated_ref)
        copy.wait()
        convolve(0, gated_ref, decay_ref, residue_ref, skip_ref, chunk_ref, local_ref, short_ref, weights)

    @pl.when(jnp.logical_not(is_last()))
    def _():
        total_ref[...] = total_in[...]

    @pl.when(is_first())
    def _():
        local_ref[...] = local_in[...]
        short_ref[...] = short_in[...]

    @pl.when(jnp.logical_not(jnp.logical_or(is_first(), is_last())))
    def _():
        convolve(0, gated_in, decay_ref, residue_ref, skip_in, chunk_in, local_ref, short_ref, weights)


def other_part_kernel(
    part, decay_ref, residue_ref, chunk_in, gated_in, skip_in, chunk_last, gated_last, skip_last,
    local_ref, short_ref, weights,
):
    @pl.when(is_last())
    def _():
        convolve(part, gated_last, decay_ref, residue_ref, skip_last, chunk_last, local_ref, short_ref, weights)

    @pl.when(jnp.logical_not(is_last()))
    def _():
        convolve(part, gated_in, decay_ref, residue_ref, skip_in, chunk_in, local_ref, short_ref, weights)


def convolve(part, gated, decay_ref, residue_ref, skip_ref, chunk_ref, local_ref, short_ref, weights):
    modes = decay_ref.shape[0]
    seg_len = gated.shape[1]
    chunk_len = seg_len // SUBLANES
    index = lax.broadcasted_iota(jnp.int32, (SUBLANES, LANES), 0)
    lanes = lane_slice(part)
    factor, start = [], []
    for n in range(modes):
        rate = row(decay_ref, n, part)
        prefix = chunk_ref[n, :, lanes]
        for shift in (1, 2, 4):
            moved = jnp.where(index >= shift, pltpu.roll(prefix, shift, 0), 0.0)
            prefix = prefix + jnp.exp(-rate * (shift * chunk_len)) * moved
        start.append(jnp.where(index >= 1, pltpu.roll(prefix, 1, 0), 0.0))
        factor.append(full(jnp.exp(-rate)))
        weights[n] = full(row(residue_ref, n, part))
    bypass = full(skip_ref[:, lanes])

    def step(t, state):
        rows = pl.ds(t, SUBLANES, stride=chunk_len)
        x = gated[part, rows, :]
        state = tuple(f * h + x for f, h in zip(factor, state))
        sums = [bypass * x] + [None] * 3
        for n, h in enumerate(state):
            term = weights[n] * h
            sums[n % 4] = term if sums[n % 4] is None else sums[n % 4] + term
        local_ref[rows, :] = (sums[0] + sums[1]) + (sums[2] + sums[3])
        return state

    lax.fori_loop(0, chunk_len, step, tuple(start), unroll=4)
    short_ref[:seg_len, :] = local_ref[...].astype(short_ref.dtype)
    left = decay_ref[:, lanes]
    for first in range(seg_len, short_ref.shape[0], modes):
        piece = left.astype(short_ref.dtype)
        short_ref[first : first + modes, :] = piece
        left = left - piece.astype(jnp.float32)


def lookup(spot, table):
    found = table[0]
    for i, entry in enumerate(table[1:]):
        found = jnp.where(spot == i + 1, entry, found)
    return found


def fold(rates, inner, total, received, stride, seg_len):
    place = lax.div(lax.axis_index("seq"), 2)
    radix = len(received) + 1
    spot = lax.rem(lax.div(place, stride), radix)
    offset = lax.rem(place, stride)

    def decayed(segments):
        return jnp.exp(-rates * (segments * 2 * seg_len).astype(jnp.float32))

    before = jnp.zeros_like(rates)
    whole = decayed((radix - 1 - spot) * stride) * total
    for route, block in zip(ROUTES[radix], received):
        source = lookup(spot, [route.index(i) for i in range(radix)])
        past = source < spot
        gap = jnp.where(past, spot - 1 - source, 0) * stride
        before += jnp.where(past, decayed(gap) * block, 0.0)
        whole += decayed((radix - 1 - source) * stride) * block
    return inner + decayed(offset) * before, whole


def fold_kernel(stride, seg_len, rates_ref, total_ref, *rest):
    inner, rest = (rest[0][...], rest[1:]) if stride > 1 else (0.0, rest)
    received, (inner_out, total_out) = [ref[...] for ref in rest[:-2]], rest[-2:]
    inner_out[...], total_out[...] = fold(
        rates_ref[...], inner, total_ref[...], received, stride, seg_len
    )


def share_kernel(stride, seg_len, rates_ref, residue_ref, own_ref, total_ref, *rest):
    inner, rest = (rest[0][...], rest[1:]) if stride > 1 else (0.0, rest)
    received, (base_ref, extra_ref) = [ref[...] for ref in rest[:-2]], rest[-2:]
    rates = rates_ref[...]
    before, _ = fold(rates, inner, total_ref[...], received, stride, seg_len)
    before *= residue_ref[...]
    step = jnp.exp(-rates * float(seg_len))
    even = lax.rem(lax.axis_index("seq"), 2) == 0
    base_ref[...] = step * before
    extra_ref[...] = jnp.where(even, residue_ref[...] * own_ref[...] + step * step * before, before)


def carry(q_ref, local_ref, rates, base_ref, extra_ref, out_ref, part, column):
    modes = rates.shape[0]
    seg_len = q_ref.shape[0]
    block = 2 * SUBLANES
    ahead = (lax.broadcasted_iota(jnp.int32, (SUBLANES, LANES), 0) + 1).astype(jnp.float32)
    lanes = lane_slice(part)
    factor, start = [], []
    for n in range(modes):
        rate = rates[n : n + 1, :]
        weight = row(base_ref, n, part) + row(extra_ref, n, part)
        start.append(weight * jnp.exp(-rate * ahead))
        factor.append(full(jnp.exp(-rate * SUBLANES)))

    def step(j, state):
        rows = pl.ds(pl.multiple_of(j * block, block), block)
        halves = []
        for _ in range(2):
            sums = list(state[:4])
            for n, h in enumerate(state[4:]):
                sums[n % 4] = sums[n % 4] + h
            halves.append((sums[0] + sums[1]) + (sums[2] + sums[3]))
            state = tuple(f * h for f, h in zip(factor, state))
        total = local_ref[rows, :].astype(jnp.float32) + jnp.concatenate(halves, axis=0)
        gate_rows = q_ref[rows, lanes].astype(jnp.float32)
        out_ref[rows, lane_slice(column)] = (gate_rows * total).astype(out_ref.dtype)
        return state

    lax.fori_loop(0, seg_len // block, step, tuple(start), unroll=4)


def own_kernel(q_ref, rates_ref, base_ref, extra_ref, *rest):
    locals_in, out_ref = rest[:-1], rest[-1]
    for part, local_ref in enumerate(locals_in):
        carry(q_ref, local_ref, rates_ref[:, lane_slice(part)], base_ref, extra_ref, out_ref, part, part)


def across_kernel(part, extra_ref, base_ref, q_ref, local_ref, out_ref):
    modes = base_ref.shape[0]
    seg_len = q_ref.shape[0]
    rates = sum(
        local_ref[first : first + modes, :].astype(jnp.float32)
        for first in reversed(range(seg_len, local_ref.shape[0], modes))
    )
    carry(q_ref, local_ref, rates, base_ref, extra_ref, out_ref, part, 0)


def project(blocks, weight_ref):
    total = None
    for rank, parts in blocks:
        depth = weight_ref.shape[0] // lax.axis_size("chan")
        offset = pl.multiple_of(rank * depth, depth)
        for block in parts:
            rows = pl.ds(offset, block.shape[1])
            term = jnp.dot(block[...], weight_ref[rows, :], preferred_element_type=jnp.float32)
            total = term if total is None else total + term
            offset = pl.multiple_of(offset + block.shape[1], block.shape[1])
    return total


def near_kernel(weight_ref, bias_ref, own_ref, *rest):
    blocks, out_ref = rest[:-1], rest[-1]
    parts = len(blocks) // 2
    rank = lax.axis_index("chan")
    blocks = [(rank, [own_ref]), (rank ^ 2, blocks[:parts]), (rank ^ 3, blocks[parts:])]
    out_ref[...] = project(blocks, weight_ref) + bias_ref[...]


def last_kernel(near_ref, weight_ref, *rest):
    pair, (out_hbm, out_ref, sems) = rest[:-3], rest[-3:]
    rank = lax.axis_index("chan")
    pieces = sems.shape[0]
    size = out_ref.shape[0] // pieces
    copies = []
    for i in range(pieces):
        rows = pl.ds(i * size, size)
        total = near_ref[rows, :] + project([(rank ^ 1, [ref.at[rows, :] for ref in pair])], weight_ref)
        out_ref[rows, :] = total.astype(out_ref.dtype)
        copies.append(pltpu.make_async_copy(out_ref.at[rows], out_hbm.at[rows], sems.at[i]))
        copies[-1].start()
    for copy in copies:
        copy.wait()


def call(kernel, out, *args, cost=0, scratch=(), hbm=(), outs=pltpu.VMEM):
    return pl.pallas_call(
        kernel,
        out_shape=out,
        in_specs=[pl.BlockSpec(memory_space=pltpu.HBM if i in hbm else pltpu.VMEM) for i in range(len(args))],
        out_specs=jax.tree.map(lambda _: pl.BlockSpec(memory_space=outs), out),
        scratch_shapes=list(scratch),
        compiler_params=pltpu.CompilerParams(vmem_limit_bytes=VMEM_LIMIT),
        cost_estimate=pl.CostEstimate(flops=cost, bytes_accessed=0, transcendentals=0),
    )(*args)


def struct(shape, dtype=jnp.float32):
    return jax.ShapeDtypeStruct(shape, dtype)


def swapped(value, bit):
    count = lax.axis_size("chan")
    return lax.ppermute(value, "chan", [(r, r ^ bit) for r in range(count)])


def beside(value):
    count = lax.axis_size("seq")
    return lax.ppermute(value, "seq", [(r, r ^ 1) for r in range(count)])


def along(value, stride, route):
    count, radix = lax.axis_size("seq"), len(route)

    def target(r):
        spot = r // stride % radix
        return r + (route[spot] - spot) * stride

    return lax.ppermute(value, "seq", [(r, target(r)) for r in range(count)])


def corner(value, step, bit):
    count, width = lax.axis_size("seq"), lax.axis_size("chan")
    pairs = [(r * width + c, (r ^ step) * width + (c ^ bit)) for r in range(count) for c in range(width)]
    return lax.ppermute(value, ("seq", "chan"), pairs)


def carry_shares(total, own, decay, residue, seg_len, also):
    count = lax.axis_size("seq") // 2
    shape = struct(total.shape)
    inner, stride = (), 1
    while True:
        radix = min(4, count // stride)
        received = [along(total, 2 * stride, route) for route in ROUTES[radix]]
        if stride * radix == count:
            break
        kernel = functools.partial(fold_kernel, stride, seg_len)
        *inner, total = call(kernel, [shape, shape], decay, total, *inner, *received)
        stride *= radix
    received, also = lax.optimization_barrier((received, also))
    kernel = functools.partial(share_kernel, stride, seg_len)
    base, extra = call(kernel, [shape, shape], decay, residue, own, total, *inner, *received, cost=FOLD_COST)
    return base, extra, also


def shards(q_gate, k_gate, value, decay, residue, skip, out_weight, out_bias):
    seg_len, channels = value.shape
    modes = decay.shape[0]
    cols = out_weight.shape[1]
    parts = channels // LANES
    bias = out_bias.reshape(1, -1)
    zero = call(first_kernel, struct((SUBLANES, LANES)), cost=FIRST_COST)
    q_across = swapped(q_gate, 2)
    few = struct((modes, channels))
    chunks, gated, bypass = (modes, SUBLANES, channels), (parts, seg_len, LANES), (1, channels)
    thin = struct((seg_len, LANES))
    tall = seg_len + PIECES * modes
    skip = pltpu.with_memory_space_constraint(skip.reshape(1, -1), pltpu.HBM)
    inputs = (zero, k_gate, value, decay, residue, skip)
    scratch = [pltpu.VMEM((modes, SUBLANES, LANES), jnp.float32), pltpu.SemaphoreType.DMA]
    thin_short = struct((tall, LANES), jnp.bfloat16)
    kept = [struct(chunks), struct(gated), struct(bypass)]
    total, *state = call(state_kernel, [few, *kept, thin, thin_short], *inputs, scratch=scratch, hbm=(5,))
    own_total, *last_state = call(
        first_part_kernel, [few, *kept, thin, thin_short], *inputs, total, *state, scratch=scratch, hbm=(5,)
    )
    local, short = [last_state[3]], [last_state[4]]
    for part in range(1, parts):
        more = call(
            functools.partial(other_part_kernel, part), [thin, thin_short],
            decay, residue, *state[:3], *last_state[:3],
            scratch=scratch[:1], cost=MORE_COST,
        )
        local.append(more[0])
        short.append(more[1])
    local_across = [swapped(block, 2) for block in short]
    base, extra, q_across = carry_shares(total, own_total, decay, residue, seg_len, q_across)
    extra_corner = corner(extra, 1, 2)
    base_across = swapped(base, 2)
    half = struct((seg_len, LANES), jnp.bfloat16)
    across = []
    for part in range(parts):
        block = call(
            functools.partial(across_kernel, part), half,
            extra_corner, base_across, q_across, local_across[part],
            cost=PART_COST,
        )
        block, extra_corner = lax.optimization_barrier((block, extra_corner))
        across.append(block)
    diagonal = [swapped(block, 1) for block in across]
    extra_beside, *across = lax.optimization_barrier((beside(extra), *across))
    whole = struct((seg_len, channels), jnp.bfloat16)
    own = call(own_kernel, whole, q_gate, decay, base, extra_beside, *local, cost=OWN_COST)
    pair = swapped(own, 1)
    near = call(
        near_kernel, struct((seg_len, cols)), out_weight, bias, own, *across, *diagonal, cost=NEAR_COST
    )
    return call(
        last_kernel, struct((seg_len, cols), jnp.bfloat16), near, out_weight, pair,
        scratch=[pltpu.VMEM((seg_len, cols), jnp.bfloat16), pltpu.SemaphoreType.DMA((STORES,))],
        outs=pltpu.HBM,
    )


def solution(mesh):
    return jax.shard_map(
        shards,
        mesh=mesh,
        in_specs=(
            P("seq", "chan"),
            P("seq", "chan"),
            P("seq", "chan"),
            P(None, "chan"),
            P(None, "chan"),
            P("chan"),
            P(None, "chan"),
            P("chan"),
        ),
        out_specs=P("seq", "chan"),
        check_vma=False,
    )
```

```python
import functools

import jax
import jax.numpy as jnp
from jax import lax
from jax.experimental import pallas as pl
from jax.experimental.pallas import tpu as pltpu
from jax.sharding import PartitionSpec as P

LANES = 128
SUBLANES = 8
STORES = 4
OWN_COST = 1000000000
FOLD_COST = 700000000
PIECES = 2
ROUTES = {2: [(1, 0)], 4: [(3, 2, 0, 1), (2, 3, 0, 1), (1, 0, 3, 2)]}
MORE_COST = 1000000000
FIRST_COST = 30000000000
PART_COST = 0
VMEM_LIMIT = 32 * 1024 * 1024


def row(ref, mode, part):
    return ref[mode : mode + 1, part * LANES : (part + 1) * LANES]


def full(value):
    return jnp.broadcast_to(value, (SUBLANES, LANES))


def lane_slice(part):
    return slice(part * LANES, (part + 1) * LANES)


def summarize(zero, k_ref, v_ref, decay_ref, total_ref, chunk_ref, gated_ref):
    modes = decay_ref.shape[0]
    chunk_len = k_ref.shape[0] // SUBLANES
    later = (SUBLANES - 1 - lax.broadcasted_iota(jnp.int32, (SUBLANES, LANES), 0)) * chunk_len
    later = later.astype(jnp.float32)
    for part in range(gated_ref.shape[0]):
        lanes = lane_slice(part)
        product = k_ref[:, lanes].astype(jnp.float32) * v_ref[:, lanes].astype(jnp.float32)
        gated_ref[part] = product.astype(jnp.bfloat16).astype(jnp.float32)
        factor = [full(jnp.exp(-row(decay_ref, n, part))) for n in range(modes)]
        square = [f * f for f in factor]

        def step(t, state):
            x = gated_ref[part, pl.ds(2 * t, SUBLANES, stride=chunk_len), :]
            y = gated_ref[part, pl.ds(2 * t + 1, SUBLANES, stride=chunk_len), :]
            return tuple(g * h + (f * x + y) for f, g, h in zip(factor, square, state))

        state = lax.fori_loop(0, chunk_len // 2, step, (zero,) * modes, unroll=4)
        for n in range(modes):
            chunk_ref[n, :, lanes] = state[n]
            weight = jnp.exp(-row(decay_ref, n, part) * later)
            total_ref[n : n + 1, lanes] = jnp.sum(weight * state[n], axis=0, keepdims=True)


def is_last():
    count = lax.axis_size("seq")
    return lax.axis_index("seq") >= count - 2


def is_first():
    return lax.axis_index("seq") < 2


def first_kernel(out_ref):
    out_ref[...] = jnp.zeros_like(out_ref)


def state_kernel(
    zero_ref, k_ref, v_ref, decay_ref, residue_ref, skip_hbm,
    total_ref, chunk_ref, gated_ref, skip_ref, local_ref, short_ref, weights, sem,
):
    @pl.when(jnp.logical_not(is_last()))
    def _():
        copy = pltpu.make_async_copy(skip_hbm, skip_ref, sem)
        copy.start()
        summarize(zero_ref[...], k_ref, v_ref, decay_ref, total_ref, chunk_ref, gated_ref)
        copy.wait()

    @pl.when(is_last())
    def _():
        total_ref[...] = jnp.zeros_like(total_ref)

    @pl.when(is_first())
    def _():
        convolve(0, gated_ref, decay_ref, residue_ref, skip_ref, chunk_ref, local_ref, short_ref, weights)


def first_part_kernel(
    zero_ref, k_ref, v_ref, decay_ref, residue_ref, skip_hbm,
    total_in, chunk_in, gated_in, skip_in, local_in, short_in,
    total_ref, chunk_ref, gated_ref, skip_ref, local_ref, short_ref, weights, sem,
):
    @pl.when(is_last())
    def _():
        copy = pltpu.make_async_copy(skip_hbm, skip_ref, sem)
        copy.start()
        summarize(zero_ref[...], k_ref, v_ref, decay_ref, total_ref, chunk_ref, gated_ref)
        copy.wait()
        convolve(0, gated_ref, decay_ref, residue_ref, skip_ref, chunk_ref, local_ref, short_ref, weights)

    @pl.when(jnp.logical_not(is_last()))
    def _():
        total_ref[...] = total_in[...]

    @pl.when(is_first())
    def _():
        local_ref[...] = local_in[...]
        short_ref[...] = short_in[...]

    @pl.when(jnp.logical_not(jnp.logical_or(is_first(), is_last())))
    def _():
        convolve(0, gated_in, decay_ref, residue_ref, skip_in, chunk_in, local_ref, short_ref, weights)


def other_part_kernel(
    part, decay_ref, residue_ref, chunk_in, gated_in, skip_in, chunk_last, gated_last, skip_last,
    local_ref, short_ref, weights,
):
    @pl.when(is_last())
    def _():
        convolve(part, gated_last, decay_ref, residue_ref, skip_last, chunk_last, local_ref, short_ref, weights)

    @pl.when(jnp.logical_not(is_last()))
    def _():
        convolve(part, gated_in, decay_ref, residue_ref, skip_in, chunk_in, local_ref, short_ref, weights)


def convolve(part, gated, decay_ref, residue_ref, skip_ref, chunk_ref, local_ref, short_ref, weights):
    modes = decay_ref.shape[0]
    seg_len = gated.shape[1]
    chunk_len = seg_len // SUBLANES
    index = lax.broadcasted_iota(jnp.int32, (SUBLANES, LANES), 0)
    lanes = lane_slice(part)
    factor, start = [], []
    for n in range(modes):
        rate = row(decay_ref, n, part)
        prefix = chunk_ref[n, :, lanes]
        for shift in (1, 2, 4):
            moved = jnp.where(index >= shift, pltpu.roll(prefix, shift, 0), 0.0)
            prefix = prefix + jnp.exp(-rate * (shift * chunk_len)) * moved
        start.append(jnp.where(index >= 1, pltpu.roll(prefix, 1, 0), 0.0))
        factor.append(full(jnp.exp(-rate)))
        weights[n] = full(row(residue_ref, n, part))
    bypass = full(skip_ref[:, lanes])

    def step(t, state):
        rows = pl.ds(t, SUBLANES, stride=chunk_len)
        x = gated[part, rows, :]
        state = tuple(f * h + x for f, h in zip(factor, state))
        sums = [bypass * x] + [None] * 3
        for n, h in enumerate(state):
            term = weights[n] * h
            sums[n % 4] = term if sums[n % 4] is None else sums[n % 4] + term
        local_ref[rows, :] = (sums[0] + sums[1]) + (sums[2] + sums[3])
        return state

    lax.fori_loop(0, chunk_len, step, tuple(start), unroll=4)
    short_ref[:seg_len, :] = local_ref[...].astype(short_ref.dtype)
    left = decay_ref[:, lanes]
    for first in range(seg_len, short_ref.shape[0], modes):
        piece = left.astype(short_ref.dtype)
        short_ref[first : first + modes, :] = piece
        left = left - piece.astype(jnp.float32)


def lookup(spot, table):
    found = table[0]
    for i, entry in enumerate(table[1:]):
        found = jnp.where(spot == i + 1, entry, found)
    return found


def fold(rates, inner, total, received, stride, seg_len):
    place = lax.div(lax.axis_index("seq"), 2)
    radix = len(received) + 1
    spot = lax.rem(lax.div(place, stride), radix)
    offset = lax.rem(place, stride)

    def decayed(segments):
        return jnp.exp(-rates * (segments * 2 * seg_len).astype(jnp.float32))

    before = jnp.zeros_like(rates)
    whole = decayed((radix - 1 - spot) * stride) * total
    for route, block in zip(ROUTES[radix], received):
        source = lookup(spot, [route.index(i) for i in range(radix)])
        past = source < spot
        gap = jnp.where(past, spot - 1 - source, 0) * stride
        before += jnp.where(past, decayed(gap) * block, 0.0)
        whole += decayed((radix - 1 - source) * stride) * block
    return inner + decayed(offset) * before, whole


def fold_kernel(stride, seg_len, rates_ref, total_ref, *rest):
    inner, rest = (rest[0][...], rest[1:]) if stride > 1 else (0.0, rest)
    received, (inner_out, total_out) = [ref[...] for ref in rest[:-2]], rest[-2:]
    inner_out[...], total_out[...] = fold(
        rates_ref[...], inner, total_ref[...], received, stride, seg_len
    )


def share_kernel(stride, seg_len, rates_ref, residue_ref, own_ref, total_ref, *rest):
    inner, rest = (rest[0][...], rest[1:]) if stride > 1 else (0.0, rest)
    received, (base_ref, extra_ref) = [ref[...] for ref in rest[:-2]], rest[-2:]
    rates = rates_ref[...]
    before, _ = fold(rates, inner, total_ref[...], received, stride, seg_len)
    before *= residue_ref[...]
    step = jnp.exp(-rates * float(seg_len))
    even = lax.rem(lax.axis_index("seq"), 2) == 0
    base_ref[...] = step * before
    extra_ref[...] = jnp.where(even, residue_ref[...] * own_ref[...] + step * step * before, before)


def carry(q_ref, local_ref, rates, base_ref, extra_ref, out_ref, part, column):
    modes = rates.shape[0]
    seg_len = q_ref.shape[0]
    block = 2 * SUBLANES
    ahead = (lax.broadcasted_iota(jnp.int32, (SUBLANES, LANES), 0) + 1).astype(jnp.float32)
    lanes = lane_slice(part)
    factor, start = [], []
    for n in range(modes):
        rate = rates[n : n + 1, :]
        weight = row(base_ref, n, part) + row(extra_ref, n, part)
        start.append(weight * jnp.exp(-rate * ahead))
        factor.append(full(jnp.exp(-rate * SUBLANES)))

    def step(j, state):
        rows = pl.ds(pl.multiple_of(j * block, block), block)
        halves = []
        for _ in range(2):
            sums = list(state[:4])
            for n, h in enumerate(state[4:]):
                sums[n % 4] = sums[n % 4] + h
            halves.append((sums[0] + sums[1]) + (sums[2] + sums[3]))
            state = tuple(f * h for f, h in zip(factor, state))
        total = local_ref[rows, :].astype(jnp.float32) + jnp.concatenate(halves, axis=0)
        gate_rows = q_ref[rows, lanes].astype(jnp.float32)
        out_ref[rows, lane_slice(column)] = (gate_rows * total).astype(out_ref.dtype)
        return state

    lax.fori_loop(0, seg_len // block, step, tuple(start), unroll=4)


def own_kernel(q_ref, rates_ref, base_ref, extra_ref, *rest):
    locals_in, out_ref = rest[:-1], rest[-1]
    for part, local_ref in enumerate(locals_in):
        carry(q_ref, local_ref, rates_ref[:, lane_slice(part)], base_ref, extra_ref, out_ref, part, part)


def across_kernel(extra_ref, base_ref, q_ref, *rest):
    blocks, out_ref = rest[:-1], rest[-1]
    modes = base_ref.shape[0]
    seg_len = q_ref.shape[0]
    for part, local_ref in enumerate(blocks):
        rates = sum(
            local_ref[first : first + modes, :].astype(jnp.float32)
            for first in reversed(range(seg_len, local_ref.shape[0], modes))
        )
        carry(q_ref, local_ref, rates, base_ref, extra_ref, out_ref, part, part)


def project(blocks, weight_ref):
    total = None
    for rank, parts in blocks:
        depth = weight_ref.shape[0] // lax.axis_size("chan")
        offset = pl.multiple_of(rank * depth, depth)
        for block in parts:
            rows = pl.ds(offset, block.shape[1])
            term = jnp.dot(block[...], weight_ref[rows, :], preferred_element_type=jnp.float32)
            total = term if total is None else total + term
            offset = pl.multiple_of(offset + block.shape[1], block.shape[1])
    return total


def near_kernel(weight_ref, bias_ref, own_ref, pair_ref, *rest):
    across, out_ref = rest[:-1], rest[-1]
    rank = lax.axis_index("chan")
    blocks = [(rank, [own_ref]), (rank ^ 1, [pair_ref]), (rank ^ 2, across)]
    out_ref[...] = project(blocks, weight_ref) + bias_ref[...]


def last_kernel(near_ref, weight_ref, *rest):
    diagonal, (out_hbm, out_ref, sems) = rest[:-3], rest[-3:]
    rank = lax.axis_index("chan")
    pieces = sems.shape[0]
    size = out_ref.shape[0] // pieces
    copies = []
    for i in range(pieces):
        rows = pl.ds(i * size, size)
        total = near_ref[rows, :] + project([(rank ^ 3, [ref.at[rows, :] for ref in diagonal])], weight_ref)
        out_ref[rows, :] = total.astype(out_ref.dtype)
        copies.append(pltpu.make_async_copy(out_ref.at[rows], out_hbm.at[rows], sems.at[i]))
        copies[-1].start()
    for copy in copies:
        copy.wait()


def call(kernel, out, *args, cost=0, scratch=(), hbm=(), outs=pltpu.VMEM):
    return pl.pallas_call(
        kernel,
        out_shape=out,
        in_specs=[pl.BlockSpec(memory_space=pltpu.HBM if i in hbm else pltpu.VMEM) for i in range(len(args))],
        out_specs=jax.tree.map(lambda _: pl.BlockSpec(memory_space=outs), out),
        scratch_shapes=list(scratch),
        compiler_params=pltpu.CompilerParams(vmem_limit_bytes=VMEM_LIMIT),
        cost_estimate=pl.CostEstimate(flops=cost, bytes_accessed=0, transcendentals=0),
    )(*args)


def struct(shape, dtype=jnp.float32):
    return jax.ShapeDtypeStruct(shape, dtype)


def swapped(value, bit):
    count = lax.axis_size("chan")
    return lax.ppermute(value, "chan", [(r, r ^ bit) for r in range(count)])


def beside(value):
    count = lax.axis_size("seq")
    return lax.ppermute(value, "seq", [(r, r ^ 1) for r in range(count)])


def along(value, stride, route):
    count, radix = lax.axis_size("seq"), len(route)

    def target(r):
        spot = r // stride % radix
        return r + (route[spot] - spot) * stride

    return lax.ppermute(value, "seq", [(r, target(r)) for r in range(count)])


def corner(value, step, bit):
    count, width = lax.axis_size("seq"), lax.axis_size("chan")
    pairs = [(r * width + c, (r ^ step) * width + (c ^ bit)) for r in range(count) for c in range(width)]
    return lax.ppermute(value, ("seq", "chan"), pairs)


def carry_shares(total, own, decay, residue, seg_len, also):
    count = lax.axis_size("seq") // 2
    shape = struct(total.shape)
    inner, stride = (), 1
    while True:
        radix = min(4, count // stride)
        received = [along(total, 2 * stride, route) for route in ROUTES[radix]]
        if stride * radix == count:
            break
        kernel = functools.partial(fold_kernel, stride, seg_len)
        *inner, total = call(kernel, [shape, shape], decay, total, *inner, *received)
        stride *= radix
    received, also = lax.optimization_barrier((received, also))
    kernel = functools.partial(share_kernel, stride, seg_len)
    base, extra = call(kernel, [shape, shape], decay, residue, own, total, *inner, *received, cost=FOLD_COST)
    return base, extra, also


def shards(q_gate, k_gate, value, decay, residue, skip, out_weight, out_bias):
    seg_len, channels = value.shape
    modes = decay.shape[0]
    cols = out_weight.shape[1]
    parts = channels // LANES
    bias = out_bias.reshape(1, -1)
    zero = call(first_kernel, struct((SUBLANES, LANES)), cost=FIRST_COST)
    q_across = swapped(q_gate, 2)
    few = struct((modes, channels))
    chunks, gated, bypass = (modes, SUBLANES, channels), (parts, seg_len, LANES), (1, channels)
    thin = struct((seg_len, LANES))
    tall = seg_len + PIECES * modes
    skip = pltpu.with_memory_space_constraint(skip.reshape(1, -1), pltpu.HBM)
    inputs = (zero, k_gate, value, decay, residue, skip)
    scratch = [pltpu.VMEM((modes, SUBLANES, LANES), jnp.float32), pltpu.SemaphoreType.DMA]
    thin_short = struct((tall, LANES), jnp.bfloat16)
    kept = [struct(chunks), struct(gated), struct(bypass)]
    total, *state = call(state_kernel, [few, *kept, thin, thin_short], *inputs, scratch=scratch, hbm=(5,))
    own_total, *last_state = call(
        first_part_kernel, [few, *kept, thin, thin_short], *inputs, total, *state, scratch=scratch, hbm=(5,)
    )
    local, short = [last_state[3]], [last_state[4]]
    for part in range(1, parts):
        more = call(
            functools.partial(other_part_kernel, part), [thin, thin_short],
            decay, residue, *state[:3], *last_state[:3],
            scratch=scratch[:1], cost=MORE_COST,
        )
        local.append(more[0])
        short.append(more[1])
    local_across = [swapped(block, 2) for block in short]
    base, extra, q_across = carry_shares(total, own_total, decay, residue, seg_len, q_across)
    extra_beside, local_across[0] = lax.optimization_barrier((beside(extra), local_across[0]))
    extra_corner = corner(extra, 1, 2)
    base_across = swapped(base, 2)
    whole = struct((seg_len, channels), jnp.bfloat16)
    own = call(own_kernel, whole, q_gate, decay, base, extra_beside, *local, cost=OWN_COST)
    pair = swapped(own, 1)
    across = call(
        across_kernel, whole, extra_corner, base_across, q_across, *local_across, cost=PART_COST
    )
    diagonal = swapped(across, 1)
    near = call(near_kernel, struct((seg_len, cols)), out_weight, bias, own, pair, across)
    return call(
        last_kernel, struct((seg_len, cols), jnp.bfloat16), near, out_weight, diagonal,
        scratch=[pltpu.VMEM((seg_len, cols), jnp.bfloat16), pltpu.SemaphoreType.DMA((STORES,))],
        outs=pltpu.HBM,
    )


def solution(mesh):
    return jax.shard_map(
        shards,
        mesh=mesh,
        in_specs=(
            P("seq", "chan"),
            P("seq", "chan"),
            P("seq", "chan"),
            P(None, "chan"),
            P(None, "chan"),
            P("chan"),
            P(None, "chan"),
            P("chan"),
        ),
        out_specs=P("seq", "chan"),
        check_vma=False,
    )
```

```python
import functools

import jax
import jax.numpy as jnp
from jax import lax
from jax.experimental import pallas as pl
from jax.experimental.pallas import tpu as pltpu
from jax.sharding import PartitionSpec as P

LANES = 128
SUBLANES = 8
STORES = 4
OWN_COST = 0
FOLD_COST = 3000000000
PIECES = 3
ROUTES = {2: [(1, 0)], 4: [(3, 2, 0, 1), (2, 3, 0, 1), (1, 0, 3, 2)]}
FIRST_COST = 30000000000
PART_COST = 1500000000
NEAR_COST = 0
VMEM_LIMIT = 32 * 1024 * 1024


def row(ref, mode, part):
    return ref[mode : mode + 1, part * LANES : (part + 1) * LANES]


def full(value):
    return jnp.broadcast_to(value, (SUBLANES, LANES))


def lane_slice(part):
    return slice(part * LANES, (part + 1) * LANES)


def summarize(zero, k_ref, v_ref, decay_ref, total_ref, chunk_ref, gated_ref):
    modes = decay_ref.shape[0]
    chunk_len = k_ref.shape[0] // SUBLANES
    later = (SUBLANES - 1 - lax.broadcasted_iota(jnp.int32, (SUBLANES, LANES), 0)) * chunk_len
    later = later.astype(jnp.float32)
    for part in range(gated_ref.shape[0]):
        lanes = lane_slice(part)
        product = k_ref[:, lanes].astype(jnp.float32) * v_ref[:, lanes].astype(jnp.float32)
        gated_ref[part] = product.astype(jnp.bfloat16).astype(jnp.float32)
        factor = [full(jnp.exp(-row(decay_ref, n, part))) for n in range(modes)]
        square = [f * f for f in factor]

        def step(t, state):
            x = gated_ref[part, pl.ds(2 * t, SUBLANES, stride=chunk_len), :]
            y = gated_ref[part, pl.ds(2 * t + 1, SUBLANES, stride=chunk_len), :]
            return tuple(g * h + (f * x + y) for f, g, h in zip(factor, square, state))

        state = lax.fori_loop(0, chunk_len // 2, step, (zero,) * modes, unroll=4)
        for n in range(modes):
            chunk_ref[n, :, lanes] = state[n]
            weight = jnp.exp(-row(decay_ref, n, part) * later)
            total_ref[n : n + 1, lanes] = jnp.sum(weight * state[n], axis=0, keepdims=True)


def is_last():
    count = lax.axis_size("seq")
    return lax.axis_index("seq") >= count - 2


def is_first():
    return lax.axis_index("seq") < 2


def first_kernel(out_ref):
    out_ref[...] = jnp.zeros_like(out_ref)


def state_kernel(
    zero_ref, k_ref, v_ref, decay_ref, residue_ref, skip_hbm,
    total_ref, chunk_ref, gated_ref, skip_ref, local_ref, short_ref, weights, sem,
):
    @pl.when(jnp.logical_not(is_last()))
    def _():
        copy = pltpu.make_async_copy(skip_hbm, skip_ref, sem)
        copy.start()
        summarize(zero_ref[...], k_ref, v_ref, decay_ref, total_ref, chunk_ref, gated_ref)
        copy.wait()

    @pl.when(is_last())
    def _():
        total_ref[...] = jnp.zeros_like(total_ref)

    @pl.when(is_first())
    def _():
        convolve(0, gated_ref, decay_ref, residue_ref, skip_ref, chunk_ref, local_ref, short_ref, weights)


def local_kernel(
    zero_ref, k_ref, v_ref, decay_ref, residue_ref, skip_hbm,
    total_in, chunk_in, gated_in, skip_in, local_in, short_in,
    total_ref, short_ref, *rest,
):
    locals_out, (chunk_ref, gated_ref, skip_ref, weights, sem) = rest[:-5], rest[-5:]

    def part_of(part, gated, skip, chunk):
        convolve(part, gated, decay_ref, residue_ref, skip, chunk, locals_out[part], short_ref, weights)

    @pl.when(is_last())
    def _():
        copy = pltpu.make_async_copy(skip_hbm, skip_ref, sem)
        copy.start()
        summarize(zero_ref[...], k_ref, v_ref, decay_ref, total_ref, chunk_ref, gated_ref)
        copy.wait()
        for part in range(len(locals_out)):
            part_of(part, gated_ref, skip_ref, chunk_ref)

    @pl.when(jnp.logical_not(is_last()))
    def _():
        total_ref[...] = total_in[...]
        for part in range(1, len(locals_out)):
            part_of(part, gated_in, skip_in, chunk_in)

    @pl.when(is_first())
    def _():
        locals_out[0][...] = local_in[...]
        short_ref[:, lane_slice(0)] = short_in[...]

    @pl.when(jnp.logical_not(jnp.logical_or(is_first(), is_last())))
    def _():
        part_of(0, gated_in, skip_in, chunk_in)


def convolve(part, gated, decay_ref, residue_ref, skip_ref, chunk_ref, local_ref, short_ref, weights):
    modes = decay_ref.shape[0]
    seg_len = gated.shape[1]
    chunk_len = seg_len // SUBLANES
    index = lax.broadcasted_iota(jnp.int32, (SUBLANES, LANES), 0)
    lanes = lane_slice(part)
    factor, start = [], []
    for n in range(modes):
        rate = row(decay_ref, n, part)
        prefix = chunk_ref[n, :, lanes]
        for shift in (1, 2, 4):
            moved = jnp.where(index >= shift, pltpu.roll(prefix, shift, 0), 0.0)
            prefix = prefix + jnp.exp(-rate * (shift * chunk_len)) * moved
        start.append(jnp.where(index >= 1, pltpu.roll(prefix, 1, 0), 0.0))
        factor.append(full(jnp.exp(-rate)))
        weights[n] = full(row(residue_ref, n, part))
    bypass = full(skip_ref[:, lanes])

    def step(t, state):
        rows = pl.ds(t, SUBLANES, stride=chunk_len)
        x = gated[part, rows, :]
        state = tuple(f * h + x for f, h in zip(factor, state))
        sums = [bypass * x] + [None] * 3
        for n, h in enumerate(state):
            term = weights[n] * h
            sums[n % 4] = term if sums[n % 4] is None else sums[n % 4] + term
        local_ref[rows, :] = (sums[0] + sums[1]) + (sums[2] + sums[3])
        return state

    lax.fori_loop(0, chunk_len, step, tuple(start), unroll=4)
    spot = lanes if short_ref.shape[1] > LANES else slice(None)
    short_ref[:seg_len, spot] = local_ref[...].astype(short_ref.dtype)
    left = decay_ref[:, lanes]
    for first in range(seg_len, short_ref.shape[0], modes):
        piece = left.astype(short_ref.dtype)
        short_ref[first : first + modes, spot] = piece
        left = left - piece.astype(jnp.float32)


def lookup(spot, table):
    found = table[0]
    for i, entry in enumerate(table[1:]):
        found = jnp.where(spot == i + 1, entry, found)
    return found


def fold(rates, inner, total, received, stride, seg_len):
    place = lax.div(lax.axis_index("seq"), 2)
    radix = len(received) + 1
    spot = lax.rem(lax.div(place, stride), radix)
    offset = lax.rem(place, stride)

    def decayed(segments):
        return jnp.exp(-rates * (segments * 2 * seg_len).astype(jnp.float32))

    before = jnp.zeros_like(rates)
    whole = decayed((radix - 1 - spot) * stride) * total
    for route, block in zip(ROUTES[radix], received):
        source = lookup(spot, [route.index(i) for i in range(radix)])
        past = source < spot
        gap = jnp.where(past, spot - 1 - source, 0) * stride
        before += jnp.where(past, decayed(gap) * block, 0.0)
        whole += decayed((radix - 1 - source) * stride) * block
    return inner + decayed(offset) * before, whole


def fold_kernel(stride, seg_len, rates_ref, total_ref, *rest):
    inner, rest = (rest[0][...], rest[1:]) if stride > 1 else (0.0, rest)
    received, (inner_out, total_out) = [ref[...] for ref in rest[:-2]], rest[-2:]
    inner_out[...], total_out[...] = fold(
        rates_ref[...], inner, total_ref[...], received, stride, seg_len
    )


def share_kernel(stride, seg_len, rates_ref, residue_ref, own_ref, total_ref, *rest):
    inner, rest = (rest[0][...], rest[1:]) if stride > 1 else (0.0, rest)
    received, (base_ref, extra_ref) = [ref[...] for ref in rest[:-2]], rest[-2:]
    rates = rates_ref[...]
    before, _ = fold(rates, inner, total_ref[...], received, stride, seg_len)
    before *= residue_ref[...]
    step = jnp.exp(-rates * float(seg_len))
    even = lax.rem(lax.axis_index("seq"), 2) == 0
    base_ref[...] = step * before
    extra_ref[...] = jnp.where(even, residue_ref[...] * own_ref[...] + step * step * before, before)


def carry(q_ref, local_ref, rates, base_ref, extra_ref, out_ref, part, first_row=0):
    modes = rates.shape[0]
    block = 2 * SUBLANES
    ahead = (lax.broadcasted_iota(jnp.int32, (SUBLANES, LANES), 0) + 1 + first_row).astype(jnp.float32)
    lanes = lane_slice(part)
    factor, start = [], []
    for n in range(modes):
        rate = rates[n : n + 1, :]
        weight = row(base_ref, n, part) + row(extra_ref, n, part)
        start.append(weight * jnp.exp(-rate * ahead))
        factor.append(full(jnp.exp(-rate * SUBLANES)))

    def step(j, state):
        rows = pl.ds(pl.multiple_of(j * block + first_row, block), block)
        halves = []
        for _ in range(2):
            sums = list(state[:4])
            for n, h in enumerate(state[4:]):
                sums[n % 4] = sums[n % 4] + h
            halves.append((sums[0] + sums[1]) + (sums[2] + sums[3]))
            state = tuple(f * h for f, h in zip(factor, state))
        total = local_ref[rows, :].astype(jnp.float32) + jnp.concatenate(halves, axis=0)
        gate_rows = q_ref[rows, lanes].astype(jnp.float32)
        out_rows = pl.ds(pl.multiple_of(j * block, block), block)
        out_ref[out_rows, lanes] = (gate_rows * total).astype(out_ref.dtype)
        return state

    lax.fori_loop(0, out_ref.shape[0] // block, step, tuple(start), unroll=4)


def own_kernel(q_ref, rates_ref, base_ref, extra_ref, *rest):
    locals_in, out_ref = rest[:-1], rest[-1]
    for part, local_ref in enumerate(locals_in):
        carry(q_ref, local_ref, rates_ref[:, lane_slice(part)], base_ref, extra_ref, out_ref, part)


def across_kernel(first_row, extra_ref, base_ref, q_ref, local_ref, out_ref):
    modes = base_ref.shape[0]
    seg_len = q_ref.shape[0]
    pieces = [
        local_ref[first : first + modes, :].astype(jnp.float32)
        for first in range(seg_len, local_ref.shape[0], modes)
    ]
    rates = (pieces[2] + pieces[1]) + pieces[0]
    for part in range(q_ref.shape[1] // LANES):
        lanes = lane_slice(part)
        carry(q_ref, local_ref.at[:, lanes], rates[:, lanes], base_ref, extra_ref, out_ref, part, first_row)


def project(blocks, weight_ref):
    total = None
    for rank, parts in blocks:
        depth = weight_ref.shape[0] // lax.axis_size("chan")
        offset = pl.multiple_of(rank * depth, depth)
        for block in parts:
            rows = pl.ds(offset, block.shape[1])
            term = jnp.dot(block[...], weight_ref[rows, :], preferred_element_type=jnp.float32)
            total = term if total is None else total + term
            offset = pl.multiple_of(offset + block.shape[1], block.shape[1])
    return total


def near_kernel(weight_ref, bias_ref, own_ref, pair_ref, *rest):
    across, out_ref = rest[:-1], rest[-1]
    rank = lax.axis_index("chan")
    first = 0
    for across_ref in across:
        rows = pl.ds(first, across_ref.shape[0])
        blocks = [(rank, [own_ref.at[rows, :]]), (rank ^ 1, [pair_ref.at[rows, :]]), (rank ^ 2, [across_ref])]
        out_ref[rows, :] = project(blocks, weight_ref) + bias_ref[...]
        first += across_ref.shape[0]


def last_kernel(near_ref, weight_ref, *rest):
    diagonal, (out_hbm, out_ref, sems) = rest[:-3], rest[-3:]
    rank = lax.axis_index("chan")
    size = out_ref.shape[0] // sems.shape[0]
    cuts = [ref.at[pl.ds(first, size), :] for ref in diagonal for first in range(0, ref.shape[0], size)]
    copies = []
    for i, cut in enumerate(cuts):
        rows = pl.ds(i * size, size)
        total = near_ref[rows, :] + project([(rank ^ 3, [cut])], weight_ref)
        out_ref[rows, :] = total.astype(out_ref.dtype)
        copies.append(pltpu.make_async_copy(out_ref.at[rows], out_hbm.at[rows], sems.at[i]))
        copies[-1].start()
    for copy in copies:
        copy.wait()


def call(kernel, out, *args, cost=0, scratch=(), hbm=(), outs=pltpu.VMEM):
    return pl.pallas_call(
        kernel,
        out_shape=out,
        in_specs=[pl.BlockSpec(memory_space=pltpu.HBM if i in hbm else pltpu.VMEM) for i in range(len(args))],
        out_specs=jax.tree.map(lambda _: pl.BlockSpec(memory_space=outs), out),
        scratch_shapes=list(scratch),
        compiler_params=pltpu.CompilerParams(vmem_limit_bytes=VMEM_LIMIT),
        cost_estimate=pl.CostEstimate(flops=cost, bytes_accessed=0, transcendentals=0),
    )(*args)


def struct(shape, dtype=jnp.float32):
    return jax.ShapeDtypeStruct(shape, dtype)


def swapped(value, bit):
    count = lax.axis_size("chan")
    return lax.ppermute(value, "chan", [(r, r ^ bit) for r in range(count)])


def beside(value):
    count = lax.axis_size("seq")
    return lax.ppermute(value, "seq", [(r, r ^ 1) for r in range(count)])


def along(value, stride, route):
    count, radix = lax.axis_size("seq"), len(route)

    def target(r):
        spot = r // stride % radix
        return r + (route[spot] - spot) * stride

    return lax.ppermute(value, "seq", [(r, target(r)) for r in range(count)])


def corner(value, step, bit):
    count, width = lax.axis_size("seq"), lax.axis_size("chan")
    pairs = [(r * width + c, (r ^ step) * width + (c ^ bit)) for r in range(count) for c in range(width)]
    return lax.ppermute(value, ("seq", "chan"), pairs)


def carry_shares(total, own, decay, residue, seg_len, also):
    count = lax.axis_size("seq") // 2
    shape = struct(total.shape)
    inner, stride = (), 1
    while True:
        radix = min(4, count // stride)
        received = [along(total, 2 * stride, route) for route in ROUTES[radix]]
        if stride * radix == count:
            break
        kernel = functools.partial(fold_kernel, stride, seg_len)
        *inner, total = call(kernel, [shape, shape], decay, total, *inner, *received)
        stride *= radix
    received, also = lax.optimization_barrier((received, also))
    kernel = functools.partial(share_kernel, stride, seg_len)
    base, extra = call(kernel, [shape, shape], decay, residue, own, total, *inner, *received, cost=FOLD_COST)
    return base, extra, also


def shards(q_gate, k_gate, value, decay, residue, skip, out_weight, out_bias):
    seg_len, channels = value.shape
    modes = decay.shape[0]
    cols = out_weight.shape[1]
    parts = channels // LANES
    bias = out_bias.reshape(1, -1)
    zero = call(first_kernel, struct((SUBLANES, LANES)), cost=FIRST_COST)
    q_across = swapped(q_gate, 2)
    few = struct((modes, channels))
    chunks, gated, bypass = (modes, SUBLANES, channels), (parts, seg_len, LANES), (1, channels)
    thin = struct((seg_len, LANES))
    tall = seg_len + PIECES * modes
    skip = pltpu.with_memory_space_constraint(skip.reshape(1, -1), pltpu.HBM)
    inputs = (zero, k_gate, value, decay, residue, skip)
    scratch = [pltpu.VMEM((modes, SUBLANES, LANES), jnp.float32), pltpu.SemaphoreType.DMA]
    total, *state = call(
        state_kernel,
        [few, struct(chunks), struct(gated), struct(bypass), thin, struct((tall, LANES), jnp.bfloat16)],
        *inputs,
        scratch=scratch, hbm=(5,),
    )
    own_total, local_short, *local = call(
        local_kernel,
        [few, struct((tall, channels), jnp.bfloat16), *[thin] * parts],
        *inputs, total, *state,
        scratch=[pltpu.VMEM(shape, jnp.float32) for shape in (chunks, gated, bypass)] + scratch, hbm=(5,),
    )
    local_across = swapped(local_short, 2)
    base, extra, q_across = carry_shares(total, own_total, decay, residue, seg_len, q_across)
    extra_beside = beside(extra)
    extra_corner = corner(extra, 1, 2)
    base_across = swapped(base, 2)
    whole = struct((seg_len, channels), jnp.bfloat16)
    own = call(own_kernel, whole, q_gate, decay, base, extra_beside, *local, cost=OWN_COST)
    pair = swapped(own, 1)
    early = seg_len - seg_len // STORES
    across = [
        call(
            functools.partial(across_kernel, first), struct((count, channels), jnp.bfloat16),
            extra_corner, base_across, q_across, local_across,
            cost=PART_COST,
        )
        for first, count in ((0, early), (early, seg_len - early))
    ]
    diagonal = [swapped(block, 1) for block in across]
    near = call(near_kernel, struct((seg_len, cols)), out_weight, bias, own, pair, *across, cost=NEAR_COST)
    return call(
        last_kernel, struct((seg_len, cols), jnp.bfloat16), near, out_weight, *diagonal,
        scratch=[pltpu.VMEM((seg_len, cols), jnp.bfloat16), pltpu.SemaphoreType.DMA((STORES,))],
        outs=pltpu.HBM,
    )


def solution(mesh):
    return jax.shard_map(
        shards,
        mesh=mesh,
        in_specs=(
            P("seq", "chan"),
            P("seq", "chan"),
            P("seq", "chan"),
            P(None, "chan"),
            P(None, "chan"),
            P("chan"),
            P(None, "chan"),
            P("chan"),
        ),
        out_specs=P("seq", "chan"),
        check_vma=False,
    )
```

```python
import functools

import jax
import jax.numpy as jnp
from jax import lax
from jax.experimental import pallas as pl
from jax.experimental.pallas import tpu as pltpu
from jax.sharding import PartitionSpec as P

LANES = 128
SUBLANES = 8
STORES = 4
OWN_COST = 0
FOLD_COST = 3000000000
PIECES = 2
ROUTES = {2: [(1, 0)], 4: [(3, 2, 0, 1), (2, 3, 0, 1), (1, 0, 3, 2)]}
FIRST_COST = 30000000000
PART_COST = 0
VMEM_LIMIT = 32 * 1024 * 1024


def row(ref, mode, part):
    return ref[mode : mode + 1, part * LANES : (part + 1) * LANES]


def full(value):
    return jnp.broadcast_to(value, (SUBLANES, LANES))


def lane_slice(part):
    return slice(part * LANES, (part + 1) * LANES)


def summarize(zero, k_ref, v_ref, decay_ref, total_ref, chunk_ref, gated_ref):
    modes = decay_ref.shape[0]
    chunk_len = k_ref.shape[0] // SUBLANES
    later = (SUBLANES - 1 - lax.broadcasted_iota(jnp.int32, (SUBLANES, LANES), 0)) * chunk_len
    later = later.astype(jnp.float32)
    for part in range(gated_ref.shape[0]):
        lanes = lane_slice(part)
        product = k_ref[:, lanes].astype(jnp.float32) * v_ref[:, lanes].astype(jnp.float32)
        gated_ref[part] = product.astype(jnp.bfloat16).astype(jnp.float32)
        factor = [full(jnp.exp(-row(decay_ref, n, part))) for n in range(modes)]
        square = [f * f for f in factor]

        def step(t, state):
            x = gated_ref[part, pl.ds(2 * t, SUBLANES, stride=chunk_len), :]
            y = gated_ref[part, pl.ds(2 * t + 1, SUBLANES, stride=chunk_len), :]
            return tuple(g * h + (f * x + y) for f, g, h in zip(factor, square, state))

        state = lax.fori_loop(0, chunk_len // 2, step, (zero,) * modes, unroll=4)
        for n in range(modes):
            chunk_ref[n, :, lanes] = state[n]
            weight = jnp.exp(-row(decay_ref, n, part) * later)
            total_ref[n : n + 1, lanes] = jnp.sum(weight * state[n], axis=0, keepdims=True)


def is_last():
    count = lax.axis_size("seq")
    return lax.axis_index("seq") >= count - 2


def is_first():
    return lax.axis_index("seq") < 2


def first_kernel(out_ref):
    out_ref[...] = jnp.zeros_like(out_ref)


def state_kernel(
    zero_ref, k_ref, v_ref, decay_ref, residue_ref, skip_hbm,
    total_ref, chunk_ref, gated_ref, skip_ref, local_ref, short_ref, weights, sem,
):
    @pl.when(jnp.logical_not(is_last()))
    def _():
        copy = pltpu.make_async_copy(skip_hbm, skip_ref, sem)
        copy.start()
        summarize(zero_ref[...], k_ref, v_ref, decay_ref, total_ref, chunk_ref, gated_ref)
        copy.wait()

    @pl.when(is_last())
    def _():
        total_ref[...] = jnp.zeros_like(total_ref)

    @pl.when(is_first())
    def _():
        convolve(0, gated_ref, decay_ref, residue_ref, skip_ref, chunk_ref, local_ref, short_ref, weights)


def local_kernel(
    zero_ref, k_ref, v_ref, decay_ref, residue_ref, skip_hbm,
    total_in, chunk_in, gated_in, skip_in, local_in, short_in,
    total_ref, short_ref, *rest,
):
    locals_out, (chunk_ref, gated_ref, skip_ref, weights, sem) = rest[:-5], rest[-5:]

    def part_of(part, gated, skip, chunk):
        convolve(part, gated, decay_ref, residue_ref, skip, chunk, locals_out[part], short_ref, weights)

    @pl.when(is_last())
    def _():
        copy = pltpu.make_async_copy(skip_hbm, skip_ref, sem)
        copy.start()
        summarize(zero_ref[...], k_ref, v_ref, decay_ref, total_ref, chunk_ref, gated_ref)
        copy.wait()
        for part in range(len(locals_out)):
            part_of(part, gated_ref, skip_ref, chunk_ref)

    @pl.when(jnp.logical_not(is_last()))
    def _():
        total_ref[...] = total_in[...]
        for part in range(1, len(locals_out)):
            part_of(part, gated_in, skip_in, chunk_in)

    @pl.when(is_first())
    def _():
        locals_out[0][...] = local_in[...]
        short_ref[:, lane_slice(0)] = short_in[...]

    @pl.when(jnp.logical_not(jnp.logical_or(is_first(), is_last())))
    def _():
        part_of(0, gated_in, skip_in, chunk_in)


def convolve(part, gated, decay_ref, residue_ref, skip_ref, chunk_ref, local_ref, short_ref, weights):
    modes = decay_ref.shape[0]
    seg_len = gated.shape[1]
    chunk_len = seg_len // SUBLANES
    index = lax.broadcasted_iota(jnp.int32, (SUBLANES, LANES), 0)
    lanes = lane_slice(part)
    factor, start = [], []
    for n in range(modes):
        rate = row(decay_ref, n, part)
        prefix = chunk_ref[n, :, lanes]
        for shift in (1, 2, 4):
            moved = jnp.where(index >= shift, pltpu.roll(prefix, shift, 0), 0.0)
            prefix = prefix + jnp.exp(-rate * (shift * chunk_len)) * moved
        start.append(jnp.where(index >= 1, pltpu.roll(prefix, 1, 0), 0.0))
        factor.append(full(jnp.exp(-rate)))
        weights[n] = full(row(residue_ref, n, part))
    bypass = full(skip_ref[:, lanes])

    def step(t, state):
        rows = pl.ds(t, SUBLANES, stride=chunk_len)
        x = gated[part, rows, :]
        state = tuple(f * h + x for f, h in zip(factor, state))
        sums = [bypass * x] + [None] * 3
        for n, h in enumerate(state):
            term = weights[n] * h
            sums[n % 4] = term if sums[n % 4] is None else sums[n % 4] + term
        local_ref[rows, :] = (sums[0] + sums[1]) + (sums[2] + sums[3])
        return state

    lax.fori_loop(0, chunk_len, step, tuple(start), unroll=4)
    spot = lanes if short_ref.shape[1] > LANES else slice(None)
    short_ref[:seg_len, spot] = local_ref[...].astype(short_ref.dtype)
    left = decay_ref[:, lanes]
    for first in range(seg_len, short_ref.shape[0], modes):
        piece = left.astype(short_ref.dtype)
        short_ref[first : first + modes, spot] = piece
        left = left - piece.astype(jnp.float32)


def lookup(spot, table):
    found = table[0]
    for i, entry in enumerate(table[1:]):
        found = jnp.where(spot == i + 1, entry, found)
    return found


def fold(rates, inner, total, received, stride, seg_len):
    place = lax.div(lax.axis_index("seq"), 2)
    radix = len(received) + 1
    spot = lax.rem(lax.div(place, stride), radix)
    offset = lax.rem(place, stride)

    def decayed(segments):
        return jnp.exp(-rates * (segments * 2 * seg_len).astype(jnp.float32))

    before = jnp.zeros_like(rates)
    whole = decayed((radix - 1 - spot) * stride) * total
    for route, block in zip(ROUTES[radix], received):
        source = lookup(spot, [route.index(i) for i in range(radix)])
        past = source < spot
        gap = jnp.where(past, spot - 1 - source, 0) * stride
        before += jnp.where(past, decayed(gap) * block, 0.0)
        whole += decayed((radix - 1 - source) * stride) * block
    return inner + decayed(offset) * before, whole


def fold_kernel(stride, seg_len, rates_ref, total_ref, *rest):
    inner, rest = (rest[0][...], rest[1:]) if stride > 1 else (0.0, rest)
    received, (inner_out, total_out) = [ref[...] for ref in rest[:-2]], rest[-2:]
    inner_out[...], total_out[...] = fold(
        rates_ref[...], inner, total_ref[...], received, stride, seg_len
    )


def share_kernel(stride, seg_len, rates_ref, residue_ref, own_ref, total_ref, *rest):
    inner, rest = (rest[0][...], rest[1:]) if stride > 1 else (0.0, rest)
    received, (base_ref, extra_ref) = [ref[...] for ref in rest[:-2]], rest[-2:]
    rates = rates_ref[...]
    before, _ = fold(rates, inner, total_ref[...], received, stride, seg_len)
    before *= residue_ref[...]
    step = jnp.exp(-rates * float(seg_len))
    even = lax.rem(lax.axis_index("seq"), 2) == 0
    base_ref[...] = step * before
    extra_ref[...] = jnp.where(even, residue_ref[...] * own_ref[...] + step * step * before, before)


def carry(q_ref, local_ref, rates, base_ref, extra_ref, out_ref, part, column):
    modes = rates.shape[0]
    seg_len = q_ref.shape[0]
    block = 2 * SUBLANES
    ahead = (lax.broadcasted_iota(jnp.int32, (SUBLANES, LANES), 0) + 1).astype(jnp.float32)
    lanes = lane_slice(part)
    factor, start = [], []
    for n in range(modes):
        rate = rates[n : n + 1, :]
        weight = row(base_ref, n, part) + row(extra_ref, n, part)
        start.append(weight * jnp.exp(-rate * ahead))
        factor.append(full(jnp.exp(-rate * SUBLANES)))

    def step(j, state):
        rows = pl.ds(pl.multiple_of(j * block, block), block)
        halves = []
        for _ in range(2):
            sums = list(state[:4])
            for n, h in enumerate(state[4:]):
                sums[n % 4] = sums[n % 4] + h
            halves.append((sums[0] + sums[1]) + (sums[2] + sums[3]))
            state = tuple(f * h for f, h in zip(factor, state))
        total = local_ref[rows, :].astype(jnp.float32) + jnp.concatenate(halves, axis=0)
        gate_rows = q_ref[rows, lanes].astype(jnp.float32)
        out_ref[rows, lane_slice(column)] = (gate_rows * total).astype(out_ref.dtype)
        return state

    lax.fori_loop(0, seg_len // block, step, tuple(start), unroll=4)


def own_kernel(q_ref, rates_ref, base_ref, extra_ref, *rest):
    locals_in, out_ref = rest[:-1], rest[-1]
    for part, local_ref in enumerate(locals_in):
        carry(q_ref, local_ref, rates_ref[:, lane_slice(part)], base_ref, extra_ref, out_ref, part, part)


def across_kernel(extra_ref, base_ref, q_ref, local_ref, out_ref):
    modes = base_ref.shape[0]
    seg_len = q_ref.shape[0]
    pieces = [
        local_ref[first : first + modes, :].astype(jnp.float32)
        for first in range(seg_len, local_ref.shape[0], modes)
    ]
    rates = pieces[1] + pieces[0]
    for part in range(q_ref.shape[1] // LANES):
        lanes = lane_slice(part)
        carry(q_ref, local_ref.at[:, lanes], rates[:, lanes], base_ref, extra_ref, out_ref, part, part)


def project(blocks, weight_ref):
    total = None
    for rank, parts in blocks:
        depth = weight_ref.shape[0] // lax.axis_size("chan")
        offset = pl.multiple_of(rank * depth, depth)
        for block in parts:
            rows = pl.ds(offset, block.shape[1])
            term = jnp.dot(block[...], weight_ref[rows, :], preferred_element_type=jnp.float32)
            total = term if total is None else total + term
            offset = pl.multiple_of(offset + block.shape[1], block.shape[1])
    return total


def near_kernel(weight_ref, bias_ref, own_ref, pair_ref, *rest):
    across, out_ref = rest[:-1], rest[-1]
    rank = lax.axis_index("chan")
    blocks = [(rank, [own_ref]), (rank ^ 1, [pair_ref]), (rank ^ 2, across)]
    out_ref[...] = project(blocks, weight_ref) + bias_ref[...]


def last_kernel(near_ref, weight_ref, *rest):
    diagonal, (out_hbm, out_ref, sems) = rest[:-3], rest[-3:]
    rank = lax.axis_index("chan")
    pieces = sems.shape[0]
    size = out_ref.shape[0] // pieces
    copies = []
    for i in range(pieces):
        rows = pl.ds(i * size, size)
        total = near_ref[rows, :] + project([(rank ^ 3, [ref.at[rows, :] for ref in diagonal])], weight_ref)
        out_ref[rows, :] = total.astype(out_ref.dtype)
        copies.append(pltpu.make_async_copy(out_ref.at[rows], out_hbm.at[rows], sems.at[i]))
        copies[-1].start()
    for copy in copies:
        copy.wait()


def call(kernel, out, *args, cost=0, scratch=(), hbm=(), outs=pltpu.VMEM):
    return pl.pallas_call(
        kernel,
        out_shape=out,
        in_specs=[pl.BlockSpec(memory_space=pltpu.HBM if i in hbm else pltpu.VMEM) for i in range(len(args))],
        out_specs=jax.tree.map(lambda _: pl.BlockSpec(memory_space=outs), out),
        scratch_shapes=list(scratch),
        compiler_params=pltpu.CompilerParams(vmem_limit_bytes=VMEM_LIMIT),
        cost_estimate=pl.CostEstimate(flops=cost, bytes_accessed=0, transcendentals=0),
    )(*args)


def struct(shape, dtype=jnp.float32):
    return jax.ShapeDtypeStruct(shape, dtype)


def swapped(value, bit):
    count = lax.axis_size("chan")
    return lax.ppermute(value, "chan", [(r, r ^ bit) for r in range(count)])


def beside(value):
    count = lax.axis_size("seq")
    return lax.ppermute(value, "seq", [(r, r ^ 1) for r in range(count)])


def along(value, stride, route):
    count, radix = lax.axis_size("seq"), len(route)

    def target(r):
        spot = r // stride % radix
        return r + (route[spot] - spot) * stride

    return lax.ppermute(value, "seq", [(r, target(r)) for r in range(count)])


def corner(value, step, bit):
    count, width = lax.axis_size("seq"), lax.axis_size("chan")
    pairs = [(r * width + c, (r ^ step) * width + (c ^ bit)) for r in range(count) for c in range(width)]
    return lax.ppermute(value, ("seq", "chan"), pairs)


def carry_shares(total, own, decay, residue, seg_len, also):
    count = lax.axis_size("seq") // 2
    shape = struct(total.shape)
    inner, stride = (), 1
    while True:
        radix = min(4, count // stride)
        received = [along(total, 2 * stride, route) for route in ROUTES[radix]]
        if stride * radix == count:
            break
        kernel = functools.partial(fold_kernel, stride, seg_len)
        *inner, total = call(kernel, [shape, shape], decay, total, *inner, *received)
        stride *= radix
    received, also = lax.optimization_barrier((received, also))
    kernel = functools.partial(share_kernel, stride, seg_len)
    base, extra = call(kernel, [shape, shape], decay, residue, own, total, *inner, *received, cost=FOLD_COST)
    return base, extra, also


def shards(q_gate, k_gate, value, decay, residue, skip, out_weight, out_bias):
    seg_len, channels = value.shape
    modes = decay.shape[0]
    cols = out_weight.shape[1]
    parts = channels // LANES
    bias = out_bias.reshape(1, -1)
    zero = call(first_kernel, struct((SUBLANES, LANES)), cost=FIRST_COST)
    q_across = swapped(q_gate, 2)
    few = struct((modes, channels))
    chunks, gated, bypass = (modes, SUBLANES, channels), (parts, seg_len, LANES), (1, channels)
    thin = struct((seg_len, LANES))
    tall = seg_len + PIECES * modes
    skip = pltpu.with_memory_space_constraint(skip.reshape(1, -1), pltpu.HBM)
    inputs = (zero, k_gate, value, decay, residue, skip)
    scratch = [pltpu.VMEM((modes, SUBLANES, LANES), jnp.float32), pltpu.SemaphoreType.DMA]
    total, *state = call(
        state_kernel,
        [few, struct(chunks), struct(gated), struct(bypass), thin, struct((tall, LANES), jnp.bfloat16)],
        *inputs,
        scratch=scratch, hbm=(5,),
    )
    own_total, local_short, *local = call(
        local_kernel,
        [few, struct((tall, channels), jnp.bfloat16), *[thin] * parts],
        *inputs, total, *state,
        scratch=[pltpu.VMEM(shape, jnp.float32) for shape in (chunks, gated, bypass)] + scratch, hbm=(5,),
    )
    local_across = swapped(local_short, 2)
    base, extra, q_across = carry_shares(total, own_total, decay, residue, seg_len, q_across)
    extra_beside = beside(extra)
    extra_corner = corner(extra, 1, 2)
    base_across = swapped(base, 2)
    whole = struct((seg_len, channels), jnp.bfloat16)
    own = call(own_kernel, whole, q_gate, decay, base, extra_beside, *local, cost=OWN_COST)
    pair = swapped(own, 1)
    across = call(
        across_kernel, whole, extra_corner, base_across, q_across, local_across, cost=PART_COST
    )
    diagonal = swapped(across, 1)
    near = call(near_kernel, struct((seg_len, cols)), out_weight, bias, own, pair, across)
    return call(
        last_kernel, struct((seg_len, cols), jnp.bfloat16), near, out_weight, diagonal,
        scratch=[pltpu.VMEM((seg_len, cols), jnp.bfloat16), pltpu.SemaphoreType.DMA((STORES,))],
        outs=pltpu.HBM,
    )


def solution(mesh):
    return jax.shard_map(
        shards,
        mesh=mesh,
        in_specs=(
            P("seq", "chan"),
            P("seq", "chan"),
            P("seq", "chan"),
            P(None, "chan"),
            P(None, "chan"),
            P("chan"),
            P(None, "chan"),
            P("chan"),
        ),
        out_specs=P("seq", "chan"),
        check_vma=False,
    )
```

```python
import functools

import jax
import jax.numpy as jnp
from jax import lax
from jax.experimental import pallas as pl
from jax.experimental.pallas import tpu as pltpu
from jax.sharding import PartitionSpec as P

LANES = 128
SUBLANES = 8
STORES = 8
OWN_COST = 0
FOLD_COST = 3000000000
PIECES = 3
ROUTES = {2: [(1, 0)], 4: [(3, 2, 0, 1), (2, 3, 0, 1), (1, 0, 3, 2)]}
FIRST_COST = 30000000000
PART_COST = 0
VMEM_LIMIT = 32 * 1024 * 1024


def row(ref, mode, part):
    return ref[mode : mode + 1, part * LANES : (part + 1) * LANES]


def full(value):
    return jnp.broadcast_to(value, (SUBLANES, LANES))


def lane_slice(part):
    return slice(part * LANES, (part + 1) * LANES)


def summarize(zero, k_ref, v_ref, decay_ref, total_ref, chunk_ref, gated_ref):
    modes = decay_ref.shape[0]
    chunk_len = k_ref.shape[0] // SUBLANES
    later = (SUBLANES - 1 - lax.broadcasted_iota(jnp.int32, (SUBLANES, LANES), 0)) * chunk_len
    later = later.astype(jnp.float32)
    for part in range(gated_ref.shape[0]):
        lanes = lane_slice(part)
        product = k_ref[:, lanes].astype(jnp.float32) * v_ref[:, lanes].astype(jnp.float32)
        gated_ref[part] = product.astype(jnp.bfloat16).astype(jnp.float32)
        factor = [full(jnp.exp(-row(decay_ref, n, part))) for n in range(modes)]
        square = [f * f for f in factor]

        def step(t, state):
            x = gated_ref[part, pl.ds(2 * t, SUBLANES, stride=chunk_len), :]
            y = gated_ref[part, pl.ds(2 * t + 1, SUBLANES, stride=chunk_len), :]
            return tuple(g * h + (f * x + y) for f, g, h in zip(factor, square, state))

        state = lax.fori_loop(0, chunk_len // 2, step, (zero,) * modes, unroll=4)
        for n in range(modes):
            chunk_ref[n, :, lanes] = state[n]
            weight = jnp.exp(-row(decay_ref, n, part) * later)
            total_ref[n : n + 1, lanes] = jnp.sum(weight * state[n], axis=0, keepdims=True)


def is_last():
    count = lax.axis_size("seq")
    return lax.axis_index("seq") >= count - 2


def is_first():
    return lax.axis_index("seq") < 2


def first_kernel(out_ref):
    out_ref[...] = jnp.zeros_like(out_ref)


def state_kernel(
    zero_ref, k_ref, v_ref, decay_ref, residue_ref, skip_hbm,
    total_ref, chunk_ref, gated_ref, skip_ref, local_ref, short_ref, weights, sem,
):
    @pl.when(jnp.logical_not(is_last()))
    def _():
        copy = pltpu.make_async_copy(skip_hbm, skip_ref, sem)
        copy.start()
        summarize(zero_ref[...], k_ref, v_ref, decay_ref, total_ref, chunk_ref, gated_ref)
        copy.wait()

    @pl.when(is_last())
    def _():
        total_ref[...] = jnp.zeros_like(total_ref)

    @pl.when(is_first())
    def _():
        convolve(0, gated_ref, decay_ref, residue_ref, skip_ref, chunk_ref, local_ref, short_ref, weights)


def local_kernel(
    zero_ref, k_ref, v_ref, decay_ref, residue_ref, skip_hbm,
    total_in, chunk_in, gated_in, skip_in, local_in, short_in,
    total_ref, short_ref, *rest,
):
    locals_out, (chunk_ref, gated_ref, skip_ref, weights, sem) = rest[:-5], rest[-5:]

    def part_of(part, gated, skip, chunk):
        convolve(part, gated, decay_ref, residue_ref, skip, chunk, locals_out[part], short_ref, weights)

    @pl.when(is_last())
    def _():
        copy = pltpu.make_async_copy(skip_hbm, skip_ref, sem)
        copy.start()
        summarize(zero_ref[...], k_ref, v_ref, decay_ref, total_ref, chunk_ref, gated_ref)
        copy.wait()
        for part in range(len(locals_out)):
            part_of(part, gated_ref, skip_ref, chunk_ref)

    @pl.when(jnp.logical_not(is_last()))
    def _():
        total_ref[...] = total_in[...]
        for part in range(1, len(locals_out)):
            part_of(part, gated_in, skip_in, chunk_in)

    @pl.when(is_first())
    def _():
        locals_out[0][...] = local_in[...]
        short_ref[:, lane_slice(0)] = short_in[...]

    @pl.when(jnp.logical_not(jnp.logical_or(is_first(), is_last())))
    def _():
        part_of(0, gated_in, skip_in, chunk_in)


def convolve(part, gated, decay_ref, residue_ref, skip_ref, chunk_ref, local_ref, short_ref, weights):
    modes = decay_ref.shape[0]
    seg_len = gated.shape[1]
    chunk_len = seg_len // SUBLANES
    index = lax.broadcasted_iota(jnp.int32, (SUBLANES, LANES), 0)
    lanes = lane_slice(part)
    factor, start = [], []
    for n in range(modes):
        rate = row(decay_ref, n, part)
        prefix = chunk_ref[n, :, lanes]
        for shift in (1, 2, 4):
            moved = jnp.where(index >= shift, pltpu.roll(prefix, shift, 0), 0.0)
            prefix = prefix + jnp.exp(-rate * (shift * chunk_len)) * moved
        start.append(jnp.where(index >= 1, pltpu.roll(prefix, 1, 0), 0.0))
        factor.append(full(jnp.exp(-rate)))
        weights[n] = full(row(residue_ref, n, part))
    bypass = full(skip_ref[:, lanes])

    def step(t, state):
        rows = pl.ds(t, SUBLANES, stride=chunk_len)
        x = gated[part, rows, :]
        state = tuple(f * h + x for f, h in zip(factor, state))
        sums = [bypass * x] + [None] * 3
        for n, h in enumerate(state):
            term = weights[n] * h
            sums[n % 4] = term if sums[n % 4] is None else sums[n % 4] + term
        local_ref[rows, :] = (sums[0] + sums[1]) + (sums[2] + sums[3])
        return state

    lax.fori_loop(0, chunk_len, step, tuple(start), unroll=4)
    spot = lanes if short_ref.shape[1] > LANES else slice(None)
    short_ref[:seg_len, spot] = local_ref[...].astype(short_ref.dtype)
    left = decay_ref[:, lanes]
    for first in range(seg_len, short_ref.shape[0], modes):
        piece = left.astype(short_ref.dtype)
        short_ref[first : first + modes, spot] = piece
        left = left - piece.astype(jnp.float32)


def lookup(spot, table):
    found = table[0]
    for i, entry in enumerate(table[1:]):
        found = jnp.where(spot == i + 1, entry, found)
    return found


def fold(rates, inner, total, received, stride, seg_len):
    place = lax.div(lax.axis_index("seq"), 2)
    radix = len(received) + 1
    spot = lax.rem(lax.div(place, stride), radix)
    offset = lax.rem(place, stride)

    def decayed(segments):
        return jnp.exp(-rates * (segments * 2 * seg_len).astype(jnp.float32))

    before = jnp.zeros_like(rates)
    whole = decayed((radix - 1 - spot) * stride) * total
    for route, block in zip(ROUTES[radix], received):
        source = lookup(spot, [route.index(i) for i in range(radix)])
        past = source < spot
        gap = jnp.where(past, spot - 1 - source, 0) * stride
        before += jnp.where(past, decayed(gap) * block, 0.0)
        whole += decayed((radix - 1 - source) * stride) * block
    return inner + decayed(offset) * before, whole


def fold_kernel(stride, seg_len, rates_ref, total_ref, *rest):
    inner, rest = (rest[0][...], rest[1:]) if stride > 1 else (0.0, rest)
    received, (inner_out, total_out) = [ref[...] for ref in rest[:-2]], rest[-2:]
    inner_out[...], total_out[...] = fold(
        rates_ref[...], inner, total_ref[...], received, stride, seg_len
    )


def share_kernel(stride, seg_len, rates_ref, residue_ref, own_ref, total_ref, *rest):
    inner, rest = (rest[0][...], rest[1:]) if stride > 1 else (0.0, rest)
    received, (base_ref, extra_ref) = [ref[...] for ref in rest[:-2]], rest[-2:]
    rates = rates_ref[...]
    before, _ = fold(rates, inner, total_ref[...], received, stride, seg_len)
    before *= residue_ref[...]
    step = jnp.exp(-rates * float(seg_len))
    even = lax.rem(lax.axis_index("seq"), 2) == 0
    base_ref[...] = step * before
    extra_ref[...] = jnp.where(even, residue_ref[...] * own_ref[...] + step * step * before, before)


def carry(q_ref, local_ref, rates, base_ref, extra_ref, out_ref, part, column):
    modes = rates.shape[0]
    seg_len = q_ref.shape[0]
    block = 2 * SUBLANES
    ahead = (lax.broadcasted_iota(jnp.int32, (SUBLANES, LANES), 0) + 1).astype(jnp.float32)
    lanes = lane_slice(part)
    factor, start = [], []
    for n in range(modes):
        rate = rates[n : n + 1, :]
        weight = row(base_ref, n, part) + row(extra_ref, n, part)
        start.append(weight * jnp.exp(-rate * ahead))
        factor.append(full(jnp.exp(-rate * SUBLANES)))

    def step(j, state):
        rows = pl.ds(pl.multiple_of(j * block, block), block)
        halves = []
        for _ in range(2):
            sums = list(state[:4])
            for n, h in enumerate(state[4:]):
                sums[n % 4] = sums[n % 4] + h
            halves.append((sums[0] + sums[1]) + (sums[2] + sums[3]))
            state = tuple(f * h for f, h in zip(factor, state))
        total = local_ref[rows, :].astype(jnp.float32) + jnp.concatenate(halves, axis=0)
        gate_rows = q_ref[rows, lanes].astype(jnp.float32)
        out_ref[rows, lane_slice(column)] = (gate_rows * total).astype(out_ref.dtype)
        return state

    lax.fori_loop(0, seg_len // block, step, tuple(start), unroll=4)


def own_kernel(q_ref, rates_ref, base_ref, extra_ref, *rest):
    locals_in, out_ref = rest[:-1], rest[-1]
    for part, local_ref in enumerate(locals_in):
        carry(q_ref, local_ref, rates_ref[:, lane_slice(part)], base_ref, extra_ref, out_ref, part, part)


def across_kernel(extra_ref, base_ref, q_ref, local_ref, out_ref):
    modes = base_ref.shape[0]
    seg_len = q_ref.shape[0]
    pieces = [
        local_ref[first : first + modes, :].astype(jnp.float32)
        for first in range(seg_len, local_ref.shape[0], modes)
    ]
    rates = (pieces[2] + pieces[1]) + pieces[0]
    for part in range(q_ref.shape[1] // LANES):
        lanes = lane_slice(part)
        carry(q_ref, local_ref.at[:, lanes], rates[:, lanes], base_ref, extra_ref, out_ref, part, part)


def project(blocks, weight_ref):
    total = None
    for rank, parts in blocks:
        depth = weight_ref.shape[0] // lax.axis_size("chan")
        offset = pl.multiple_of(rank * depth, depth)
        for block in parts:
            rows = pl.ds(offset, block.shape[1])
            term = jnp.dot(block[...], weight_ref[rows, :], preferred_element_type=jnp.float32)
            total = term if total is None else total + term
            offset = pl.multiple_of(offset + block.shape[1], block.shape[1])
    return total


def near_kernel(weight_ref, bias_ref, own_ref, pair_ref, *rest):
    across, out_ref = rest[:-1], rest[-1]
    rank = lax.axis_index("chan")
    blocks = [(rank, [own_ref]), (rank ^ 1, [pair_ref]), (rank ^ 2, across)]
    out_ref[...] = project(blocks, weight_ref) + bias_ref[...]


def last_kernel(near_ref, weight_ref, *rest):
    diagonal, (out_hbm, out_ref, sems) = rest[:-3], rest[-3:]
    rank = lax.axis_index("chan")
    pieces = sems.shape[0]
    size = out_ref.shape[0] // pieces
    copies = []
    for i in range(pieces):
        rows = pl.ds(i * size, size)
        total = near_ref[rows, :] + project([(rank ^ 3, [ref.at[rows, :] for ref in diagonal])], weight_ref)
        out_ref[rows, :] = total.astype(out_ref.dtype)
        copies.append(pltpu.make_async_copy(out_ref.at[rows], out_hbm.at[rows], sems.at[i]))
        copies[-1].start()
    for copy in copies:
        copy.wait()


def call(kernel, out, *args, cost=0, scratch=(), hbm=(), outs=pltpu.VMEM):
    return pl.pallas_call(
        kernel,
        out_shape=out,
        in_specs=[pl.BlockSpec(memory_space=pltpu.HBM if i in hbm else pltpu.VMEM) for i in range(len(args))],
        out_specs=jax.tree.map(lambda _: pl.BlockSpec(memory_space=outs), out),
        scratch_shapes=list(scratch),
        compiler_params=pltpu.CompilerParams(vmem_limit_bytes=VMEM_LIMIT),
        cost_estimate=pl.CostEstimate(flops=cost, bytes_accessed=0, transcendentals=0),
    )(*args)


def struct(shape, dtype=jnp.float32):
    return jax.ShapeDtypeStruct(shape, dtype)


def swapped(value, bit):
    count = lax.axis_size("chan")
    return lax.ppermute(value, "chan", [(r, r ^ bit) for r in range(count)])


def beside(value):
    count = lax.axis_size("seq")
    return lax.ppermute(value, "seq", [(r, r ^ 1) for r in range(count)])


def along(value, stride, route):
    count, radix = lax.axis_size("seq"), len(route)

    def target(r):
        spot = r // stride % radix
        return r + (route[spot] - spot) * stride

    return lax.ppermute(value, "seq", [(r, target(r)) for r in range(count)])


def corner(value, step, bit):
    count, width = lax.axis_size("seq"), lax.axis_size("chan")
    pairs = [(r * width + c, (r ^ step) * width + (c ^ bit)) for r in range(count) for c in range(width)]
    return lax.ppermute(value, ("seq", "chan"), pairs)


def carry_shares(total, own, decay, residue, seg_len, also):
    count = lax.axis_size("seq") // 2
    shape = struct(total.shape)
    inner, stride = (), 1
    while True:
        radix = min(4, count // stride)
        received = [along(total, 2 * stride, route) for route in ROUTES[radix]]
        if stride * radix == count:
            break
        kernel = functools.partial(fold_kernel, stride, seg_len)
        *inner, total = call(kernel, [shape, shape], decay, total, *inner, *received)
        stride *= radix
    received, also = lax.optimization_barrier((received, also))
    kernel = functools.partial(share_kernel, stride, seg_len)
    base, extra = call(kernel, [shape, shape], decay, residue, own, total, *inner, *received, cost=FOLD_COST)
    return base, extra, also


def shards(q_gate, k_gate, value, decay, residue, skip, out_weight, out_bias):
    seg_len, channels = value.shape
    modes = decay.shape[0]
    cols = out_weight.shape[1]
    parts = channels // LANES
    bias = out_bias.reshape(1, -1)
    zero = call(first_kernel, struct((SUBLANES, LANES)), cost=FIRST_COST)
    q_across = swapped(q_gate, 2)
    few = struct((modes, channels))
    chunks, gated, bypass = (modes, SUBLANES, channels), (parts, seg_len, LANES), (1, channels)
    thin = struct((seg_len, LANES))
    tall = seg_len + PIECES * modes
    skip = pltpu.with_memory_space_constraint(skip.reshape(1, -1), pltpu.HBM)
    inputs = (zero, k_gate, value, decay, residue, skip)
    scratch = [pltpu.VMEM((modes, SUBLANES, LANES), jnp.float32), pltpu.SemaphoreType.DMA]
    total, *state = call(
        state_kernel,
        [few, struct(chunks), struct(gated), struct(bypass), thin, struct((tall, LANES), jnp.bfloat16)],
        *inputs,
        scratch=scratch, hbm=(5,),
    )
    own_total, local_short, *local = call(
        local_kernel,
        [few, struct((tall, channels), jnp.bfloat16), *[thin] * parts],
        *inputs, total, *state,
        scratch=[pltpu.VMEM(shape, jnp.float32) for shape in (chunks, gated, bypass)] + scratch, hbm=(5,),
    )
    local_across = swapped(local_short, 2)
    base, extra, q_across = carry_shares(total, own_total, decay, residue, seg_len, q_across)
    extra_beside = beside(extra)
    extra_corner = corner(extra, 1, 2)
    base_across = swapped(base, 2)
    whole = struct((seg_len, channels), jnp.bfloat16)
    own = call(own_kernel, whole, q_gate, decay, base, extra_beside, *local, cost=OWN_COST)
    pair = swapped(own, 1)
    across = call(
        across_kernel, whole, extra_corner, base_across, q_across, local_across, cost=PART_COST
    )
    diagonal = swapped(across, 1)
    near = call(near_kernel, struct((seg_len, cols)), out_weight, bias, own, pair, across)
    return call(
        last_kernel, struct((seg_len, cols), jnp.bfloat16), near, out_weight, diagonal,
        scratch=[pltpu.VMEM((seg_len, cols), jnp.bfloat16), pltpu.SemaphoreType.DMA((STORES,))],
        outs=pltpu.HBM,
    )


def solution(mesh):
    return jax.shard_map(
        shards,
        mesh=mesh,
        in_specs=(
            P("seq", "chan"),
            P("seq", "chan"),
            P("seq", "chan"),
            P(None, "chan"),
            P(None, "chan"),
            P("chan"),
            P(None, "chan"),
            P("chan"),
        ),
        out_specs=P("seq", "chan"),
        check_vma=False,
    )
```
